32 devices in a mesh: batch: 8 (over z, core), seq: 4 (over y, x).
Axes of the slice: x: 2, y: 2, z: 4, core: 2. Of those that a mesh axis runs over, the one named last changes fastest.
Arguments:
- inputs: bfloat16 [4096, 7168], P(('batch', 'seq')), parts along dimension 0, may hold values from -6 to 6
- adapter_down: bfloat16 [7168, 384], replicated, may hold values from -0.0625 to 0.0625
- adapter_up: bfloat16 [3, 128, 3584], P(None, None, 'seq'), may hold values from -0.52734375 to 0.52734375
- shared_qkv: bfloat16 [4096, 10752], P(('batch', 'seq')), parts along dimension 0, may hold values from -8 to 8
- sink_logits: float32 [16], P('seq'), may hold values from 0 to 3
- lengths: int32 [64], P('batch'), parts along dimension 0, may hold values from 1 to 384, as said below
- block_table: int32 [64, 24], P('batch'), parts along dimension 0, may hold values from 0 to 39, as said below
Outputs:
- hidden: bfloat16 [4096, 3584], P(('batch', 'seq')), parts along dimension 0
- kv_cache: bfloat16 [16, 320, 2, 3584], P('seq', 'batch'), parts along dimension 1
The draws below stay inside these ranges and needn't reach their ends.
There are 8 independent parts, one for each index of `batch`. The reference program is written for one: setup_inputs(seed, part) draws one part's arguments, and reference() takes and returns one part's arrays. A program takes and returns all parts, laid end to end along the dimension named above; an argument that names none is the same for every part. Nothing has to cross between parts.
Inputs may be any that keep to these rules, and one draw needn't show every extreme that they name: The lengths sum to 512; exactly one prompt has 384 tokens. `block_table`: entry b of row s is the page of positions b * 16 to b * 16 + 15 of prompt s; only entries below ceil(lengths[s] / 16) are read, and all entries that are read are distinct pages.
All inputs are finite; a program needn't handle non-finite values.
Results may differ from the reference program's by a relative error of at most 0.011.
Values may be sent and summed in bfloat16 or wider, within the bound.
No kernel may reach another device: no remote copies, remote signals or barrier semaphores. Data moves between devices by JAX's collectives and lax.ppermute only.
A program may use at most 128 MiB of HBM per device.

```python
import jax
import jax.numpy as jnp
from jax import lax

DIN = 7168
HD = 224
RANK = 128
HEADS = 16
SEGS = 8
PAGE = 16
TOKENS = 512
WINDOW = 256
MAXLEN = 384
MAXB = 24
PAGES = 40


def prompt_lengths(key):
    remaining = TOKENS - MAXLEN
    first_key, second_key = jax.random.split(jax.random.fold_in(key, 11))
    cuts = jnp.sort(jax.random.permutation(first_key, remaining - 1)[:SEGS - 2] + 1).astype(jnp.int32)
    edges = jnp.concatenate([jnp.zeros((1,), jnp.int32), cuts, jnp.full((1,), remaining, jnp.int32)])
    shorter = (edges[1:] - edges[:-1]).astype(jnp.int32)
    chosen = jax.random.randint(second_key, (), 0, SEGS)
    places = jnp.arange(SEGS, dtype=jnp.int32)
    source = jnp.clip(places - (places > chosen).astype(jnp.int32), 0, SEGS - 2)
    return jnp.where(places == chosen, MAXLEN, shorter[source]).astype(jnp.int32)


def draw_lengths(key, part):
    return prompt_lengths(key)


def draw_block_table(key, part):
    lengths = prompt_lengths(key)
    needed = ((lengths + PAGE - 1) // PAGE).astype(jnp.int32)
    before = (jnp.cumsum(needed) - needed).astype(jnp.int32)
    order = jax.random.permutation(jax.random.fold_in(key, 23), PAGES).astype(jnp.int32)
    column = jnp.arange(MAXB, dtype=jnp.int32)
    used = column[None, :] < needed[:, None]
    spare_rank = (jnp.cumsum(jnp.logical_not(used).reshape(-1).astype(jnp.int32)) - 1).reshape(SEGS, MAXB)
    total_needed = jnp.sum(needed).astype(jnp.int32)
    index = jnp.where(used, before[:, None] + column[None, :], total_needed + spare_rank)
    return order[index % PAGES].astype(jnp.int32)


def draw_shared_qkv(key, part):
    head_width = HEADS * HD
    base_key = jax.random.fold_in(jax.random.fold_in(key, 5), 0)
    column = jnp.arange(3 * head_width)
    scaling = jnp.where(column >= 2 * head_width, 2.0, 0.8)
    values = jnp.clip(jax.random.normal(base_key, (TOKENS, 3 * head_width), jnp.float32) * scaling[None, :], -8.0, 8.0)
    return values.astype(jnp.bfloat16)


def shard_levels(own_key, dims, pieces, least, high):
    def one(dim, shards_of):
        steps = jax.random.uniform(jax.random.fold_in(jax.random.fold_in(own_key, 6), dim), (shards_of,), jnp.float32, least / len(pieces), high / len(pieces))
        return jnp.repeat(jnp.exp(steps), dims[dim] // shards_of).reshape((-1,) + (1,) * (len(dims) - dim - 1))

    loudness = one(*pieces[0])
    for cut in pieces[1:]:
        loudness = loudness * one(*cut)
    return loudness


def scatter_about(stream_key, shape, scale, most, shards=(), kind=jnp.bfloat16):
    entries = jax.random.normal(stream_key, shape, jnp.float32) * scale
    if len(shards) > 0:
        entries = shard_levels(stream_key, shape, shards, -0.22, 0.18) * entries
    return jnp.clip(entries, min=-most, max=most).astype(kind)


def setup_inputs(seed: int = 0, part: int = 0) -> dict:
    key_list = jax.random.split(jax.random.key(seed), 8)
    own_keys = jax.random.split(jax.random.fold_in(key_list[7], part), 8)
    inputs = scatter_about(own_keys[0], (TOKENS, DIN), 1.0, 6.0, ((0, 4),))
    adapter_down = scatter_about(key_list[1], (DIN, 3 * RANK), DIN ** -0.5, 0.0625)
    adapter_up = scatter_about(key_list[2], (3, RANK, HEADS * HD), (0.5 * RANK ** -0.5), 0.52734375, ((2, 4),))
    shared_qkv = draw_shared_qkv(jax.random.fold_in(jax.random.fold_in(key_list[7], part), 71), part)
    sink_logits = jnp.clip(3.0 * jax.random.uniform(key_list[4], (HEADS,), jnp.float32) ** shard_levels(key_list[4], (HEADS,), ((0, 4),), -0.2, 0.2), 0.0, 3.0)
    lengths = draw_lengths(jax.random.fold_in(jax.random.fold_in(key_list[7], part), 71), part)
    block_table = draw_block_table(jax.random.fold_in(jax.random.fold_in(key_list[7], part), 71), part)
    return {"inputs": inputs, "adapter_down": adapter_down, "adapter_up": adapter_up, "shared_qkv": shared_qkv, "sink_logits": sink_logits, "lengths": lengths, "block_table": block_table}


def segment_positions(lengths):
    segment_ends = jnp.cumsum(lengths).astype(jnp.int32)
    segment_starts = (segment_ends - lengths).astype(jnp.int32)
    places = jnp.arange(TOKENS, dtype=jnp.int32)
    segment = jnp.sum((places[:, None] >= segment_ends[None, :]).astype(jnp.int32), axis=1).astype(jnp.int32)
    member = segment[:, None] == jnp.arange(SEGS, dtype=jnp.int32)[None, :]
    offsets = jnp.sum(jnp.where(member, segment_starts[None, :], 0), axis=1).astype(jnp.int32)
    position = (places - offsets).astype(jnp.int32)
    return segment, position


def reference(inputs, adapter_down, adapter_up, shared_qkv, sink_logits, lengths, block_table):
    low_codes = jnp.dot(inputs, adapter_down, preferred_element_type=jnp.float32).astype(jnp.bfloat16)
    low_rank = jnp.einsum("tcr,crf->tcf", low_codes.reshape(TOKENS, 3, RANK).astype(jnp.float32), adapter_up.astype(jnp.float32))
    projected = (shared_qkv.reshape(TOKENS, 3, HEADS * HD).astype(jnp.float32) + low_rank).astype(jnp.bfloat16)
    projected = projected.reshape(TOKENS, 3, HEADS, HD)
    segment, position = segment_positions(lengths)
    places = jnp.arange(TOKENS, dtype=jnp.int32)
    visible = (segment[:, None] == segment[None, :]) & (places[None, :] <= places[:, None]) & (places[:, None] - places[None, :] < WINDOW)

    def one_head(head_index):
        query_rows = projected[:, 0, head_index]
        key_rows = projected[:, 1, head_index]
        value_rows = projected[:, 2, head_index]
        sink_logit = sink_logits[head_index]
        scores = jnp.dot(query_rows, key_rows.T, preferred_element_type=jnp.float32) * (HD ** -0.5)
        scores = jnp.where(visible, scores, -jnp.inf)
        running_max = jnp.maximum(jnp.max(scores, axis=1), sink_logit)
        weights = jnp.exp(scores - running_max[:, None])
        denominator = jnp.sum(weights, axis=1) + jnp.exp(sink_logit - running_max)
        mixture = jnp.dot(weights.astype(jnp.bfloat16), value_rows, preferred_element_type=jnp.float32) / denominator[:, None]
        return mixture.astype(jnp.bfloat16)

    outputs = lax.map(one_head, jnp.arange(HEADS, dtype=jnp.int32))
    hidden = outputs.transpose(1, 0, 2).reshape(TOKENS, HEADS * HD)
    page_index = block_table.reshape(-1)[(segment * MAXB + position // PAGE).astype(jnp.int32)]
    cache_row = (page_index * PAGE + position % PAGE).astype(jnp.int32)

    def place(values_in):
        flat_cache = jnp.zeros((PAGES * PAGE, HEADS, HD), jnp.bfloat16).at[cache_row].set(values_in)
        return flat_cache.reshape(PAGES, PAGE, HEADS, HD).transpose(2, 0, 1, 3).reshape(HEADS, PAGES, PAGE * HD)

    kv_cache = jnp.stack([place(projected[:, 1]), place(projected[:, 2])], axis=2)
    return hidden, kv_cache
```

```python
import jax
import jax.numpy as jnp
from jax import lax
from jax.experimental import pallas as pl
from jax.experimental.pallas import tpu as pltpu
from jax.sharding import PartitionSpec as P

HD = 224
RANK = 128
HEADS = 16
SEGS = 8
PAGE = 16


def segment_positions(lengths, total_rows):
    segment_ends = jnp.cumsum(lengths)
    segment_starts = segment_ends - lengths
    places = jnp.arange(total_rows, dtype=jnp.int32)
    segment = jnp.sum((places[:, None] >= segment_ends[None, :]).astype(jnp.int32), axis=1)
    member = segment[:, None] == jnp.arange(SEGS, dtype=jnp.int32)[None, :]
    offsets = jnp.sum(jnp.where(member, segment_starts[None, :], 0), axis=1)
    return (segment, places - offsets)


def per_device_general(inputs, adapter_down, adapter_up, shared_qkv, sink_logits, lengths, block_table):
    group_size = lax.axis_size("seq")
    tok_rows = inputs.shape[0]
    total_rows = tok_rows * group_size
    heads_local = adapter_up.shape[2] // HD
    window_span = total_rows // 2
    low_codes = jnp.dot(inputs, adapter_down, preferred_element_type=jnp.float32).astype(
        jnp.bfloat16
    )
    shared_base = shared_qkv.reshape(tok_rows, 3, HEADS * HD)
    low_rank = jnp.einsum(
        "tcr,crf->tcf",
        low_codes.reshape(tok_rows, 3, RANK),
        lax.all_gather(adapter_up, "seq", axis=2, tiled=True),
        preferred_element_type=jnp.float32,
    )
    merged = (shared_base.astype(jnp.float32) + low_rank).astype(jnp.bfloat16)
    sending = merged.reshape(tok_rows, 3, HEADS, HD)
    arrived = lax.all_to_all(sending, "seq", split_axis=2, concat_axis=0, tiled=True)
    segment, position = segment_positions(lengths, total_rows)
    tile_rows = min(512, total_rows)
    tile_count = total_rows // tile_rows
    scale_factor = HD ** (-0.5)

    def one_head(head_index):
        query_all = arrived[:, 0, head_index]
        key_all = arrived[:, 1, head_index]
        value_all = arrived[:, 2, head_index]
        sink_logit = sink_logits[head_index]

        def query_tile(tile_index):
            query_first = tile_index * tile_rows
            query_rows = lax.dynamic_slice_in_dim(query_all, query_first, tile_rows, 0)
            query_segs = lax.dynamic_slice_in_dim(segment, query_first, tile_rows, 0)
            query_place = query_first + jnp.arange(tile_rows, dtype=jnp.int32)
            start_state = (
                jnp.full((tile_rows,), sink_logit, jnp.float32),
                jnp.zeros((tile_rows,), jnp.float32),
                jnp.zeros((tile_rows, HD), jnp.float32),
            )

            def visit(key_tile, state):
                key_first = key_tile * tile_rows
                running_max, running_sum, weighted = state
                key_rows = lax.dynamic_slice_in_dim(key_all, key_first, tile_rows, 0)
                value_rows = lax.dynamic_slice_in_dim(value_all, key_first, tile_rows, 0)
                key_segs = lax.dynamic_slice_in_dim(segment, key_first, tile_rows, 0)
                key_place = key_first + jnp.arange(tile_rows, dtype=jnp.int32)
                scores = (
                    jnp.dot(query_rows, key_rows.T, preferred_element_type=jnp.float32)
                    * scale_factor
                )
                visible = (
                    (query_segs[:, None] == key_segs[None, :])
                    & (key_place[None, :] <= query_place[:, None])
                    & (query_place[:, None] - key_place[None, :] < window_span)
                )
                scores = jnp.where(visible, scores, -jnp.inf)
                new_max = jnp.maximum(running_max, jnp.max(scores, axis=1))
                rescale = jnp.exp(running_max - new_max)
                weights = jnp.exp(scores - new_max[:, None])
                new_sum = running_sum * rescale + jnp.sum(weights, axis=1)
                new_weighted = weighted * rescale[:, None] + jnp.dot(
                    weights.astype(jnp.bfloat16), value_rows, preferred_element_type=jnp.float32
                )
                return (new_max, new_sum, new_weighted)

            final_max, final_sum, weighted = lax.fori_loop(0, tile_count, visit, start_state)
            denominator = final_sum + jnp.exp(sink_logit - final_max)
            return (weighted / denominator[:, None]).astype(jnp.bfloat16)

        return lax.map(query_tile, jnp.arange(tile_count, dtype=jnp.int32)).reshape(total_rows, HD)

    attended = lax.map(one_head, jnp.arange(heads_local, dtype=jnp.int32))
    returned = lax.all_to_all(attended, "seq", split_axis=1, concat_axis=0, tiled=True)
    hidden = returned.transpose(1, 0, 2).reshape(tok_rows, HEADS * HD)
    page_count = total_rows // PAGE + SEGS
    page_index = block_table.reshape(-1)[segment * block_table.shape[1] + position // PAGE]
    cache_row = page_index * PAGE + position % PAGE

    def place(values_in):
        flat_cache = (
            jnp.zeros((page_count * PAGE, heads_local, HD), jnp.bfloat16)
            .at[cache_row]
            .set(values_in)
        )
        return (
            flat_cache.reshape(page_count, PAGE, heads_local, HD)
            .transpose(2, 0, 1, 3)
            .reshape(heads_local, page_count, PAGE * HD)
        )

    kv_cache = jnp.stack([place(arrived[:, 1]), place(arrived[:, 2])], axis=2)
    return (hidden, kv_cache)


LANES = 128
BF16 = jnp.bfloat16
F32 = jnp.float32
ANYWHERE = pl.BlockSpec(memory_space=pl.ANY)
IN_VMEM = pl.BlockSpec(memory_space=pltpu.VMEM)
IN_SMEM = pl.BlockSpec(memory_space=pltpu.SMEM)


def sends(group_size):
    return sorted(range(1, group_size), key=lambda bits: (-bits.bit_count(), bits))


def to_partner(values, bits, group_size):
    return lax.ppermute(values, "seq", [(i, i ^ bits) for i in range(group_size)])


def params(**more):
    return pltpu.CompilerParams(vmem_limit_bytes=40 * 1024 * 1024, **more)


def cost(flops, moved):
    return pl.CostEstimate(flops=flops, bytes_accessed=moved, transcendentals=0)


def pack_qkv(shared_qkv, width, group_size):
    tok_rows = shared_qkv.shape[0]
    partners = sends(group_size)

    def body(shared, *refs):
        outs, sem = refs[:-1], refs[-1]
        me = lax.axis_index("seq")
        copies = []
        for n, bits in enumerate(partners):
            owner = jnp.bitwise_xor(me, bits)
            for c in range(3):
                first = pl.multiple_of(c * HEADS * HD + owner * width, LANES)
                copies.append(
                    pltpu.make_async_copy(
                        shared.at[:, pl.ds(first, width)],
                        outs[n].at[pl.ds(c * tok_rows, tok_rows), :],
                        sem.at[n, c],
                    )
                )
        for copy in copies:
            copy.start()
        for copy in copies:
            copy.wait()

    shape = jax.ShapeDtypeStruct((3 * tok_rows, width), BF16)
    return pl.pallas_call(
        body,
        out_shape=[shape] * len(partners),
        in_specs=[ANYWHERE],
        out_specs=[ANYWHERE] * len(partners),
        scratch_shapes=[pltpu.SemaphoreType.DMA((len(partners), 3))],
        compiler_params=params(),
        cost_estimate=cost(0, 2 * len(partners) * 3 * tok_rows * width * 2),
        name="pack_qkv",
    )(shared_qkv)


def head_windows(heads_local):
    return [(h * HD // LANES, -(-(h + 1) * HD // LANES)) for h in range(heads_local)]


def attend(shared_qkv, up, sink_logits, lengths, codes, arrived, group_size):
    tok_rows = shared_qkv.shape[0]
    width = up.shape[2]
    heads_local = width // HD
    total_rows = tok_rows * group_size
    window_span = total_rows // 2
    windows = head_windows(heads_local)
    scale_factor = HD ** (-0.5)

    def body(*refs):
        refs = list(refs)
        take = lambda n: [refs.pop(0) for _ in range(n)]
        shared, up_ref, sinks, lens = take(4)
        code_refs = take(group_size)
        arrived_refs = [None] + take(group_size - 1)
        outs = take(group_size)
        keys, values = take(2)
        queries, own, merged, sem = take(4)
        me = lax.axis_index("seq")
        copies = []
        for c in range(3):
            first = pl.multiple_of(c * HEADS * HD + me * width, LANES)
            copies.append(
                pltpu.make_async_copy(
                    shared.at[:, pl.ds(first, width)],
                    own.at[pl.ds(c * tok_rows, tok_rows), :],
                    sem.at[c],
                )
            )
        for copy in copies:
            copy.start()
        for bits in list(range(1, group_size)) + [0]:
            if bits == 0:
                for copy in copies:
                    copy.wait()
            source = own if bits == 0 else arrived_refs[bits]
            place = pl.ds(pl.multiple_of(jnp.bitwise_xor(me, bits) * tok_rows, tok_rows), tok_rows)
            for c, target in enumerate((queries, keys, values)):
                low = jnp.dot(
                    code_refs[bits][:, c * RANK : (c + 1) * RANK],
                    up_ref[c],
                    preferred_element_type=F32,
                )
                base = source[c * tok_rows : (c + 1) * tok_rows, :].astype(F32)
                target[place, :] = (base + low).astype(BF16)

        ends = []
        for s in range(SEGS):
            ends.append(lens[s] + (ends[-1] if ends else 0))
        for b in range(group_size):
            first_query = b * tok_rows
            first_key = max(0, (first_query - window_span + 1) // tok_rows * tok_rows)
            key_rows = first_query + tok_rows - first_key
            query_place = first_query + lax.broadcasted_iota(jnp.int32, (tok_rows, 1), 0)
            earliest = query_place - (window_span - 1)
            for s in range(SEGS):
                earliest = jnp.where(ends[s] <= query_place, jnp.maximum(earliest, ends[s]), earliest)
            key_place = first_key + lax.broadcasted_iota(jnp.int32, (tok_rows, key_rows), 1)
            visible = (key_place >= earliest) & (key_place <= query_place)
            parts = {}
            for h in range(heads_local):
                lo, hi = windows[h][0] * LANES, windows[h][1] * LANES
                column = lo + lax.broadcasted_iota(jnp.int32, (1, hi - lo), 1)
                mine = (column >= h * HD) & (column < (h + 1) * HD)
                query = queries[first_query : first_query + tok_rows, lo:hi]
                query = jnp.where(mine, query, jnp.zeros_like(query))
                scores = lax.dot_general(
                    query,
                    keys[first_key : first_key + key_rows, lo:hi],
                    (((1,), (1,)), ((), ())),
                    preferred_element_type=F32,
                )
                scores = jnp.where(visible, scores * scale_factor, -jnp.inf)
                top = jnp.maximum(jnp.max(scores, axis=1, keepdims=True), sinks[h])
                weights = jnp.exp(scores - top)
                denominator = jnp.sum(weights, axis=1, keepdims=True) + jnp.exp(sinks[h] - top)
                mixed = jnp.dot(
                    weights.astype(BF16),
                    values[first_key : first_key + key_rows, lo:hi],
                    preferred_element_type=F32,
                ) / denominator
                for tile in range(*windows[h]):
                    at = tile * LANES - lo
                    piece = mixed[:, at : at + LANES]
                    if tile in parts:
                        lane = tile * LANES + lax.broadcasted_iota(jnp.int32, (1, LANES), 1)
                        piece = jnp.where(lane < h * HD, parts[tile], piece)
                    parts[tile] = piece
            for tile, piece in parts.items():
                merged[first_query : first_query + tok_rows, tile * LANES : (tile + 1) * LANES] = piece.astype(BF16)
        for bits in range(group_size):
            place = pl.ds(pl.multiple_of(jnp.bitwise_xor(me, bits) * tok_rows, tok_rows), tok_rows)
            outs[bits][...] = merged[place, :]

    block = jax.ShapeDtypeStruct((tok_rows, width), BF16)
    stream = jax.ShapeDtypeStruct((total_rows, width), BF16)
    results = pl.pallas_call(
        body,
        out_shape=[block] * group_size + [stream] * 2,
        in_specs=[ANYWHERE, IN_VMEM, IN_SMEM, IN_SMEM] + [IN_VMEM] * (2 * group_size - 1),
        out_specs=[IN_VMEM] * (group_size + 2),
        scratch_shapes=[
            pltpu.VMEM((total_rows, width), BF16),
            pltpu.VMEM((3 * tok_rows, width), BF16),
            pltpu.VMEM((total_rows, width), BF16),
            pltpu.SemaphoreType.DMA((3,)),
        ],
        compiler_params=params(),
        cost_estimate=cost(4 * total_rows * total_rows * width, 8 * total_rows * width * 2),
        name="attend",
    )(shared_qkv, up, sink_logits, lengths, *codes, *arrived)
    return results[:group_size], results[group_size], results[group_size + 1]


def build_cache(keys, values, lengths, block_table):
    total_rows, width = keys.shape
    heads_local = width // HD
    page_count = total_rows // PAGE + SEGS
    blocks = block_table.shape[1]
    rows = 2 * page_count

    def body(keys_ref, values_ref, lens, table, out):
        row = lax.broadcasted_iota(jnp.int32, (rows, blocks), 0)
        page = lax.shift_right_logical(row, 1)
        block = lax.broadcasted_iota(jnp.int32, (rows, blocks), 1)
        first = jnp.zeros((rows, blocks), jnp.int32)
        count = jnp.zeros((rows, blocks), jnp.int32)
        start = 0
        for s in range(SEGS):
            left = lens[s] - block * PAGE
            held = (table[s : s + 1, :] == page) & (left > 0)
            first = jnp.where(held, start + block * PAGE, first)
            count = jnp.where(held, jnp.minimum(left, PAGE), count)
            start = start + lens[s]
        first = jnp.sum(first, axis=1, keepdims=True)
        count = jnp.sum(count, axis=1, keepdims=True)
        odd = jnp.bitwise_and(lax.broadcasted_iota(jnp.int32, (rows, 1), 0), 1)
        place = lax.broadcasted_iota(jnp.int32, (rows, total_rows), 1)
        pieces = []
        for r in range(PAGE):
            for_keys = jnp.where((odd == 0) & (count > r), first + r, -1)
            for_values = jnp.where((odd == 1) & (count > r), first + r, -1)
            pick_keys = (place == for_keys).astype(F32).astype(BF16)
            pick_values = (place == for_values).astype(F32).astype(BF16)
            picked = jnp.dot(pick_keys, keys_ref[...], preferred_element_type=F32) + jnp.dot(
                pick_values, values_ref[...], preferred_element_type=F32
            )
            pieces.append(picked)
        for h in range(heads_local):
            line = jnp.concatenate([piece[:, h * HD : (h + 1) * HD] for piece in pieces], axis=1)
            out[h] = line.astype(BF16).reshape(page_count, 2, PAGE * HD)

    return pl.pallas_call(
        body,
        out_shape=jax.ShapeDtypeStruct((heads_local, page_count, 2, PAGE * HD), BF16),
        in_specs=[IN_VMEM, IN_VMEM, IN_SMEM, IN_VMEM],
        out_specs=IN_VMEM,
        compiler_params=params(),
        cost_estimate=cost(4 * rows * PAGE * total_rows * width, 4 * total_rows * width * 2),
        name="build_cache",
    )(keys, values, lengths, block_table)


def join_heads(blocks, group_size):
    tok_rows, width = blocks[0].shape

    def body(*refs):
        sources, out, sem = refs[:group_size], refs[group_size], refs[group_size + 1]
        me = lax.axis_index("seq")
        copies = []
        for bits in range(group_size):
            first = pl.multiple_of(jnp.bitwise_xor(me, bits) * width, LANES)
            copies.append(
                pltpu.make_async_copy(sources[bits], out.at[:, pl.ds(first, width)], sem.at[bits])
            )
        for copy in copies:
            copy.start()
        for copy in copies:
            copy.wait()

    return pl.pallas_call(
        body,
        out_shape=jax.ShapeDtypeStruct((tok_rows, width * group_size), BF16),
        in_specs=[ANYWHERE] * group_size,
        out_specs=ANYWHERE,
        scratch_shapes=[pltpu.SemaphoreType.DMA((group_size,))],
        compiler_params=params(),
        cost_estimate=cost(0, 2 * tok_rows * width * group_size * 2),
        name="join_heads",
    )(*blocks)


def per_device_tiled(inputs, adapter_down, adapter_up, shared_qkv, sink_logits, lengths, block_table):
    group_size = lax.axis_size("seq")
    partners = sends(group_size)
    packed = pack_qkv(shared_qkv, adapter_up.shape[2], group_size)
    arrived = {bits: to_partner(part, bits, group_size) for bits, part in zip(partners, packed)}
    own_codes = jnp.dot(inputs, adapter_down, preferred_element_type=F32).astype(BF16)
    codes = {bits: to_partner(own_codes, bits, group_size) for bits in partners}
    codes[0] = own_codes
    blocks, keys, values = attend(
        shared_qkv,
        adapter_up,
        sink_logits,
        lengths,
        [codes[bits] for bits in range(group_size)],
        [arrived[bits] for bits in range(1, group_size)],
        group_size,
    )
    returned = {bits: to_partner(blocks[bits], bits, group_size) for bits in partners}
    returned[0] = blocks[0]
    kv_cache = build_cache(keys, values, lengths, block_table)
    hidden = join_heads([returned[bits] for bits in range(group_size)], group_size)
    return (hidden, kv_cache)


def per_device(inputs, adapter_down, adapter_up, shared_qkv, sink_logits, lengths, block_table):
    group_size = lax.axis_size("seq")
    tiled = (
        group_size & (group_size - 1) == 0
        and adapter_up.shape[2] % LANES == 0
        and inputs.shape[0] % LANES == 0
        and inputs.shape[0] * group_size <= 512
    )
    chosen = per_device_tiled if tiled else per_device_general
    return chosen(inputs, adapter_down, adapter_up, shared_qkv, sink_logits, lengths, block_table)


def solution(mesh):
    return jax.shard_map(
        per_device,
        mesh=mesh,
        in_specs=(
            P(("batch", "seq"), None),
            P(),
            P(None, None, "seq"),
            P(("batch", "seq"), None),
            P("seq"),
            P("batch"),
            P("batch", None),
        ),
        out_specs=(P(("batch", "seq"), None), P("seq", "batch", None, None)),
        check_vma=False,
    )
```

```python
import jax
import jax.numpy as jnp
from jax import lax
from jax.experimental import pallas as pl
from jax.experimental.pallas import tpu as pltpu
from jax.sharding import PartitionSpec as P

HD = 224
RANK = 128
HEADS = 16
SEGS = 8
PAGE = 16


def segment_positions(lengths, total_rows):
    segment_ends = jnp.cumsum(lengths)
    segment_starts = segment_ends - lengths
    places = jnp.arange(total_rows, dtype=jnp.int32)
    segment = jnp.sum((places[:, None] >= segment_ends[None, :]).astype(jnp.int32), axis=1)
    member = segment[:, None] == jnp.arange(SEGS, dtype=jnp.int32)[None, :]
    offsets = jnp.sum(jnp.where(member, segment_starts[None, :], 0), axis=1)
    return (segment, places - offsets)


def per_device_general(inputs, adapter_down, adapter_up, shared_qkv, sink_logits, lengths, block_table):
    group_size = lax.axis_size("seq")
    tok_rows = inputs.shape[0]
    total_rows = tok_rows * group_size
    heads_local = adapter_up.shape[2] // HD
    window_span = total_rows // 2
    low_codes = jnp.dot(inputs, adapter_down, preferred_element_type=jnp.float32).astype(
        jnp.bfloat16
    )
    shared_base = shared_qkv.reshape(tok_rows, 3, HEADS * HD)
    low_rank = jnp.einsum(
        "tcr,crf->tcf",
        low_codes.reshape(tok_rows, 3, RANK),
        lax.all_gather(adapter_up, "seq", axis=2, tiled=True),
        preferred_element_type=jnp.float32,
    )
    merged = (shared_base.astype(jnp.float32) + low_rank).astype(jnp.bfloat16)
    sending = merged.reshape(tok_rows, 3, HEADS, HD)
    arrived = lax.all_to_all(sending, "seq", split_axis=2, concat_axis=0, tiled=True)
    segment, position = segment_positions(lengths, total_rows)
    tile_rows = min(512, total_rows)
    tile_count = total_rows // tile_rows
    scale_factor = HD ** (-0.5)

    def one_head(head_index):
        query_all = arrived[:, 0, head_index]
        key_all = arrived[:, 1, head_index]
        value_all = arrived[:, 2, head_index]
        sink_logit = sink_logits[head_index]

        def query_tile(tile_index):
            query_first = tile_index * tile_rows
            query_rows = lax.dynamic_slice_in_dim(query_all, query_first, tile_rows, 0)
            query_segs = lax.dynamic_slice_in_dim(segment, query_first, tile_rows, 0)
            query_place = query_first + jnp.arange(tile_rows, dtype=jnp.int32)
            start_state = (
                jnp.full((tile_rows,), sink_logit, jnp.float32),
                jnp.zeros((tile_rows,), jnp.float32),
                jnp.zeros((tile_rows, HD), jnp.float32),
            )

            def visit(key_tile, state):
                key_first = key_tile * tile_rows
                running_max, running_sum, weighted = state
                key_rows = lax.dynamic_slice_in_dim(key_all, key_first, tile_rows, 0)
                value_rows = lax.dynamic_slice_in_dim(value_all, key_first, tile_rows, 0)
                key_segs = lax.dynamic_slice_in_dim(segment, key_first, tile_rows, 0)
                key_place = key_first + jnp.arange(tile_rows, dtype=jnp.int32)
                scores = (
                    jnp.dot(query_rows, key_rows.T, preferred_element_type=jnp.float32)
                    * scale_factor
                )
                visible = (
                    (query_segs[:, None] == key_segs[None, :])
                    & (key_place[None, :] <= query_place[:, None])
                    & (query_place[:, None] - key_place[None, :] < window_span)
                )
                scores = jnp.where(visible, scores, -jnp.inf)
                new_max = jnp.maximum(running_max, jnp.max(scores, axis=1))
                rescale = jnp.exp(running_max - new_max)
                weights = jnp.exp(scores - new_max[:, None])
                new_sum = running_sum * rescale + jnp.sum(weights, axis=1)
                new_weighted = weighted * rescale[:, None] + jnp.dot(
                    weights.astype(jnp.bfloat16), value_rows, preferred_element_type=jnp.float32
                )
                return (new_max, new_sum, new_weighted)

            final_max, final_sum, weighted = lax.fori_loop(0, tile_count, visit, start_state)
            denominator = final_sum + jnp.exp(sink_logit - final_max)
            return (weighted / denominator[:, None]).astype(jnp.bfloat16)

        return lax.map(query_tile, jnp.arange(tile_count, dtype=jnp.int32)).reshape(total_rows, HD)

    attended = lax.map(one_head, jnp.arange(heads_local, dtype=jnp.int32))
    returned = lax.all_to_all(attended, "seq", split_axis=1, concat_axis=0, tiled=True)
    hidden = returned.transpose(1, 0, 2).reshape(tok_rows, HEADS * HD)
    page_count = total_rows // PAGE + SEGS
    page_index = block_table.reshape(-1)[segment * block_table.shape[1] + position // PAGE]
    cache_row = page_index * PAGE + position % PAGE

    def place(values_in):
        flat_cache = (
            jnp.zeros((page_count * PAGE, heads_local, HD), jnp.bfloat16)
            .at[cache_row]
            .set(values_in)
        )
        return (
            flat_cache.reshape(page_count, PAGE, heads_local, HD)
            .transpose(2, 0, 1, 3)
            .reshape(heads_local, page_count, PAGE * HD)
        )

    kv_cache = jnp.stack([place(arrived[:, 1]), place(arrived[:, 2])], axis=2)
    return (hidden, kv_cache)


LANES = 128
BF16 = jnp.bfloat16
F32 = jnp.float32
ANYWHERE = pl.BlockSpec(memory_space=pl.ANY)
IN_HBM = pl.BlockSpec(memory_space=pltpu.HBM)
IN_VMEM = pl.BlockSpec(memory_space=pltpu.VMEM)
IN_SMEM = pl.BlockSpec(memory_space=pltpu.SMEM)


def sends(group_size):
    return sorted(range(1, group_size), key=lambda bits: (-bits.bit_count(), bits))


def to_partner(values, bits, group_size):
    return lax.ppermute(values, "seq", [(i, i ^ bits) for i in range(group_size)])


def params(mebibytes=40):
    return pltpu.CompilerParams(vmem_limit_bytes=mebibytes * 1024 * 1024)


def stay(values):
    return pltpu.with_memory_space_constraint(values, pltpu.HBM)


def cost(flops, moved):
    return pl.CostEstimate(flops=flops, bytes_accessed=moved, transcendentals=0)


def column_copies(shared, outs, sem, width, tiles, group_size):
    me = lax.axis_index("seq")
    span = (tiles[1] - tiles[0]) * LANES
    copies = []
    for n, bits in enumerate(sends(group_size) + [0]):
        owner = jnp.bitwise_xor(me, bits)
        for c in range(3):
            first = pl.multiple_of(c * HEADS * HD + owner * width + tiles[0] * LANES, LANES)
            copies.append(
                pltpu.make_async_copy(
                    shared.at[:, pl.ds(first, span)],
                    outs[n].at[:, pl.ds(c * span, span)],
                    sem.at[n, c],
                )
            )
    return copies


def make_codes(inputs, adapter_down, shared_qkv, width, tiles, group_size):
    tok_rows, depth = inputs.shape
    code_width = adapter_down.shape[1]
    steps = 8
    chunk = depth // steps
    span = 3 * (tiles[1] - tiles[0]) * LANES

    def body(inputs_ref, down_ref, shared, *refs):
        outs, (held, down, in_sem, down_sem, sem) = refs[:-5], refs[-5:]
        loads = []
        for step in range(steps):
            at = pl.ds(step * chunk, chunk)
            loads.append(
                (
                    pltpu.make_async_copy(inputs_ref.at[:, at], held.at[:, at], in_sem.at[step]),
                    pltpu.make_async_copy(down_ref.at[at, :], down.at[at, :], down_sem.at[step]),
                )
            )
            for load in loads[-1]:
                load.start()
        copies = column_copies(shared, outs, sem, width, tiles, group_size)
        for copy in copies:
            copy.start()
        total = None
        for step in range(steps):
            for load in loads[step]:
                load.wait()
            at = slice(step * chunk, (step + 1) * chunk)
            term = jnp.dot(held[:, at], down[at, :], preferred_element_type=F32)
            total = term if total is None else total + term
        own_codes = total.astype(BF16)
        for out in outs:
            out[:, span:] = own_codes
        for copy in copies:
            copy.wait()

    return pl.pallas_call(
        body,
        out_shape=[jax.ShapeDtypeStruct((tok_rows, span + code_width), BF16)] * group_size,
        in_specs=[IN_HBM, IN_HBM, IN_HBM],
        out_specs=[IN_VMEM] * group_size,
        scratch_shapes=[
            pltpu.VMEM((tok_rows, depth), BF16),
            pltpu.VMEM((depth, code_width), BF16),
            pltpu.SemaphoreType.DMA((steps,)),
            pltpu.SemaphoreType.DMA((steps,)),
            pltpu.SemaphoreType.DMA((group_size, 3)),
        ],
        compiler_params=params(20),
        cost_estimate=cost(2 * tok_rows * depth * code_width, depth * code_width * 2),
        name="make_codes",
    )(stay(inputs), stay(adapter_down), stay(shared_qkv))


def pack_qkv(shared_qkv, after, width, tiles, group_size):
    tok_rows = shared_qkv.shape[0]
    span = 3 * (tiles[1] - tiles[0]) * LANES

    def body(shared, _, *refs):
        copies = column_copies(shared, refs[:-1], refs[-1], width, tiles, group_size)
        for copy in copies:
            copy.start()
        for copy in copies:
            copy.wait()

    return pl.pallas_call(
        body,
        out_shape=[jax.ShapeDtypeStruct((tok_rows, span), BF16)] * group_size,
        in_specs=[IN_HBM, ANYWHERE],
        out_specs=[IN_VMEM] * group_size,
        scratch_shapes=[pltpu.SemaphoreType.DMA((group_size, 3))],
        compiler_params=params(20),
        cost_estimate=cost(0, 2 * group_size * tok_rows * span * 2),
        name="pack_qkv",
    )(stay(shared_qkv), after)


def head_tiles(h):
    return (h * HD // LANES, -(-(h + 1) * HD // LANES))


def side_by_side(ref, window, rows):
    return jnp.concatenate([ref[tile, rows, :] for tile in window], axis=1)


def attend(up, sink_logits, lengths, low_rank, arrived, carried, after, heads, tiles, done_tiles, group_size):
    tok_rows = arrived[0].shape[0]
    total_rows = tok_rows * group_size
    window_span = total_rows // 2
    scale_factor = HD ** (-0.5)
    span = (tiles[1] - tiles[0]) * LANES
    done_span = (done_tiles[1] - done_tiles[0]) * LANES
    low_tile = min(tiles[0], done_tiles[0])
    kept = (tiles[0] - low_tile) * LANES
    left = (tiles[1] - done_tiles[1]) * LANES
    first_call, last = low_rank is None, left == 0
    all_tiles = (kept + span) // LANES
    given_low = [] if first_call else [low_rank]
    rest = up.shape[2] - tiles[1] * LANES

    def body(*refs):
        refs = list(refs)
        take = lambda n: [refs.pop(0) for _ in range(n)]
        up_ref, sinks, lens = take(3)
        low_refs = take(len(given_low))
        arrived_refs = take(group_size)
        before = take(len(carried))
        take(len(after))
        outs = take(group_size)
        keys, values = take(2)
        carried_out = take(0 if last else 3)
        queries, merged = take(2)
        me = lax.axis_index("seq")
        kept_tiles = kept // LANES
        if kept:
            for target, source in zip((queries, merged, keys, values), before):
                target[:kept_tiles] = source[source.shape[0] - kept_tiles :]
        for bits in range(group_size):
            source = arrived_refs[bits]
            place = pl.ds(pl.multiple_of(jnp.bitwise_xor(me, bits) * tok_rows, tok_rows), tok_rows)
            for c, target in enumerate((queries, keys, values)):
                if first_call:
                    at = 3 * span + c * RANK
                    codes = source[:, at : at + RANK]
                    low = jnp.dot(codes, up_ref[c, :, :span], preferred_element_type=F32)
                    carried_out[0][bits, :, c * rest : (c + 1) * rest] = jnp.dot(
                        codes, up_ref[c, :, span:], preferred_element_type=F32
                    )
                else:
                    low = low_refs[0][bits, :, c * span : (c + 1) * span]
                base = source[:, c * span : (c + 1) * span].astype(F32)
                new = (base + low).astype(BF16)
                for n in range(tiles[1] - tiles[0]):
                    target[kept_tiles + n, place, :] = new[:, n * LANES : (n + 1) * LANES]

        ends = []
        for s in range(SEGS):
            ends.append(lens[s] + (ends[-1] if ends else 0))
        blocks = []
        for b in range(group_size):
            first_query = b * tok_rows
            rows = slice(first_query, first_query + tok_rows)
            first_key = max(0, (first_query - window_span + 1) // tok_rows * tok_rows)
            key_rows = slice(first_key, first_query + tok_rows)
            query_place = first_query + lax.broadcasted_iota(jnp.int32, (tok_rows, 1), 0)
            earliest = query_place - (window_span - 1)
            for s in range(SEGS):
                earliest = jnp.where(ends[s] <= query_place, jnp.maximum(earliest, ends[s]), earliest)
            key_place = first_key + lax.broadcasted_iota(jnp.int32, (tok_rows, key_rows.stop - first_key), 1)
            visible = (key_place >= earliest) & (key_place <= query_place)
            scores = {}
            for h in heads:
                first_tile, end_tile = head_tiles(h)
                window = range(first_tile - low_tile, end_tile - low_tile)
                column = first_tile * LANES + lax.broadcasted_iota(jnp.int32, (1, len(window) * LANES), 1)
                mine = (column >= h * HD) & (column < (h + 1) * HD)
                query = side_by_side(queries, window, rows)
                query = jnp.where(mine, query, jnp.zeros_like(query))
                scores[h] = lax.dot_general(
                    query,
                    side_by_side(keys, window, key_rows),
                    (((1,), (1,)), ((), ())),
                    preferred_element_type=F32,
                )
            blocks.append((rows, key_rows, visible, scores))
        for rows, key_rows, visible, scores in blocks:
            parts = {}
            for tile in range(low_tile, tiles[0]):
                parts[tile] = merged[tile - low_tile, rows, :].astype(F32)
            for h in heads:
                first_tile, end_tile = head_tiles(h)
                window = range(first_tile - low_tile, end_tile - low_tile)
                seen = jnp.where(visible, scores[h] * scale_factor, -jnp.inf)
                top = jnp.maximum(jnp.max(seen, axis=1, keepdims=True), sinks[h])
                weights = jnp.exp(seen - top)
                denominator = jnp.sum(weights, axis=1, keepdims=True) + jnp.exp(sinks[h] - top)
                mixed = jnp.dot(
                    weights.astype(BF16),
                    side_by_side(values, window, key_rows),
                    preferred_element_type=F32,
                ) / denominator
                for tile in range(first_tile, end_tile):
                    at = (tile - first_tile) * LANES
                    piece = mixed[:, at : at + LANES]
                    if tile in parts:
                        lane = tile * LANES + lax.broadcasted_iota(jnp.int32, (1, LANES), 1)
                        piece = jnp.where(lane < h * HD, parts[tile], piece)
                    parts[tile] = piece
            for tile, piece in parts.items():
                merged[tile - low_tile, rows, :] = piece.astype(BF16)
        for bits in range(group_size):
            place = pl.ds(pl.multiple_of(jnp.bitwise_xor(me, bits) * tok_rows, tok_rows), tok_rows)
            outs[bits][...] = side_by_side(merged, range(done_tiles[1] - done_tiles[0]), place)
        if not last:
            carried_out[1][...] = queries[all_tiles - left // LANES :]
            carried_out[2][...] = merged[all_tiles - left // LANES :]

    block = jax.ShapeDtypeStruct((tok_rows, done_span), BF16)
    stream = jax.ShapeDtypeStruct((all_tiles, total_rows, LANES), BF16)
    leftover = jax.ShapeDtypeStruct((left // LANES, total_rows, LANES), BF16)
    next_low = jax.ShapeDtypeStruct((group_size, tok_rows, 3 * rest), F32)
    out_shape = [block] * group_size + [stream] * 2 + ([] if last else [next_low, leftover, leftover])
    results = pl.pallas_call(
        body,
        out_shape=out_shape,
        in_specs=[IN_VMEM, IN_SMEM, IN_SMEM]
        + [IN_VMEM] * (len(given_low) + group_size + len(carried))
        + [ANYWHERE] * len(after),
        out_specs=[IN_VMEM] * len(out_shape),
        scratch_shapes=[pltpu.VMEM((all_tiles, total_rows, LANES), BF16)] * 2,
        compiler_params=params(),
        cost_estimate=cost(4 * total_rows * total_rows * span, 8 * total_rows * span * 2),
        name="attend",
    )(up, sink_logits, lengths, *given_low, *arrived, *carried, *map(stay, after))
    blocks, (keys, values) = results[:group_size], results[group_size : group_size + 2]
    if last:
        return blocks, keys, values, None, []
    next_low, *leftovers = results[group_size + 2 :]
    return blocks, keys, values, next_low, [*leftovers, keys, values]


def build_cache(cache, after, keys, values, first_tile, lengths, block_table, heads, heads_local):
    total_rows, width = keys.shape[1], keys.shape[0] * LANES
    page_count = total_rows // PAGE + SEGS
    blocks = block_table.shape[1]
    rows = 2 * page_count
    given = [] if cache is None else [cache]

    def body(*refs):
        refs = list(refs)
        take = lambda n: [refs.pop(0) for _ in range(n)]
        key_ref, value_ref, lens, table = take(4)
        take(len(given) + len(after))
        out, built, sem = take(3)
        row = lax.broadcasted_iota(jnp.int32, (rows, blocks), 0)
        page = lax.shift_right_logical(row, 1)
        block = lax.broadcasted_iota(jnp.int32, (rows, blocks), 1)
        first = jnp.zeros((rows, blocks), jnp.int32)
        count = jnp.zeros((rows, blocks), jnp.int32)
        start = 0
        for s in range(SEGS):
            left = lens[s] - block * PAGE
            held = (table[s : s + 1, :] == page) & (left > 0)
            first = jnp.where(held, start + block * PAGE, first)
            count = jnp.where(held, jnp.minimum(left, PAGE), count)
            start = start + lens[s]
        first = jnp.sum(first, axis=1, keepdims=True)
        count = jnp.sum(count, axis=1, keepdims=True)
        odd = jnp.bitwise_and(lax.broadcasted_iota(jnp.int32, (rows, 1), 0), 1)
        place = lax.broadcasted_iota(jnp.int32, (rows, total_rows), 1)
        every = (range(keys.shape[0]), slice(None))
        all_keys, all_values = side_by_side(key_ref, *every), side_by_side(value_ref, *every)
        picked = []
        for r in range(PAGE):
            for_keys = jnp.where((odd == 0) & (count > r), first + r, -1)
            for_values = jnp.where((odd == 1) & (count > r), first + r, -1)
            pick_keys = (place == for_keys).astype(F32).astype(BF16)
            pick_values = (place == for_values).astype(F32).astype(BF16)
            picked.append(
                jnp.dot(pick_keys, all_keys, preferred_element_type=F32)
                + jnp.dot(pick_values, all_values, preferred_element_type=F32)
            )
        copies = []
        for n, h in enumerate(heads):
            lo = h * HD - first_tile * LANES
            line = jnp.concatenate([columns[:, lo : lo + HD] for columns in picked], axis=1)
            built[n] = line.astype(BF16).reshape(page_count, 2, PAGE * HD)
            copies.append(pltpu.make_async_copy(built.at[n], out.at[h], sem.at[n]))
            copies[-1].start()
        for copy in copies:
            copy.wait()

    return pl.pallas_call(
        body,
        out_shape=jax.ShapeDtypeStruct((heads_local, page_count, 2, PAGE * HD), BF16),
        in_specs=[IN_VMEM, IN_VMEM, IN_SMEM, IN_VMEM] + [IN_HBM] * len(given) + [ANYWHERE] * len(after),
        out_specs=IN_HBM,
        scratch_shapes=[
            pltpu.VMEM((len(heads), page_count, 2, PAGE * HD), BF16),
            pltpu.SemaphoreType.DMA((len(heads),)),
        ],
        input_output_aliases={4: 0} if given else {},
        compiler_params=params(),
        cost_estimate=cost(4 * rows * PAGE * total_rows * width, 4 * total_rows * width * 2),
        name="build_cache",
    )(keys, values, lengths, block_table, *map(stay, given), *map(stay, after))


def join_heads(hidden, blocks, first_column, width, group_size):
    tok_rows, span = blocks[0].shape
    given = [] if hidden is None else [hidden]

    def body(*refs):
        sources, out, sem = refs[:group_size], refs[-2], refs[-1]
        me = lax.axis_index("seq")
        copies = []
        for bits in range(group_size):
            first = pl.multiple_of(jnp.bitwise_xor(me, bits) * width + first_column, LANES)
            copies.append(
                pltpu.make_async_copy(sources[bits], out.at[:, pl.ds(first, span)], sem.at[bits])
            )
        for copy in copies:
            copy.start()
        for copy in copies:
            copy.wait()

    return pl.pallas_call(
        body,
        out_shape=jax.ShapeDtypeStruct((tok_rows, width * group_size), BF16),
        in_specs=[ANYWHERE] * group_size + [IN_HBM] * len(given),
        out_specs=IN_HBM,
        scratch_shapes=[pltpu.SemaphoreType.DMA((group_size,))],
        input_output_aliases={group_size: 0} if given else {},
        compiler_params=params(),
        cost_estimate=cost(0, 2 * tok_rows * span * group_size * 2),
        name="join_heads",
    )(*blocks, *map(stay, given))


def per_device_tiled(inputs, adapter_down, adapter_up, shared_qkv, sink_logits, lengths, block_table):
    group_size = lax.axis_size("seq")
    partners = sends(group_size)
    width = adapter_up.shape[2]
    heads_local = width // HD
    half = heads_local // 2
    all_tiles = width // LANES
    cut = -(-half * HD // LANES)
    done_cut = half * HD // LANES
    tiles = [(0, cut), (cut, all_tiles)]
    done_tiles = [(0, done_cut), (done_cut, all_tiles)]
    heads = [tuple(range(half)), tuple(range(half, heads_local))]

    def send(parts):
        return {bits: to_partner(part, bits, group_size) for bits, part in zip(partners, parts)}

    *parts, own = make_codes(inputs, adapter_down, shared_qkv, width, tiles[0], group_size)
    arrived = [{0: own, **send(parts)}]
    *parts, own = pack_qkv(shared_qkv, own, width, tiles[1], group_size)
    arrived.append({0: own, **send(parts)})
    low_rank, carried, cache, hidden = None, [], None, None
    for n in range(2):
        blocks, keys, values, low_rank, carried = attend(
            adapter_up,
            sink_logits,
            lengths,
            low_rank,
            [arrived[n][bits] for bits in range(group_size)],
            carried,
            [] if cache is None else [cache],
            heads[n],
            tiles[n],
            done_tiles[n],
            group_size,
        )
        returned = send([blocks[bits] for bits in partners])
        returned[0] = blocks[0]
        cache = build_cache(
            cache,
            [] if hidden is None else [hidden],
            keys,
            values,
            done_tiles[n][0],
            lengths,
            block_table,
            heads[n],
            heads_local,
        )
        hidden = join_heads(
            hidden, [returned[bits] for bits in range(group_size)], done_tiles[n][0] * LANES, width, group_size
        )
    return (hidden, cache)


def per_device(inputs, adapter_down, adapter_up, shared_qkv, sink_logits, lengths, block_table):
    group_size = lax.axis_size("seq")
    width = adapter_up.shape[2]
    tiled = (
        group_size & (group_size - 1) == 0
        and width % (2 * HD) == 0
        and width % LANES == 0
        and inputs.shape[0] % LANES == 0
        and inputs.shape[0] * group_size <= 512
    )
    chosen = per_device_tiled if tiled else per_device_general
    return chosen(inputs, adapter_down, adapter_up, shared_qkv, sink_logits, lengths, block_table)


def solution(mesh):
    return jax.shard_map(
        per_device,
        mesh=mesh,
        in_specs=(
            P(("batch", "seq"), None),
            P(),
            P(None, None, "seq"),
            P(("batch", "seq"), None),
            P("seq"),
            P("batch"),
            P("batch", None),
        ),
        out_specs=(P(("batch", "seq"), None), P("seq", "batch", None, None)),
        check_vma=False,
    )
```

```python
import jax
import jax.numpy as jnp
from jax import lax
from jax.experimental import pallas as pl
from jax.experimental.pallas import tpu as pltpu
from jax.sharding import PartitionSpec as P

HD = 224
RANK = 128
HEADS = 16
SEGS = 8
PAGE = 16


def segment_positions(lengths, total_rows):
    segment_ends = jnp.cumsum(lengths)
    segment_starts = segment_ends - lengths
    places = jnp.arange(total_rows, dtype=jnp.int32)
    segment = jnp.sum((places[:, None] >= segment_ends[None, :]).astype(jnp.int32), axis=1)
    member = segment[:, None] == jnp.arange(SEGS, dtype=jnp.int32)[None, :]
    offsets = jnp.sum(jnp.where(member, segment_starts[None, :], 0), axis=1)
    return (segment, places - offsets)


def per_device_general(inputs, adapter_down, adapter_up, shared_qkv, sink_logits, lengths, block_table):
    group_size = lax.axis_size("seq")
    tok_rows = inputs.shape[0]
    total_rows = tok_rows * group_size
    heads_local = adapter_up.shape[2] // HD
    window_span = total_rows // 2
    low_codes = jnp.dot(inputs, adapter_down, preferred_element_type=jnp.float32).astype(
        jnp.bfloat16
    )
    shared_base = shared_qkv.reshape(tok_rows, 3, HEADS * HD)
    low_rank = jnp.einsum(
        "tcr,crf->tcf",
        low_codes.reshape(tok_rows, 3, RANK),
        lax.all_gather(adapter_up, "seq", axis=2, tiled=True),
        preferred_element_type=jnp.float32,
    )
    merged = (shared_base.astype(jnp.float32) + low_rank).astype(jnp.bfloat16)
    sending = merged.reshape(tok_rows, 3, HEADS, HD)
    arrived = lax.all_to_all(sending, "seq", split_axis=2, concat_axis=0, tiled=True)
    segment, position = segment_positions(lengths, total_rows)
    tile_rows = min(512, total_rows)
    tile_count = total_rows // tile_rows
    scale_factor = HD ** (-0.5)

    def one_head(head_index):
        query_all = arrived[:, 0, head_index]
        key_all = arrived[:, 1, head_index]
        value_all = arrived[:, 2, head_index]
        sink_logit = sink_logits[head_index]

        def query_tile(tile_index):
            query_first = tile_index * tile_rows
            query_rows = lax.dynamic_slice_in_dim(query_all, query_first, tile_rows, 0)
            query_segs = lax.dynamic_slice_in_dim(segment, query_first, tile_rows, 0)
            query_place = query_first + jnp.arange(tile_rows, dtype=jnp.int32)
            start_state = (
                jnp.full((tile_rows,), sink_logit, jnp.float32),
                jnp.zeros((tile_rows,), jnp.float32),
                jnp.zeros((tile_rows, HD), jnp.float32),
            )

            def visit(key_tile, state):
                key_first = key_tile * tile_rows
                running_max, running_sum, weighted = state
                key_rows = lax.dynamic_slice_in_dim(key_all, key_first, tile_rows, 0)
                value_rows = lax.dynamic_slice_in_dim(value_all, key_first, tile_rows, 0)
                key_segs = lax.dynamic_slice_in_dim(segment, key_first, tile_rows, 0)
                key_place = key_first + jnp.arange(tile_rows, dtype=jnp.int32)
                scores = (
                    jnp.dot(query_rows, key_rows.T, preferred_element_type=jnp.float32)
                    * scale_factor
                )
                visible = (
                    (query_segs[:, None] == key_segs[None, :])
                    & (key_place[None, :] <= query_place[:, None])
                    & (query_place[:, None] - key_place[None, :] < window_span)
                )
                scores = jnp.where(visible, scores, -jnp.inf)
                new_max = jnp.maximum(running_max, jnp.max(scores, axis=1))
                rescale = jnp.exp(running_max - new_max)
                weights = jnp.exp(scores - new_max[:, None])
                new_sum = running_sum * rescale + jnp.sum(weights, axis=1)
                new_weighted = weighted * rescale[:, None] + jnp.dot(
                    weights.astype(jnp.bfloat16), value_rows, preferred_element_type=jnp.float32
                )
                return (new_max, new_sum, new_weighted)

            final_max, final_sum, weighted = lax.fori_loop(0, tile_count, visit, start_state)
            denominator = final_sum + jnp.exp(sink_logit - final_max)
            return (weighted / denominator[:, None]).astype(jnp.bfloat16)

        return lax.map(query_tile, jnp.arange(tile_count, dtype=jnp.int32)).reshape(total_rows, HD)

    attended = lax.map(one_head, jnp.arange(heads_local, dtype=jnp.int32))
    returned = lax.all_to_all(attended, "seq", split_axis=1, concat_axis=0, tiled=True)
    hidden = returned.transpose(1, 0, 2).reshape(tok_rows, HEADS * HD)
    page_count = total_rows // PAGE + SEGS
    page_index = block_table.reshape(-1)[segment * block_table.shape[1] + position // PAGE]
    cache_row = page_index * PAGE + position % PAGE

    def place(values_in):
        flat_cache = (
            jnp.zeros((page_count * PAGE, heads_local, HD), jnp.bfloat16)
            .at[cache_row]
            .set(values_in)
        )
        return (
            flat_cache.reshape(page_count, PAGE, heads_local, HD)
            .transpose(2, 0, 1, 3)
            .reshape(heads_local, page_count, PAGE * HD)
        )

    kv_cache = jnp.stack([place(arrived[:, 1]), place(arrived[:, 2])], axis=2)
    return (hidden, kv_cache)


LANES = 128
BF16 = jnp.bfloat16
F32 = jnp.float32
ANYWHERE = pl.BlockSpec(memory_space=pl.ANY)
IN_HBM = pl.BlockSpec(memory_space=pltpu.HBM)
IN_VMEM = pl.BlockSpec(memory_space=pltpu.VMEM)
IN_SMEM = pl.BlockSpec(memory_space=pltpu.SMEM)


def sends(group_size):
    return sorted(range(1, group_size), key=lambda bits: (-bits.bit_count(), bits))


def to_partner(values, bits, group_size):
    return lax.ppermute(values, "seq", [(i, i ^ bits) for i in range(group_size)])


def map_partners(partners, parts, group_size):
    sent = [to_partner(part, bits, group_size) for bits, part in zip(partners, parts)]
    return sent + list(parts[len(partners) :])


def params(mebibytes=40):
    return pltpu.CompilerParams(vmem_limit_bytes=mebibytes * 1024 * 1024)


def stay(values):
    return pltpu.with_memory_space_constraint(values, pltpu.HBM)


def cost(flops, moved):
    return pl.CostEstimate(flops=flops, bytes_accessed=moved, transcendentals=0)


def start_columns(shared, outs, sem, width, tiles, wanted):
    me = lax.axis_index("seq")
    span = (tiles[1] - tiles[0]) * LANES
    copies = []
    for n, (bits, kinds) in enumerate(wanted):
        owner = jnp.bitwise_xor(me, bits)
        for m, c in enumerate(kinds):
            first = pl.multiple_of(c * HEADS * HD + owner * width + tiles[0] * LANES, LANES)
            copies.append(
                pltpu.make_async_copy(
                    shared.at[:, pl.ds(first, span)],
                    outs[n].at[:, pl.ds(m * span, span)],
                    sem.at[n, m],
                )
            )
    for copy in copies:
        copy.start()
    return copies


def make_codes(inputs, adapter_down, shared_qkv, after, width, tiles, wanted):
    tok_rows, depth = inputs.shape
    code_width = adapter_down.shape[1]
    steps = 8
    chunk = depth // steps
    spans = [len(kinds) * (tiles[1] - tiles[0]) * LANES for _, kinds in wanted]

    def body(inputs_ref, down_ref, shared, _, *refs):
        outs, (held, down, in_sem, down_sem, sem) = refs[:-5], refs[-5:]
        loads = []
        for step in range(steps):
            at = pl.ds(step * chunk, chunk)
            loads.append(
                (
                    pltpu.make_async_copy(inputs_ref.at[:, at], held.at[:, at], in_sem.at[step]),
                    pltpu.make_async_copy(down_ref.at[at, :], down.at[at, :], down_sem.at[step]),
                )
            )
            for load in loads[-1]:
                load.start()
        copies = start_columns(shared, outs, sem, width, tiles, wanted)
        total = None
        for step in range(steps):
            for load in loads[step]:
                load.wait()
            at = slice(step * chunk, (step + 1) * chunk)
            term = jnp.dot(held[:, at], down[at, :], preferred_element_type=F32)
            total = term if total is None else total + term
        own_codes = total.astype(BF16)
        for out, span in zip(outs, spans):
            out[:, span:] = own_codes
        for copy in copies:
            copy.wait()

    return pl.pallas_call(
        body,
        out_shape=[jax.ShapeDtypeStruct((tok_rows, span + code_width), BF16) for span in spans],
        in_specs=[IN_HBM, IN_HBM, IN_HBM, ANYWHERE],
        out_specs=[IN_VMEM] * len(wanted),
        scratch_shapes=[
            pltpu.VMEM((tok_rows, depth), BF16),
            pltpu.VMEM((depth, code_width), BF16),
            pltpu.SemaphoreType.DMA((steps,)),
            pltpu.SemaphoreType.DMA((steps,)),
            pltpu.SemaphoreType.DMA((len(wanted), 3)),
        ],
        compiler_params=params(20),
        cost_estimate=cost(2 * tok_rows * depth * code_width, depth * code_width * 2),
        name="make_codes",
    )(stay(inputs), stay(adapter_down), stay(shared_qkv), after)


def pack_qkv(shared_qkv, after, width, tiles, wanted):
    tok_rows = shared_qkv.shape[0]
    spans = [len(kinds) * (tiles[1] - tiles[0]) * LANES for _, kinds in wanted]

    def body(shared, *refs):
        outs, sem = refs[len(after) : -1], refs[-1]
        for copy in start_columns(shared, outs, sem, width, tiles, wanted):
            copy.wait()

    return pl.pallas_call(
        body,
        out_shape=[jax.ShapeDtypeStruct((tok_rows, span), BF16) for span in spans],
        in_specs=[IN_HBM] + [ANYWHERE] * len(after),
        out_specs=[IN_VMEM] * len(wanted),
        scratch_shapes=[pltpu.SemaphoreType.DMA((len(wanted), 3))],
        compiler_params=params(20),
        cost_estimate=cost(0, 2 * tok_rows * sum(spans) * 2),
        name="pack_qkv",
    )(stay(shared_qkv), *after)


def head_tiles(h):
    return (h * HD // LANES, -(-(h + 1) * HD // LANES))


def side_by_side(ref, window, rows):
    return jnp.concatenate([ref[tile, rows, :] for tile in window], axis=1)


def attend(up, sink_logits, lengths, low_rank, arrived, places, carried, after, heads, tiles, done_tiles):
    group_size = len(places)
    tok_rows = arrived[0].shape[0]
    total_rows = tok_rows * group_size
    window_span = total_rows // 2
    scale_factor = HD ** (-0.5)
    span = (tiles[1] - tiles[0]) * LANES
    done_span = (done_tiles[1] - done_tiles[0]) * LANES
    low_tile = min(tiles[0], done_tiles[0])
    kept = (tiles[0] - low_tile) * LANES
    left = (tiles[1] - done_tiles[1]) * LANES
    first_call, last = low_rank is None, left == 0
    all_tiles = (kept + span) // LANES
    given_low = [] if first_call else [low_rank]
    rest = up.shape[2] - tiles[1] * LANES

    def body(*refs):
        refs = list(refs)
        take = lambda n: [refs.pop(0) for _ in range(n)]
        up_ref, sinks, lens = take(3)
        low_refs = take(len(given_low))
        arrived_refs = take(len(arrived))
        before = take(len(carried))
        take(len(after))
        outs = take(group_size)
        keys, values = take(2)
        carried_out = take(0 if last else 3)
        queries, merged = take(2)
        me = lax.axis_index("seq")
        kept_tiles = kept // LANES
        if kept:
            for target, source in zip((queries, merged, keys, values), before):
                target[:kept_tiles] = source[source.shape[0] - kept_tiles :]
        for bits in range(group_size):
            place = pl.ds(pl.multiple_of(jnp.bitwise_xor(me, bits) * tok_rows, tok_rows), tok_rows)
            for c, target in enumerate((queries, keys, values)):
                if first_call:
                    which, at = places[bits][3]
                    codes = arrived_refs[which][:, at + c * RANK : at + (c + 1) * RANK]
                    low = jnp.dot(codes, up_ref[c, :, :span], preferred_element_type=F32)
                    carried_out[0][bits, :, c * rest : (c + 1) * rest] = jnp.dot(
                        codes, up_ref[c, :, span:], preferred_element_type=F32
                    )
                else:
                    low = low_refs[0][bits, :, c * span : (c + 1) * span]
                which, at = places[bits][c]
                base = arrived_refs[which][:, at : at + span].astype(F32)
                new = (base + low).astype(BF16)
                for n in range(tiles[1] - tiles[0]):
                    target[kept_tiles + n, place, :] = new[:, n * LANES : (n + 1) * LANES]

        ends = []
        for s in range(SEGS):
            ends.append(lens[s] + (ends[-1] if ends else 0))
        blocks = []
        for b in range(group_size):
            first_query = b * tok_rows
            rows = slice(first_query, first_query + tok_rows)
            first_key = max(0, (first_query - window_span + 1) // tok_rows * tok_rows)
            key_rows = slice(first_key, first_query + tok_rows)
            query_place = first_query + lax.broadcasted_iota(jnp.int32, (tok_rows, 1), 0)
            earliest = query_place - (window_span - 1)
            for s in range(SEGS):
                earliest = jnp.where(ends[s] <= query_place, jnp.maximum(earliest, ends[s]), earliest)
            key_place = first_key + lax.broadcasted_iota(jnp.int32, (tok_rows, key_rows.stop - first_key), 1)
            visible = (key_place >= earliest) & (key_place <= query_place)
            scores = {}
            for h in heads:
                first_tile, end_tile = head_tiles(h)
                window = range(first_tile - low_tile, end_tile - low_tile)
                column = first_tile * LANES + lax.broadcasted_iota(jnp.int32, (1, len(window) * LANES), 1)
                mine = (column >= h * HD) & (column < (h + 1) * HD)
                query = side_by_side(queries, window, rows)
                query = jnp.where(mine, query, jnp.zeros_like(query))
                scores[h] = lax.dot_general(
                    query,
                    side_by_side(keys, window, key_rows),
                    (((1,), (1,)), ((), ())),
                    preferred_element_type=F32,
                )
            blocks.append((rows, key_rows, visible, scores))
        for rows, key_rows, visible, scores in blocks:
            parts = {}
            for tile in range(low_tile, tiles[0]):
                parts[tile] = merged[tile - low_tile, rows, :].astype(F32)
            for h in heads:
                first_tile, end_tile = head_tiles(h)
                window = range(first_tile - low_tile, end_tile - low_tile)
                seen = jnp.where(visible, scores[h] * scale_factor, -jnp.inf)
                top = jnp.maximum(jnp.max(seen, axis=1, keepdims=True), sinks[h])
                weights = jnp.exp(seen - top)
                denominator = jnp.sum(weights, axis=1, keepdims=True) + jnp.exp(sinks[h] - top)
                mixed = jnp.dot(
                    weights.astype(BF16),
                    side_by_side(values, window, key_rows),
                    preferred_element_type=F32,
                ) / denominator
                for tile in range(first_tile, end_tile):
                    at = (tile - first_tile) * LANES
                    piece = mixed[:, at : at + LANES]
                    if tile in parts:
                        lane = tile * LANES + lax.broadcasted_iota(jnp.int32, (1, LANES), 1)
                        piece = jnp.where(lane < h * HD, parts[tile], piece)
                    parts[tile] = piece
            for tile, piece in parts.items():
                merged[tile - low_tile, rows, :] = piece.astype(BF16)
        for bits in range(group_size):
            place = pl.ds(pl.multiple_of(jnp.bitwise_xor(me, bits) * tok_rows, tok_rows), tok_rows)
            outs[bits][...] = side_by_side(merged, range(done_tiles[1] - done_tiles[0]), place)
        if not last:
            carried_out[1][...] = queries[all_tiles - left // LANES :]
            carried_out[2][...] = merged[all_tiles - left // LANES :]

    block = jax.ShapeDtypeStruct((tok_rows, done_span), BF16)
    stream = jax.ShapeDtypeStruct((all_tiles, total_rows, LANES), BF16)
    leftover = jax.ShapeDtypeStruct((left // LANES, total_rows, LANES), BF16)
    next_low = jax.ShapeDtypeStruct((group_size, tok_rows, 3 * rest), F32)
    out_shape = [block] * group_size + [stream] * 2 + ([] if last else [next_low, leftover, leftover])
    results = pl.pallas_call(
        body,
        out_shape=out_shape,
        in_specs=[IN_VMEM, IN_SMEM, IN_SMEM]
        + [IN_VMEM] * (len(given_low) + len(arrived) + len(carried))
        + [ANYWHERE] * len(after),
        out_specs=[IN_VMEM] * len(out_shape),
        scratch_shapes=[pltpu.VMEM((all_tiles, total_rows, LANES), BF16)] * 2,
        compiler_params=params(),
        cost_estimate=cost(4 * total_rows * total_rows * span, 8 * total_rows * span * 2),
        name="attend",
    )(up, sink_logits, lengths, *given_low, *arrived, *carried, *map(stay, after))
    blocks, (keys, values) = results[:group_size], results[group_size : group_size + 2]
    if last:
        return blocks, keys, values, None, []
    next_low, *leftovers = results[group_size + 2 :]
    return blocks, keys, values, next_low, [*leftovers, keys, values]


def build_cache(cache, after, keys, values, first_tile, lengths, block_table, heads, heads_local):
    total_rows, width = keys.shape[1], keys.shape[0] * LANES
    page_count = total_rows // PAGE + SEGS
    blocks = block_table.shape[1]
    rows = 2 * page_count
    given = [] if cache is None else [cache]

    def body(*refs):
        refs = list(refs)
        take = lambda n: [refs.pop(0) for _ in range(n)]
        key_ref, value_ref, lens, table = take(4)
        take(len(given) + len(after))
        out, built, sem = take(3)
        row = lax.broadcasted_iota(jnp.int32, (rows, blocks), 0)
        page = lax.shift_right_logical(row, 1)
        block = lax.broadcasted_iota(jnp.int32, (rows, blocks), 1)
        first = jnp.zeros((rows, blocks), jnp.int32)
        count = jnp.zeros((rows, blocks), jnp.int32)
        start = 0
        for s in range(SEGS):
            left = lens[s] - block * PAGE
            held = (table[s : s + 1, :] == page) & (left > 0)
            first = jnp.where(held, start + block * PAGE, first)
            count = jnp.where(held, jnp.minimum(left, PAGE), count)
            start = start + lens[s]
        first = jnp.sum(first, axis=1, keepdims=True)
        count = jnp.sum(count, axis=1, keepdims=True)
        odd = jnp.bitwise_and(lax.broadcasted_iota(jnp.int32, (rows, 1), 0), 1)
        place = lax.broadcasted_iota(jnp.int32, (4 * rows, total_rows), 1)
        every = (range(keys.shape[0]), slice(None))
        all_keys, all_values = side_by_side(key_ref, *every), side_by_side(value_ref, *every)
        copies = []
        group = 4
        for r in range(0, PAGE, group):
            wanted = [jnp.where(count > r + n, first + r + n, -1) for n in range(group)]
            for_keys = jnp.concatenate([jnp.where(odd == 0, want, -1) for want in wanted], axis=0)
            for_values = jnp.concatenate([jnp.where(odd == 1, want, -1) for want in wanted], axis=0)
            pick_keys = (place == for_keys).astype(F32).astype(BF16)
            pick_values = (place == for_values).astype(F32).astype(BF16)
            picked = jnp.dot(pick_keys, all_keys, preferred_element_type=F32) + jnp.dot(
                pick_values, all_values, preferred_element_type=F32
            )
            lanes = slice(r * HD, (r + group) * HD)
            for n, h in enumerate(heads):
                lo = h * HD - first_tile * LANES
                line = jnp.concatenate(
                    [picked[m * rows : (m + 1) * rows, lo : lo + HD] for m in range(group)], axis=1
                )
                built[n, :, :, lanes] = line.astype(BF16).reshape(page_count, 2, group * HD)
                copies.append(
                    pltpu.make_async_copy(
                        built.at[n, :, :, lanes], out.at[h, :, :, lanes], sem.at[n, r // group]
                    )
                )
                copies[-1].start()
        for copy in copies:
            copy.wait()

    return pl.pallas_call(
        body,
        out_shape=jax.ShapeDtypeStruct((heads_local, page_count, 2, PAGE * HD), BF16),
        in_specs=[IN_VMEM, IN_VMEM, IN_SMEM, IN_VMEM] + [IN_HBM] * len(given) + [ANYWHERE] * len(after),
        out_specs=IN_HBM,
        scratch_shapes=[
            pltpu.VMEM((len(heads), page_count, 2, PAGE * HD), BF16),
            pltpu.SemaphoreType.DMA((len(heads), 4)),
        ],
        input_output_aliases={4: 0} if given else {},
        compiler_params=params(),
        cost_estimate=cost(4 * rows * PAGE * total_rows * width, 4 * total_rows * width * 2),
        name="build_cache",
    )(keys, values, lengths, block_table, *map(stay, given), *map(stay, after))


def join_heads(hidden, blocks, first_column, width, group_size):
    tok_rows, span = blocks[0].shape
    given = [] if hidden is None else [hidden]

    def body(*refs):
        sources, out, sem = refs[:group_size], refs[-2], refs[-1]
        me = lax.axis_index("seq")
        copies = []
        for bits in range(group_size):
            first = pl.multiple_of(jnp.bitwise_xor(me, bits) * width + first_column, LANES)
            copies.append(
                pltpu.make_async_copy(sources[bits], out.at[:, pl.ds(first, span)], sem.at[bits])
            )
        for copy in copies:
            copy.start()
        for copy in copies:
            copy.wait()

    return pl.pallas_call(
        body,
        out_shape=jax.ShapeDtypeStruct((tok_rows, width * group_size), BF16),
        in_specs=[ANYWHERE] * group_size + [IN_HBM] * len(given),
        out_specs=IN_HBM,
        scratch_shapes=[pltpu.SemaphoreType.DMA((group_size,))],
        input_output_aliases={group_size: 0} if given else {},
        compiler_params=params(),
        cost_estimate=cost(0, 2 * tok_rows * span * group_size * 2),
        name="join_heads",
    )(*blocks, *map(stay, given))


def per_device_tiled(inputs, adapter_down, adapter_up, shared_qkv, sink_logits, lengths, block_table):
    group_size = lax.axis_size("seq")
    partners = sends(group_size)
    width = adapter_up.shape[2]
    heads_local = width // HD
    half = heads_local // 2
    all_tiles = width // LANES
    cut = -(-half * HD // LANES)
    done_cut = half * HD // LANES
    tiles = [(0, cut), (cut, all_tiles)]
    done_tiles = [(0, done_cut), (done_cut, all_tiles)]
    heads = [tuple(range(half)), tuple(range(half, heads_local))]

    def send(parts):
        return {bits: to_partner(part, bits, group_size) for bits, part in zip(partners, parts)}

    every = (0, 1, 2)
    first, others = partners[0], partners[1:]
    (early,) = pack_qkv(shared_qkv, [], width, tiles[0], [(first, (0, 1))])
    wanted = [(bits, every) for bits in others + [0]]
    parts = make_codes(inputs, adapter_down, shared_qkv, early, width, tiles[0], [(first, (2,))] + wanted)
    early = to_partner(early, first, group_size)
    arrived = [[early, *map_partners(partners, parts, group_size)]]
    parts = pack_qkv(shared_qkv, [parts[-1], early], width, tiles[1], [(first, every)] + wanted)
    arrived.append(map_partners(partners, parts, group_size))
    places = []
    for n in range(2):
        span = (tiles[n][1] - tiles[n][0]) * LANES
        columns = (0, span, 2 * span, 3 * span)
        at = {bits: [(m + 2 - n, column) for column in columns] for m, bits in enumerate(others + [0])}
        at[first] = [(0, 0), (0, span), (1, 0), (1, span)] if n == 0 else [(0, column) for column in columns]
        places.append([at[bits] for bits in range(group_size)])
    low_rank, carried, cache, hidden = None, [], None, None
    for n in range(2):
        blocks, keys, values, low_rank, carried = attend(
            adapter_up,
            sink_logits,
            lengths,
            low_rank,
            arrived[n],
            places[n],
            carried,
            [] if cache is None else [cache],
            heads[n],
            tiles[n],
            done_tiles[n],
        )
        returned = send([blocks[bits] for bits in partners])
        returned[0] = blocks[0]
        cache = build_cache(
            cache,
            [] if hidden is None else [hidden],
            keys,
            values,
            done_tiles[n][0],
            lengths,
            block_table,
            heads[n],
            heads_local,
        )
        hidden = join_heads(
            hidden, [returned[bits] for bits in range(group_size)], done_tiles[n][0] * LANES, width, group_size
        )
    return (hidden, cache)


def per_device(inputs, adapter_down, adapter_up, shared_qkv, sink_logits, lengths, block_table):
    group_size = lax.axis_size("seq")
    width = adapter_up.shape[2]
    tiled = (
        group_size & (group_size - 1) == 0
        and width % (2 * HD) == 0
        and width % LANES == 0
        and inputs.shape[0] % LANES == 0
        and inputs.shape[0] * group_size <= 512
    )
    chosen = per_device_tiled if tiled else per_device_general
    return chosen(inputs, adapter_down, adapter_up, shared_qkv, sink_logits, lengths, block_table)


def solution(mesh):
    return jax.shard_map(
        per_device,
        mesh=mesh,
        in_specs=(
            P(("batch", "seq"), None),
            P(),
            P(None, None, "seq"),
            P(("batch", "seq"), None),
            P("seq"),
            P("batch"),
            P("batch", None),
        ),
        out_specs=(P(("batch", "seq"), None), P("seq", "batch", None, None)),
        check_vma=False,
    )
```

```python
import jax
import jax.numpy as jnp
from jax import lax
from jax.experimental import pallas as pl
from jax.experimental.pallas import tpu as pltpu
from jax.sharding import PartitionSpec as P

HD = 224
RANK = 128
HEADS = 16
SEGS = 8
PAGE = 16


def segment_positions(lengths, total_rows):
    segment_ends = jnp.cumsum(lengths)
    segment_starts = segment_ends - lengths
    places = jnp.arange(total_rows, dtype=jnp.int32)
    segment = jnp.sum((places[:, None] >= segment_ends[None, :]).astype(jnp.int32), axis=1)
    member = segment[:, None] == jnp.arange(SEGS, dtype=jnp.int32)[None, :]
    offsets = jnp.sum(jnp.where(member, segment_starts[None, :], 0), axis=1)
    return (segment, places - offsets)


def per_device_general(inputs, adapter_down, adapter_up, shared_qkv, sink_logits, lengths, block_table):
    group_size = lax.axis_size("seq")
    tok_rows = inputs.shape[0]
    total_rows = tok_rows * group_size
    heads_local = adapter_up.shape[2] // HD
    window_span = total_rows // 2
    low_codes = jnp.dot(inputs, adapter_down, preferred_element_type=jnp.float32).astype(
        jnp.bfloat16
    )
    shared_base = shared_qkv.reshape(tok_rows, 3, HEADS * HD)
    low_rank = jnp.einsum(
        "tcr,crf->tcf",
        low_codes.reshape(tok_rows, 3, RANK),
        lax.all_gather(adapter_up, "seq", axis=2, tiled=True),
        preferred_element_type=jnp.float32,
    )
    merged = (shared_base.astype(jnp.float32) + low_rank).astype(jnp.bfloat16)
    sending = merged.reshape(tok_rows, 3, HEADS, HD)
    arrived = lax.all_to_all(sending, "seq", split_axis=2, concat_axis=0, tiled=True)
    segment, position = segment_positions(lengths, total_rows)
    tile_rows = min(512, total_rows)
    tile_count = total_rows // tile_rows
    scale_factor = HD ** (-0.5)

    def one_head(head_index):
        query_all = arrived[:, 0, head_index]
        key_all = arrived[:, 1, head_index]
        value_all = arrived[:, 2, head_index]
        sink_logit = sink_logits[head_index]

        def query_tile(tile_index):
            query_first = tile_index * tile_rows
            query_rows = lax.dynamic_slice_in_dim(query_all, query_first, tile_rows, 0)
            query_segs = lax.dynamic_slice_in_dim(segment, query_first, tile_rows, 0)
            query_place = query_first + jnp.arange(tile_rows, dtype=jnp.int32)
            start_state = (
                jnp.full((tile_rows,), sink_logit, jnp.float32),
                jnp.zeros((tile_rows,), jnp.float32),
                jnp.zeros((tile_rows, HD), jnp.float32),
            )

            def visit(key_tile, state):
                key_first = key_tile * tile_rows
                running_max, running_sum, weighted = state
                key_rows = lax.dynamic_slice_in_dim(key_all, key_first, tile_rows, 0)
                value_rows = lax.dynamic_slice_in_dim(value_all, key_first, tile_rows, 0)
                key_segs = lax.dynamic_slice_in_dim(segment, key_first, tile_rows, 0)
                key_place = key_first + jnp.arange(tile_rows, dtype=jnp.int32)
                scores = (
                    jnp.dot(query_rows, key_rows.T, preferred_element_type=jnp.float32)
                    * scale_factor
                )
                visible = (
                    (query_segs[:, None] == key_segs[None, :])
                    & (key_place[None, :] <= query_place[:, None])
                    & (query_place[:, None] - key_place[None, :] < window_span)
                )
                scores = jnp.where(visible, scores, -jnp.inf)
                new_max = jnp.maximum(running_max, jnp.max(scores, axis=1))
                rescale = jnp.exp(running_max - new_max)
                weights = jnp.exp(scores - new_max[:, None])
                new_sum = running_sum * rescale + jnp.sum(weights, axis=1)
                new_weighted = weighted * rescale[:, None] + jnp.dot(
                    weights.astype(jnp.bfloat16), value_rows, preferred_element_type=jnp.float32
                )
                return (new_max, new_sum, new_weighted)

            final_max, final_sum, weighted = lax.fori_loop(0, tile_count, visit, start_state)
            denominator = final_sum + jnp.exp(sink_logit - final_max)
            return (weighted / denominator[:, None]).astype(jnp.bfloat16)

        return lax.map(query_tile, jnp.arange(tile_count, dtype=jnp.int32)).reshape(total_rows, HD)

    attended = lax.map(one_head, jnp.arange(heads_local, dtype=jnp.int32))
    returned = lax.all_to_all(attended, "seq", split_axis=1, concat_axis=0, tiled=True)
    hidden = returned.transpose(1, 0, 2).reshape(tok_rows, HEADS * HD)
    page_count = total_rows // PAGE + SEGS
    page_index = block_table.reshape(-1)[segment * block_table.shape[1] + position // PAGE]
    cache_row = page_index * PAGE + position % PAGE

    def place(values_in):
        flat_cache = (
            jnp.zeros((page_count * PAGE, heads_local, HD), jnp.bfloat16)
            .at[cache_row]
            .set(values_in)
        )
        return (
            flat_cache.reshape(page_count, PAGE, heads_local, HD)
            .transpose(2, 0, 1, 3)
            .reshape(heads_local, page_count, PAGE * HD)
        )

    kv_cache = jnp.stack([place(arrived[:, 1]), place(arrived[:, 2])], axis=2)
    return (hidden, kv_cache)


LANES = 128
BF16 = jnp.bfloat16
F32 = jnp.float32
ANYWHERE = pl.BlockSpec(memory_space=pl.ANY)
IN_HBM = pl.BlockSpec(memory_space=pltpu.HBM)
IN_VMEM = pl.BlockSpec(memory_space=pltpu.VMEM)
IN_SMEM = pl.BlockSpec(memory_space=pltpu.SMEM)


def sends(group_size):
    return sorted(range(1, group_size), key=lambda bits: (-bits.bit_count(), bits))


def to_partner(values, bits, group_size):
    return lax.ppermute(values, "seq", [(i, i ^ bits) for i in range(group_size)])


def map_partners(partners, parts, group_size):
    sent = [to_partner(part, bits, group_size) for bits, part in zip(partners, parts)]
    return sent + list(parts[len(partners) :])


def params(mebibytes=40):
    return pltpu.CompilerParams(vmem_limit_bytes=mebibytes * 1024 * 1024)


def stay(values):
    return pltpu.with_memory_space_constraint(values, pltpu.HBM)


def cost(flops, moved):
    return pl.CostEstimate(flops=flops, bytes_accessed=moved, transcendentals=0)


def start_columns(shared, outs, sem, width, wanted):
    me = lax.axis_index("seq")
    copies = []
    for n, (bits, kinds, tiles) in enumerate(wanted):
        span = (tiles[1] - tiles[0]) * LANES
        owner = jnp.bitwise_xor(me, bits)
        for m, c in enumerate(kinds):
            first = pl.multiple_of(c * HEADS * HD + owner * width + tiles[0] * LANES, LANES)
            copies.append(
                pltpu.make_async_copy(
                    shared.at[:, pl.ds(first, span)],
                    outs[n].at[:, pl.ds(m * span, span)],
                    sem.at[n, m],
                )
            )
    for copy in copies:
        copy.start()
    return copies


def make_codes(inputs, adapter_down, shared_qkv, after, width, wanted):
    tok_rows, depth = inputs.shape
    code_width = adapter_down.shape[1]
    steps = 8
    chunk = depth // steps
    spans = [len(kinds) * (tiles[1] - tiles[0]) * LANES for _, kinds, tiles in wanted]

    def body(inputs_ref, down_ref, shared, _, *refs):
        outs, (held, down, in_sem, down_sem, sem) = refs[:-5], refs[-5:]
        loads = []
        for step in range(steps):
            at = pl.ds(step * chunk, chunk)
            loads.append(
                (
                    pltpu.make_async_copy(inputs_ref.at[:, at], held.at[:, at], in_sem.at[step]),
                    pltpu.make_async_copy(down_ref.at[at, :], down.at[at, :], down_sem.at[step]),
                )
            )
            for load in loads[-1]:
                load.start()
        copies = start_columns(shared, outs, sem, width, wanted)
        total = None
        for step in range(steps):
            for load in loads[step]:
                load.wait()
            at = slice(step * chunk, (step + 1) * chunk)
            term = jnp.dot(held[:, at], down[at, :], preferred_element_type=F32)
            total = term if total is None else total + term
        own_codes = total.astype(BF16)
        for out, span in zip(outs, spans):
            out[:, span:] = own_codes
        for copy in copies:
            copy.wait()

    return pl.pallas_call(
        body,
        out_shape=[jax.ShapeDtypeStruct((tok_rows, span + code_width), BF16) for span in spans],
        in_specs=[IN_HBM, IN_HBM, IN_HBM, ANYWHERE],
        out_specs=[IN_VMEM] * len(wanted),
        scratch_shapes=[
            pltpu.VMEM((tok_rows, depth), BF16),
            pltpu.VMEM((depth, code_width), BF16),
            pltpu.SemaphoreType.DMA((steps,)),
            pltpu.SemaphoreType.DMA((steps,)),
            pltpu.SemaphoreType.DMA((len(wanted), 3)),
        ],
        compiler_params=params(20),
        cost_estimate=cost(2 * tok_rows * depth * code_width, depth * code_width * 2),
        name="make_codes",
    )(stay(inputs), stay(adapter_down), stay(shared_qkv), after)


def pack_qkv(shared_qkv, after, width, wanted):
    tok_rows = shared_qkv.shape[0]
    spans = [len(kinds) * (tiles[1] - tiles[0]) * LANES for _, kinds, tiles in wanted]

    def body(shared, *refs):
        outs, sem = refs[len(after) : -1], refs[-1]
        for copy in start_columns(shared, outs, sem, width, wanted):
            copy.wait()

    return pl.pallas_call(
        body,
        out_shape=[jax.ShapeDtypeStruct((tok_rows, span), BF16) for span in spans],
        in_specs=[IN_HBM] + [ANYWHERE] * len(after),
        out_specs=[IN_VMEM] * len(wanted),
        scratch_shapes=[pltpu.SemaphoreType.DMA((len(wanted), 3))],
        compiler_params=params(20),
        cost_estimate=cost(0, 2 * tok_rows * sum(spans) * 2),
        name="pack_qkv",
    )(stay(shared_qkv), *after)


def head_tiles(h):
    return (h * HD // LANES, -(-(h + 1) * HD // LANES))


def side_by_side(ref, window, rows):
    return jnp.concatenate([ref[tile, rows, :] for tile in window], axis=1)


def attend(up, sink_logits, lengths, low_rank, arrived, places, carried, heads, tiles, done_tiles):
    group_size = len(places)
    tok_rows = arrived[0].shape[0]
    total_rows = tok_rows * group_size
    window_span = total_rows // 2
    scale_factor = HD ** (-0.5)
    span = (tiles[1] - tiles[0]) * LANES
    done_span = (done_tiles[1] - done_tiles[0]) * LANES
    low_tile = min(tiles[0], done_tiles[0])
    kept = (tiles[0] - low_tile) * LANES
    left = (tiles[1] - done_tiles[1]) * LANES
    first_call, last = low_rank is None, left == 0
    all_tiles = (kept + span) // LANES
    given_low = [] if first_call else [low_rank]
    rest = up.shape[2] - tiles[1] * LANES

    def body(*refs):
        refs = list(refs)
        take = lambda n: [refs.pop(0) for _ in range(n)]
        up_ref, sinks, lens = take(3)
        low_refs = take(len(given_low))
        arrived_refs = take(len(arrived))
        before = take(len(carried))
        outs = take(group_size)
        keys, values = take(2)
        carried_out = take(0 if last else 3)
        queries, merged = take(2)
        me = lax.axis_index("seq")
        kept_tiles = kept // LANES
        if kept:
            for target, source in zip((queries, merged, keys, values), before):
                target[:kept_tiles] = source[source.shape[0] - kept_tiles :]
        for bits in range(group_size):
            place = pl.ds(pl.multiple_of(jnp.bitwise_xor(me, bits) * tok_rows, tok_rows), tok_rows)
            for c, target in enumerate((queries, keys, values)):
                if first_call:
                    which, at = places[bits][3]
                    codes = arrived_refs[which][:, at + c * RANK : at + (c + 1) * RANK]
                    low = jnp.dot(codes, up_ref[c, :, :span], preferred_element_type=F32)
                    carried_out[0][bits, :, c * rest : (c + 1) * rest] = jnp.dot(
                        codes, up_ref[c, :, span:], preferred_element_type=F32
                    )
                else:
                    low = low_refs[0][bits, :, c * span : (c + 1) * span]
                which, at = places[bits][c]
                base = arrived_refs[which][:, at : at + span].astype(F32)
                new = (base + low).astype(BF16)
                for n in range(tiles[1] - tiles[0]):
                    target[kept_tiles + n, place, :] = new[:, n * LANES : (n + 1) * LANES]

        ends = []
        for s in range(SEGS):
            ends.append(lens[s] + (ends[-1] if ends else 0))
        blocks = []
        for b in range(group_size):
            first_query = b * tok_rows
            rows = slice(first_query, first_query + tok_rows)
            first_key = max(0, (first_query - window_span + 1) // tok_rows * tok_rows)
            key_rows = slice(first_key, first_query + tok_rows)
            query_place = first_query + lax.broadcasted_iota(jnp.int32, (tok_rows, 1), 0)
            earliest = query_place - (window_span - 1)
            for s in range(SEGS):
                earliest = jnp.where(ends[s] <= query_place, jnp.maximum(earliest, ends[s]), earliest)
            key_place = first_key + lax.broadcasted_iota(jnp.int32, (tok_rows, key_rows.stop - first_key), 1)
            visible = (key_place >= earliest) & (key_place <= query_place)
            scores = {}
            for h in heads:
                first_tile, end_tile = head_tiles(h)
                window = range(first_tile - low_tile, end_tile - low_tile)
                column = first_tile * LANES + lax.broadcasted_iota(jnp.int32, (1, len(window) * LANES), 1)
                mine = (column >= h * HD) & (column < (h + 1) * HD)
                query = side_by_side(queries, window, rows)
                query = jnp.where(mine, query, jnp.zeros_like(query))
                scores[h] = lax.dot_general(
                    query,
                    side_by_side(keys, window, key_rows),
                    (((1,), (1,)), ((), ())),
                    preferred_element_type=F32,
                )
            blocks.append((rows, key_rows, visible, scores))
        for rows, key_rows, visible, scores in blocks:
            parts = {}
            for tile in range(low_tile, tiles[0]):
                parts[tile] = merged[tile - low_tile, rows, :].astype(F32)
            for h in heads:
                first_tile, end_tile = head_tiles(h)
                window = range(first_tile - low_tile, end_tile - low_tile)
                seen = jnp.where(visible, scores[h] * scale_factor, -jnp.inf)
                top = jnp.maximum(jnp.max(seen, axis=1, keepdims=True), sinks[h])
                weights = jnp.exp(seen - top)
                denominator = jnp.sum(weights, axis=1, keepdims=True) + jnp.exp(sinks[h] - top)
                mixed = jnp.dot(
                    weights.astype(BF16),
                    side_by_side(values, window, key_rows),
                    preferred_element_type=F32,
                ) / denominator
                for tile in range(first_tile, end_tile):
                    at = (tile - first_tile) * LANES
                    piece = mixed[:, at : at + LANES]
                    if tile in parts:
                        lane = tile * LANES + lax.broadcasted_iota(jnp.int32, (1, LANES), 1)
                        piece = jnp.where(lane < h * HD, parts[tile], piece)
                    parts[tile] = piece
            for tile, piece in parts.items():
                merged[tile - low_tile, rows, :] = piece.astype(BF16)
        for bits in range(group_size):
            place = pl.ds(pl.multiple_of(jnp.bitwise_xor(me, bits) * tok_rows, tok_rows), tok_rows)
            outs[bits][...] = side_by_side(merged, range(done_tiles[1] - done_tiles[0]), place)
        if not last:
            carried_out[1][...] = queries[all_tiles - left // LANES :]
            carried_out[2][...] = merged[all_tiles - left // LANES :]

    block = jax.ShapeDtypeStruct((tok_rows, done_span), BF16)
    stream = jax.ShapeDtypeStruct((all_tiles, total_rows, LANES), BF16)
    leftover = jax.ShapeDtypeStruct((left // LANES, total_rows, LANES), BF16)
    next_low = jax.ShapeDtypeStruct((group_size, tok_rows, 3 * rest), F32)
    out_shape = [block] * group_size + [stream] * 2 + ([] if last else [next_low, leftover, leftover])
    results = pl.pallas_call(
        body,
        out_shape=out_shape,
        in_specs=[IN_VMEM, IN_SMEM, IN_SMEM]
        + [IN_VMEM] * (len(given_low) + len(arrived) + len(carried)),
        out_specs=[IN_VMEM] * len(out_shape),
        scratch_shapes=[pltpu.VMEM((all_tiles, total_rows, LANES), BF16)] * 2,
        compiler_params=params(),
        cost_estimate=cost(4 * total_rows * total_rows * span, 8 * total_rows * span * 2),
        name="attend",
    )(up, sink_logits, lengths, *given_low, *arrived, *carried)
    blocks, (keys, values) = results[:group_size], results[group_size : group_size + 2]
    if last:
        return blocks, keys, values, None, []
    next_low, *leftovers = results[group_size + 2 :]
    return blocks, keys, values, next_low, [*leftovers, keys, values]


def build_cache(keys, values, starts, lengths, block_table):
    total_rows = keys[0].shape[1]
    parts = len(keys)
    width = sum(part.shape[0] - start for part, start in zip(keys, starts)) * LANES
    heads_local = width // HD
    page_count = total_rows // PAGE + SEGS
    blocks = block_table.shape[1]
    rows = 2 * page_count
    group = 4

    def body(*refs):
        key_refs, value_refs = refs[:parts], refs[parts : 2 * parts]
        lens, table, out, built, sem = refs[2 * parts :]
        row = lax.broadcasted_iota(jnp.int32, (rows, blocks), 0)
        page = lax.shift_right_logical(row, 1)
        block = lax.broadcasted_iota(jnp.int32, (rows, blocks), 1)
        first = jnp.zeros((rows, blocks), jnp.int32)
        count = jnp.zeros((rows, blocks), jnp.int32)
        start = 0
        for s in range(SEGS):
            left = lens[s] - block * PAGE
            held = (table[s : s + 1, :] == page) & (left > 0)
            first = jnp.where(held, start + block * PAGE, first)
            count = jnp.where(held, jnp.minimum(left, PAGE), count)
            start = start + lens[s]
        first = jnp.sum(first, axis=1, keepdims=True)
        count = jnp.sum(count, axis=1, keepdims=True)
        odd = jnp.bitwise_and(lax.broadcasted_iota(jnp.int32, (rows, 1), 0), 1)
        place = lax.broadcasted_iota(jnp.int32, (group * rows, total_rows), 1)

        def columns(part_refs):
            every = [(ref, tile) for ref, low in zip(part_refs, starts) for tile in range(low, ref.shape[0])]
            return jnp.concatenate([ref[tile] for ref, tile in every], axis=1)

        all_keys, all_values = columns(key_refs), columns(value_refs)
        copies = []
        for r in range(0, PAGE, group):
            wanted = [jnp.where(count > r + n, first + r + n, -1) for n in range(group)]
            for_keys = jnp.concatenate([jnp.where(odd == 0, want, -1) for want in wanted], axis=0)
            for_values = jnp.concatenate([jnp.where(odd == 1, want, -1) for want in wanted], axis=0)
            pick_keys = (place == for_keys).astype(F32).astype(BF16)
            pick_values = (place == for_values).astype(F32).astype(BF16)
            picked = jnp.dot(pick_keys, all_keys, preferred_element_type=F32) + jnp.dot(
                pick_values, all_values, preferred_element_type=F32
            )
            lanes = slice(r * HD, (r + group) * HD)
            for h in range(heads_local):
                line = jnp.concatenate(
                    [picked[m * rows : (m + 1) * rows, h * HD : (h + 1) * HD] for m in range(group)], axis=1
                )
                built[h, :, :, lanes] = line.astype(BF16).reshape(page_count, 2, group * HD)
                copies.append(
                    pltpu.make_async_copy(
                        built.at[h, :, :, lanes], out.at[h, :, :, lanes], sem.at[h, r // group]
                    )
                )
                copies[-1].start()
        for copy in copies:
            copy.wait()

    cache = (heads_local, page_count, 2, PAGE * HD)
    return pl.pallas_call(
        body,
        out_shape=jax.ShapeDtypeStruct(cache, BF16),
        in_specs=[IN_VMEM] * (2 * parts) + [IN_SMEM, IN_VMEM],
        out_specs=IN_HBM,
        scratch_shapes=[pltpu.VMEM(cache, BF16), pltpu.SemaphoreType.DMA((heads_local, PAGE // group))],
        compiler_params=params(),
        cost_estimate=cost(4 * rows * PAGE * total_rows * width, 4 * total_rows * width * 2),
        name="build_cache",
    )(*keys, *values, lengths, block_table)


def join_heads(parts, group_size):
    tok_rows = parts[0][0].shape[0]
    width = sum(blocks[0].shape[1] for blocks in parts)
    sources = [block for blocks in parts for block in blocks]

    def body(*refs):
        out, sem = refs[-2:]
        me = lax.axis_index("seq")
        copies = []
        begin = 0
        for n, blocks in enumerate(parts):
            span = blocks[0].shape[1]
            for bits in range(group_size):
                first = pl.multiple_of(jnp.bitwise_xor(me, bits) * width + begin, LANES)
                copies.append(
                    pltpu.make_async_copy(
                        refs[n * group_size + bits], out.at[:, pl.ds(first, span)], sem.at[n, bits]
                    )
                )
            begin += span
        for copy in copies:
            copy.start()
        for copy in copies:
            copy.wait()

    return pl.pallas_call(
        body,
        out_shape=jax.ShapeDtypeStruct((tok_rows, width * group_size), BF16),
        in_specs=[ANYWHERE] * len(sources),
        out_specs=IN_HBM,
        scratch_shapes=[pltpu.SemaphoreType.DMA((len(parts), group_size))],
        compiler_params=params(),
        cost_estimate=cost(0, 2 * tok_rows * width * group_size * 2),
        name="join_heads",
    )(*sources)


def per_device_tiled(inputs, adapter_down, adapter_up, shared_qkv, sink_logits, lengths, block_table):
    group_size = lax.axis_size("seq")
    partners = sends(group_size)
    width = adapter_up.shape[2]
    heads_local = width // HD
    half = heads_local // 2
    all_tiles = width // LANES
    cut = -(-half * HD // LANES)
    done_cut = half * HD // LANES
    tiles = [(0, cut), (cut, all_tiles)]
    done_tiles = [(0, done_cut), (done_cut, all_tiles)]
    heads = [tuple(range(half)), tuple(range(half, heads_local))]

    every = (0, 1, 2)
    first, others = partners[0], partners[1:]
    whole = (0, all_tiles)
    (early,) = pack_qkv(shared_qkv, [], width, [(first, (0, 1), whole)])
    wanted = [(bits, every, tiles[0]) for bits in others + [0]]
    parts = make_codes(inputs, adapter_down, shared_qkv, early, width, [(first, (2,), whole)] + wanted)
    early = to_partner(early, first, group_size)
    parts = map_partners(partners, parts, group_size)
    arrived = [[early, *parts]]
    wanted = [(bits, every, tiles[1]) for bits in others + [0]]
    later = pack_qkv(shared_qkv, [parts[-1], early], width, wanted)
    arrived.append([early, parts[0], *map_partners(others, later, group_size)])
    places = []
    for n in range(2):
        span = (tiles[n][1] - tiles[n][0]) * LANES
        at = {bits: [(m + 2, c * span) for c in range(4)] for m, bits in enumerate(others + [0])}
        begin = tiles[n][0] * LANES
        at[first] = [(0, begin), (0, width + begin), (1, begin), (1, width)]
        places.append([at[bits] for bits in range(group_size)])
    low_rank, carried, hidden, keys, values = None, [], [], [], []
    for n in range(2):
        blocks, new_keys, new_values, low_rank, carried = attend(
            adapter_up,
            sink_logits,
            lengths,
            low_rank,
            arrived[n],
            places[n],
            carried,
            heads[n],
            tiles[n],
            done_tiles[n],
        )
        returned = {bits: to_partner(blocks[bits], bits, group_size) for bits in partners}
        hidden.append([blocks[0]] + [returned[bits] for bits in range(1, group_size)])
        keys, values = keys + [new_keys], values + [new_values]
    starts = [0, cut - done_cut]
    cache = build_cache(keys, values, starts, lengths, block_table)
    return (join_heads(hidden, group_size), cache)


def per_device(inputs, adapter_down, adapter_up, shared_qkv, sink_logits, lengths, block_table):
    group_size = lax.axis_size("seq")
    width = adapter_up.shape[2]
    tiled = (
        group_size & (group_size - 1) == 0
        and width % (2 * HD) == 0
        and width % LANES == 0
        and inputs.shape[0] % LANES == 0
        and inputs.shape[0] * group_size <= 512
    )
    chosen = per_device_tiled if tiled else per_device_general
    return chosen(inputs, adapter_down, adapter_up, shared_qkv, sink_logits, lengths, block_table)


def solution(mesh):
    return jax.shard_map(
        per_device,
        mesh=mesh,
        in_specs=(
            P(("batch", "seq"), None),
            P(),
            P(None, None, "seq"),
            P(("batch", "seq"), None),
            P("seq"),
            P("batch"),
            P("batch", None),
        ),
        out_specs=(P(("batch", "seq"), None), P("seq", "batch", None, None)),
        check_vma=False,
    )
```

```python
import jax
import jax.numpy as jnp
from jax import lax
from jax.experimental import pallas as pl
from jax.experimental.pallas import tpu as pltpu
from jax.sharding import PartitionSpec as P

HD = 224
RANK = 128
HEADS = 16
SEGS = 8
PAGE = 16


def segment_positions(lengths, total_rows):
    segment_ends = jnp.cumsum(lengths)
    segment_starts = segment_ends - lengths
    places = jnp.arange(total_rows, dtype=jnp.int32)
    segment = jnp.sum((places[:, None] >= segment_ends[None, :]).astype(jnp.int32), axis=1)
    member = segment[:, None] == jnp.arange(SEGS, dtype=jnp.int32)[None, :]
    offsets = jnp.sum(jnp.where(member, segment_starts[None, :], 0), axis=1)
    return (segment, places - offsets)


def per_device_general(inputs, adapter_down, adapter_up, shared_qkv, sink_logits, lengths, block_table):
    group_size = lax.axis_size("seq")
    tok_rows = inputs.shape[0]
    total_rows = tok_rows * group_size
    heads_local = adapter_up.shape[2] // HD
    window_span = total_rows // 2
    low_codes = jnp.dot(inputs, adapter_down, preferred_element_type=jnp.float32).astype(
        jnp.bfloat16
    )
    shared_base = shared_qkv.reshape(tok_rows, 3, HEADS * HD)
    low_rank = jnp.einsum(
        "tcr,crf->tcf",
        low_codes.reshape(tok_rows, 3, RANK),
        lax.all_gather(adapter_up, "seq", axis=2, tiled=True),
        preferred_element_type=jnp.float32,
    )
    merged = (shared_base.astype(jnp.float32) + low_rank).astype(jnp.bfloat16)
    sending = merged.reshape(tok_rows, 3, HEADS, HD)
    arrived = lax.all_to_all(sending, "seq", split_axis=2, concat_axis=0, tiled=True)
    segment, position = segment_positions(lengths, total_rows)
    tile_rows = min(512, total_rows)
    tile_count = total_rows // tile_rows
    scale_factor = HD ** (-0.5)

    def one_head(head_index):
        query_all = arrived[:, 0, head_index]
        key_all = arrived[:, 1, head_index]
        value_all = arrived[:, 2, head_index]
        sink_logit = sink_logits[head_index]

        def query_tile(tile_index):
            query_first = tile_index * tile_rows
            query_rows = lax.dynamic_slice_in_dim(query_all, query_first, tile_rows, 0)
            query_segs = lax.dynamic_slice_in_dim(segment, query_first, tile_rows, 0)
            query_place = query_first + jnp.arange(tile_rows, dtype=jnp.int32)
            start_state = (
                jnp.full((tile_rows,), sink_logit, jnp.float32),
                jnp.zeros((tile_rows,), jnp.float32),
                jnp.zeros((tile_rows, HD), jnp.float32),
            )

            def visit(key_tile, state):
                key_first = key_tile * tile_rows
                running_max, running_sum, weighted = state
                key_rows = lax.dynamic_slice_in_dim(key_all, key_first, tile_rows, 0)
                value_rows = lax.dynamic_slice_in_dim(value_all, key_first, tile_rows, 0)
                key_segs = lax.dynamic_slice_in_dim(segment, key_first, tile_rows, 0)
                key_place = key_first + jnp.arange(tile_rows, dtype=jnp.int32)
                scores = (
                    jnp.dot(query_rows, key_rows.T, preferred_element_type=jnp.float32)
                    * scale_factor
                )
                visible = (
                    (query_segs[:, None] == key_segs[None, :])
                    & (key_place[None, :] <= query_place[:, None])
                    & (query_place[:, None] - key_place[None, :] < window_span)
                )
                scores = jnp.where(visible, scores, -jnp.inf)
                new_max = jnp.maximum(running_max, jnp.max(scores, axis=1))
                rescale = jnp.exp(running_max - new_max)
                weights = jnp.exp(scores - new_max[:, None])
                new_sum = running_sum * rescale + jnp.sum(weights, axis=1)
                new_weighted = weighted * rescale[:, None] + jnp.dot(
                    weights.astype(jnp.bfloat16), value_rows, preferred_element_type=jnp.float32
                )
                return (new_max, new_sum, new_weighted)

            final_max, final_sum, weighted = lax.fori_loop(0, tile_count, visit, start_state)
            denominator = final_sum + jnp.exp(sink_logit - final_max)
            return (weighted / denominator[:, None]).astype(jnp.bfloat16)

        return lax.map(query_tile, jnp.arange(tile_count, dtype=jnp.int32)).reshape(total_rows, HD)

    attended = lax.map(one_head, jnp.arange(heads_local, dtype=jnp.int32))
    returned = lax.all_to_all(attended, "seq", split_axis=1, concat_axis=0, tiled=True)
    hidden = returned.transpose(1, 0, 2).reshape(tok_rows, HEADS * HD)
    page_count = total_rows // PAGE + SEGS
    page_index = block_table.reshape(-1)[segment * block_table.shape[1] + position // PAGE]
    cache_row = page_index * PAGE + position % PAGE

    def place(values_in):
        flat_cache = (
            jnp.zeros((page_count * PAGE, heads_local, HD), jnp.bfloat16)
            .at[cache_row]
            .set(values_in)
        )
        return (
            flat_cache.reshape(page_count, PAGE, heads_local, HD)
            .transpose(2, 0, 1, 3)
            .reshape(heads_local, page_count, PAGE * HD)
        )

    kv_cache = jnp.stack([place(arrived[:, 1]), place(arrived[:, 2])], axis=2)
    return (hidden, kv_cache)


LANES = 128
SLABS = 1
BF16 = jnp.bfloat16
F32 = jnp.float32
ANYWHERE = pl.BlockSpec(memory_space=pl.ANY)
IN_HBM = pl.BlockSpec(memory_space=pltpu.HBM)
IN_VMEM = pl.BlockSpec(memory_space=pltpu.VMEM)
IN_SMEM = pl.BlockSpec(memory_space=pltpu.SMEM)


def sends(group_size):
    return sorted(range(1, group_size), key=lambda bits: (-bits.bit_count(), bits))


def to_partner(values, bits, group_size):
    return lax.ppermute(values, "seq", [(i, i ^ bits) for i in range(group_size)])


def map_partners(partners, parts, group_size):
    sent = [to_partner(part, bits, group_size) for bits, part in zip(partners, parts)]
    return sent + list(parts[len(partners) :])


def params(mebibytes=40):
    return pltpu.CompilerParams(vmem_limit_bytes=mebibytes * 1024 * 1024)


def stay(values):
    return pltpu.with_memory_space_constraint(values, pltpu.HBM)


def cost(flops, moved):
    return pl.CostEstimate(flops=flops, bytes_accessed=moved, transcendentals=0)


def start_columns(shared, outs, sem, width, wanted):
    me = lax.axis_index("seq")
    slab = shared.shape[0] // SLABS
    copies = []
    for n, (bits, kinds, tiles) in enumerate(wanted):
        span = (tiles[1] - tiles[0]) * LANES
        owner = jnp.bitwise_xor(me, bits)
        for m, c in enumerate(kinds):
            first = pl.multiple_of(c * HEADS * HD + owner * width + tiles[0] * LANES, LANES)
            for k in range(SLABS):
                rows = pl.ds(k * slab, slab)
                copies.append(
                    pltpu.make_async_copy(
                        shared.at[rows, pl.ds(first, span)],
                        outs[n].at[rows, pl.ds(m * span, span)],
                        sem.at[n, m, k],
                    )
                )
    for copy in copies:
        copy.start()
    return copies


def make_codes(inputs, adapter_down, shared_qkv, after, width, wanted):
    tok_rows, depth = inputs.shape
    code_width = adapter_down.shape[1]
    steps = 8
    chunk = depth // steps
    spans = [len(kinds) * (tiles[1] - tiles[0]) * LANES for _, kinds, tiles in wanted]

    def body(inputs_ref, down_ref, shared, _, *refs):
        outs, (held, down, in_sem, down_sem, sem) = refs[:-5], refs[-5:]
        loads = []
        for step in range(steps):
            at = pl.ds(step * chunk, chunk)
            loads.append(
                (
                    pltpu.make_async_copy(inputs_ref.at[:, at], held.at[:, at], in_sem.at[step]),
                    pltpu.make_async_copy(down_ref.at[at, :], down.at[at, :], down_sem.at[step]),
                )
            )
            for load in loads[-1]:
                load.start()
        copies = start_columns(shared, outs, sem, width, wanted)
        total = None
        for step in range(steps):
            for load in loads[step]:
                load.wait()
            at = slice(step * chunk, (step + 1) * chunk)
            term = jnp.dot(held[:, at], down[at, :], preferred_element_type=F32)
            total = term if total is None else total + term
        own_codes = total.astype(BF16)
        for out, span in zip(outs, spans):
            out[:, span:] = own_codes
        for copy in copies:
            copy.wait()

    return pl.pallas_call(
        body,
        out_shape=[jax.ShapeDtypeStruct((tok_rows, span + code_width), BF16) for span in spans],
        in_specs=[IN_HBM, IN_HBM, IN_HBM, ANYWHERE],
        out_specs=[IN_VMEM] * len(wanted),
        scratch_shapes=[
            pltpu.VMEM((tok_rows, depth), BF16),
            pltpu.VMEM((depth, code_width), BF16),
            pltpu.SemaphoreType.DMA((steps,)),
            pltpu.SemaphoreType.DMA((steps,)),
            pltpu.SemaphoreType.DMA((len(wanted), 3, SLABS)),
        ],
        compiler_params=params(20),
        cost_estimate=cost(2 * tok_rows * depth * code_width, depth * code_width * 2),
        name="make_codes",
    )(stay(inputs), stay(adapter_down), stay(shared_qkv), after)


def pack_qkv(shared_qkv, after, width, wanted):
    tok_rows = shared_qkv.shape[0]
    spans = [len(kinds) * (tiles[1] - tiles[0]) * LANES for _, kinds, tiles in wanted]

    def body(shared, *refs):
        outs, sem = refs[len(after) : -1], refs[-1]
        for copy in start_columns(shared, outs, sem, width, wanted):
            copy.wait()

    return pl.pallas_call(
        body,
        out_shape=[jax.ShapeDtypeStruct((tok_rows, span), BF16) for span in spans],
        in_specs=[IN_HBM] + [ANYWHERE] * len(after),
        out_specs=[IN_VMEM] * len(wanted),
        scratch_shapes=[pltpu.SemaphoreType.DMA((len(wanted), 3, SLABS))],
        compiler_params=params(20),
        cost_estimate=cost(0, 2 * tok_rows * sum(spans) * 2),
        name="pack_qkv",
    )(stay(shared_qkv), *after)


def head_tiles(h):
    return (h * HD // LANES, -(-(h + 1) * HD // LANES))


def side_by_side(ref, window, rows):
    return jnp.concatenate([ref[tile, rows, :] for tile in window], axis=1)


def attend(up, sink_logits, lengths, low_rank, arrived, places, carried, heads, tiles, done_tiles):
    group_size = len(places)
    tok_rows = arrived[0].shape[0]
    total_rows = tok_rows * group_size
    window_span = total_rows // 2
    scale_factor = HD ** (-0.5)
    span = (tiles[1] - tiles[0]) * LANES
    done_span = (done_tiles[1] - done_tiles[0]) * LANES
    low_tile = min(tiles[0], done_tiles[0])
    kept = (tiles[0] - low_tile) * LANES
    left = (tiles[1] - done_tiles[1]) * LANES
    first_call, last = low_rank is None, left == 0
    all_tiles = (kept + span) // LANES
    given_low = [] if first_call else [low_rank]
    rest = up.shape[2] - tiles[1] * LANES

    def body(*refs):
        refs = list(refs)
        take = lambda n: [refs.pop(0) for _ in range(n)]
        up_ref, sinks, lens = take(3)
        low_refs = take(len(given_low))
        arrived_refs = take(len(arrived))
        before = take(len(carried))
        outs = take(group_size)
        keys, values = take(2)
        carried_out = take(0 if last else 3)
        queries, merged = take(2)
        me = lax.axis_index("seq")
        kept_tiles = kept // LANES
        if kept:
            for target, source in zip((queries, merged, keys, values), before):
                target[:kept_tiles] = source[source.shape[0] - kept_tiles :]
        for bits in range(group_size):
            place = pl.ds(pl.multiple_of(jnp.bitwise_xor(me, bits) * tok_rows, tok_rows), tok_rows)
            for c, target in enumerate((queries, keys, values)):
                if first_call:
                    which, at = places[bits][3]
                    codes = arrived_refs[which][:, at + c * RANK : at + (c + 1) * RANK]
                    low = jnp.dot(codes, up_ref[c, :, :span], preferred_element_type=F32)
                    carried_out[0][bits, :, c * rest : (c + 1) * rest] = jnp.dot(
                        codes, up_ref[c, :, span:], preferred_element_type=F32
                    )
                else:
                    low = low_refs[0][bits, :, c * span : (c + 1) * span]
                which, at = places[bits][c]
                base = arrived_refs[which][:, at : at + span].astype(F32)
                new = (base + low).astype(BF16)
                for n in range(tiles[1] - tiles[0]):
                    target[kept_tiles + n, place, :] = new[:, n * LANES : (n + 1) * LANES]

        ends = []
        for s in range(SEGS):
            ends.append(lens[s] + (ends[-1] if ends else 0))
        blocks = []
        for b in range(group_size):
            first_query = b * tok_rows
            rows = slice(first_query, first_query + tok_rows)
            first_key = max(0, (first_query - window_span + 1) // tok_rows * tok_rows)
            key_rows = slice(first_key, first_query + tok_rows)
            query_place = first_query + lax.broadcasted_iota(jnp.int32, (tok_rows, 1), 0)
            earliest = query_place - (window_span - 1)
            for s in range(SEGS):
                earliest = jnp.where(ends[s] <= query_place, jnp.maximum(earliest, ends[s]), earliest)
            key_place = first_key + lax.broadcasted_iota(jnp.int32, (tok_rows, key_rows.stop - first_key), 1)
            visible = (key_place >= earliest) & (key_place <= query_place)
            scores = {}
            for h in heads:
                first_tile, end_tile = head_tiles(h)
                window = range(first_tile - low_tile, end_tile - low_tile)
                column = first_tile * LANES + lax.broadcasted_iota(jnp.int32, (1, len(window) * LANES), 1)
                mine = (column >= h * HD) & (column < (h + 1) * HD)
                query = side_by_side(queries, window, rows)
                query = jnp.where(mine, query, jnp.zeros_like(query))
                scores[h] = lax.dot_general(
                    query,
                    side_by_side(keys, window, key_rows),
                    (((1,), (1,)), ((), ())),
                    preferred_element_type=F32,
                )
            blocks.append((rows, key_rows, visible, scores))
        for rows, key_rows, visible, scores in blocks:
            parts = {}
            for tile in range(low_tile, tiles[0]):
                parts[tile] = merged[tile - low_tile, rows, :].astype(F32)
            for h in heads:
                first_tile, end_tile = head_tiles(h)
                window = range(first_tile - low_tile, end_tile - low_tile)
                seen = jnp.where(visible, scores[h] * scale_factor, -jnp.inf)
                top = jnp.maximum(jnp.max(seen, axis=1, keepdims=True), sinks[h])
                weights = jnp.exp(seen - top)
                denominator = jnp.sum(weights, axis=1, keepdims=True) + jnp.exp(sinks[h] - top)
                mixed = jnp.dot(
                    weights.astype(BF16),
                    side_by_side(values, window, key_rows),
                    preferred_element_type=F32,
                ) / denominator
                for tile in range(first_tile, end_tile):
                    at = (tile - first_tile) * LANES
                    piece = mixed[:, at : at + LANES]
                    if tile in parts:
                        lane = tile * LANES + lax.broadcasted_iota(jnp.int32, (1, LANES), 1)
                        piece = jnp.where(lane < h * HD, parts[tile], piece)
                    parts[tile] = piece
            for tile, piece in parts.items():
                merged[tile - low_tile, rows, :] = piece.astype(BF16)
        for bits in range(group_size):
            place = pl.ds(pl.multiple_of(jnp.bitwise_xor(me, bits) * tok_rows, tok_rows), tok_rows)
            outs[bits][...] = side_by_side(merged, range(done_tiles[1] - done_tiles[0]), place)
        if not last:
            carried_out[1][...] = queries[all_tiles - left // LANES :]
            carried_out[2][...] = merged[all_tiles - left // LANES :]

    block = jax.ShapeDtypeStruct((tok_rows, done_span), BF16)
    stream = jax.ShapeDtypeStruct((all_tiles, total_rows, LANES), BF16)
    leftover = jax.ShapeDtypeStruct((left // LANES, total_rows, LANES), BF16)
    next_low = jax.ShapeDtypeStruct((group_size, tok_rows, 3 * rest), F32)
    out_shape = [block] * group_size + [stream] * 2 + ([] if last else [next_low, leftover, leftover])
    results = pl.pallas_call(
        body,
        out_shape=out_shape,
        in_specs=[IN_VMEM, IN_SMEM, IN_SMEM]
        + [IN_VMEM] * (len(given_low) + len(arrived) + len(carried)),
        out_specs=[IN_VMEM] * len(out_shape),
        scratch_shapes=[pltpu.VMEM((all_tiles, total_rows, LANES), BF16)] * 2,
        compiler_params=params(),
        cost_estimate=cost(4 * total_rows * total_rows * span, 8 * total_rows * span * 2),
        name="attend",
    )(up, sink_logits, lengths, *given_low, *arrived, *carried)
    blocks, (keys, values) = results[:group_size], results[group_size : group_size + 2]
    if last:
        return blocks, keys, values, None, []
    next_low, *leftovers = results[group_size + 2 :]
    return blocks, keys, values, next_low, [*leftovers, keys, values]


def build_cache(keys, values, starts, lengths, block_table):
    total_rows = keys[0].shape[1]
    parts = len(keys)
    width = sum(part.shape[0] - start for part, start in zip(keys, starts)) * LANES
    heads_local = width // HD
    page_count = total_rows // PAGE + SEGS
    blocks = block_table.shape[1]
    group = 4

    def body(*refs):
        key_refs, value_refs = refs[:parts], refs[parts : 2 * parts]
        lens, table, out, built, sem = refs[2 * parts :]
        page = lax.broadcasted_iota(jnp.int32, (page_count, blocks), 0)
        block = lax.broadcasted_iota(jnp.int32, (page_count, blocks), 1)
        first = jnp.zeros((page_count, blocks), jnp.int32)
        count = jnp.zeros((page_count, blocks), jnp.int32)
        start = 0
        for s in range(SEGS):
            left = lens[s] - block * PAGE
            held = (table[s : s + 1, :] == page) & (left > 0)
            first = jnp.where(held, start + block * PAGE, first)
            count = jnp.where(held, jnp.minimum(left, PAGE), count)
            start = start + lens[s]
        first = jnp.sum(first, axis=1, keepdims=True)
        count = jnp.sum(count, axis=1, keepdims=True)
        place = lax.broadcasted_iota(jnp.int32, (group * page_count, total_rows), 1)

        def gathered(part_refs):
            every = [(ref, tile) for ref, low in zip(part_refs, starts) for tile in range(low, ref.shape[0])]
            return jnp.concatenate([ref[tile] for ref, tile in every], axis=1)

        all_keys, all_values = gathered(key_refs), gathered(value_refs)
        copies = []
        for r in range(0, PAGE, group):
            wanted = [jnp.where(count > r + n, first + r + n, -1) for n in range(group)]
            pick = (place == jnp.concatenate(wanted, axis=0)).astype(F32).astype(BF16)
            picked = [jnp.dot(pick, every, preferred_element_type=F32) for every in (all_keys, all_values)]
            lanes = slice(r * HD, (r + group) * HD)
            for h in range(heads_local):
                columns = slice(h * HD, (h + 1) * HD)
                for c in range(2):
                    line = jnp.concatenate(
                        [picked[c][m * page_count : (m + 1) * page_count, columns] for m in range(group)], axis=1
                    )
                    built[h, :, c, lanes] = line.astype(BF16)
                copies.append(
                    pltpu.make_async_copy(
                        built.at[h, :, :, lanes], out.at[h, :, :, lanes], sem.at[h, r // group]
                    )
                )
                copies[-1].start()
        for copy in copies:
            copy.wait()

    cache = (heads_local, page_count, 2, PAGE * HD)
    return pl.pallas_call(
        body,
        out_shape=jax.ShapeDtypeStruct(cache, BF16),
        in_specs=[IN_VMEM] * (2 * parts) + [IN_SMEM, IN_VMEM],
        out_specs=IN_HBM,
        scratch_shapes=[pltpu.VMEM(cache, BF16), pltpu.SemaphoreType.DMA((heads_local, PAGE // group))],
        compiler_params=params(),
        cost_estimate=cost(4 * page_count * PAGE * total_rows * width, 4 * total_rows * width * 2),
        name="build_cache",
    )(*keys, *values, lengths, block_table)


def join_heads(hidden, parts, width, group_size):
    tok_rows = parts[0][0].shape[0]
    slab = tok_rows // SLABS
    given = [] if hidden is None else [hidden]

    def body(*refs):
        out, sem = refs[-2:]
        me = lax.axis_index("seq")
        copies = []
        for n, (part, bits, begin) in enumerate(parts):
            first = pl.multiple_of(jnp.bitwise_xor(me, bits) * width + begin, LANES)
            for k in range(SLABS):
                rows = pl.ds(k * slab, slab)
                copies.append(
                    pltpu.make_async_copy(
                        refs[n].at[rows, :], out.at[rows, pl.ds(first, part.shape[1])], sem.at[n, k]
                    )
                )
        for copy in copies:
            copy.start()
        for copy in copies:
            copy.wait()

    return pl.pallas_call(
        body,
        out_shape=jax.ShapeDtypeStruct((tok_rows, width * group_size), BF16),
        in_specs=[ANYWHERE] * len(parts) + [IN_HBM] * len(given),
        out_specs=IN_HBM,
        scratch_shapes=[pltpu.SemaphoreType.DMA((len(parts), SLABS))],
        input_output_aliases={len(parts): 0} if given else {},
        compiler_params=params(),
        cost_estimate=cost(0, 4 * tok_rows * sum(part.shape[1] for part, _, _ in parts)),
        name="join_heads",
    )(*[part for part, _, _ in parts], *map(stay, given))


def per_device_tiled(inputs, adapter_down, adapter_up, shared_qkv, sink_logits, lengths, block_table):
    group_size = lax.axis_size("seq")
    partners = sends(group_size)
    width = adapter_up.shape[2]
    heads_local = width // HD
    half = heads_local // 2
    all_tiles = width // LANES
    cut = -(-half * HD // LANES)
    done_cut = half * HD // LANES
    tiles = [(0, cut), (cut, all_tiles)]
    done_tiles = [(0, done_cut), (done_cut, all_tiles)]
    heads = [tuple(range(half)), tuple(range(half, heads_local))]

    every = (0, 1, 2)
    first, others = partners[0], partners[1:]
    whole = (0, all_tiles)
    (early,) = pack_qkv(shared_qkv, [], width, [(first, (0, 1), whole)])
    wanted = [(bits, every, tiles[0]) for bits in others + [0]]
    parts = make_codes(inputs, adapter_down, shared_qkv, early, width, [(first, (2,), whole)] + wanted)
    early = to_partner(early, first, group_size)
    parts = map_partners(partners, parts, group_size)
    arrived = [[early, *parts]]
    wanted = [(bits, every, tiles[1]) for bits in others + [0]]
    later = pack_qkv(shared_qkv, [parts[-1], early], width, wanted)
    arrived.append([early, parts[0], *map_partners(others, later, group_size)])
    places = []
    for n in range(2):
        span = (tiles[n][1] - tiles[n][0]) * LANES
        at = {bits: [(m + 2, c * span) for c in range(4)] for m, bits in enumerate(others + [0])}
        begin = tiles[n][0] * LANES
        at[first] = [(0, begin), (0, width + begin), (1, begin), (1, width)]
        places.append([at[bits] for bits in range(group_size)])
    low_rank, carried, keys, values, own, back = None, [], [], [], [], []
    for n in range(2):
        blocks, new_keys, new_values, low_rank, carried = attend(
            adapter_up,
            sink_logits,
            lengths,
            low_rank,
            arrived[n],
            places[n],
            carried,
            heads[n],
            tiles[n],
            done_tiles[n],
        )
        begin = done_tiles[n][0] * LANES
        own.append((blocks[0], 0, begin))
        back.append([(to_partner(blocks[bits], bits, group_size), bits, begin) for bits in partners])
        keys, values = keys + [new_keys], values + [new_values]
    starts = [0, cut - done_cut]
    cache = build_cache(keys, values, starts, lengths, block_table)
    hidden = join_heads(None, own + back[0], width, group_size)
    hidden = join_heads(hidden, back[1], width, group_size)
    return (hidden, cache)


def per_device(inputs, adapter_down, adapter_up, shared_qkv, sink_logits, lengths, block_table):
    group_size = lax.axis_size("seq")
    width = adapter_up.shape[2]
    tiled = (
        group_size & (group_size - 1) == 0
        and width % (2 * HD) == 0
        and width % LANES == 0
        and inputs.shape[0] % LANES == 0
        and inputs.shape[0] * group_size <= 512
    )
    chosen = per_device_tiled if tiled else per_device_general
    return chosen(inputs, adapter_down, adapter_up, shared_qkv, sink_logits, lengths, block_table)


def solution(mesh):
    return jax.shard_map(
        per_device,
        mesh=mesh,
        in_specs=(
            P(("batch", "seq"), None),
            P(),
            P(None, None, "seq"),
            P(("batch", "seq"), None),
            P("seq"),
            P("batch"),
            P("batch", None),
        ),
        out_specs=(P(("batch", "seq"), None), P("seq", "batch", None, None)),
        check_vma=False,
    )
```

```python
import jax
import jax.numpy as jnp
from jax import lax
from jax.experimental import pallas as pl
from jax.experimental.pallas import tpu as pltpu
from jax.sharding import PartitionSpec as P

HD = 224
RANK = 128
HEADS = 16
SEGS = 8
PAGE = 16


def segment_positions(lengths, total_rows):
    segment_ends = jnp.cumsum(lengths)
    segment_starts = segment_ends - lengths
    places = jnp.arange(total_rows, dtype=jnp.int32)
    segment = jnp.sum((places[:, None] >= segment_ends[None, :]).astype(jnp.int32), axis=1)
    member = segment[:, None] == jnp.arange(SEGS, dtype=jnp.int32)[None, :]
    offsets = jnp.sum(jnp.where(member, segment_starts[None, :], 0), axis=1)
    return (segment, places - offsets)


def per_device_general(inputs, adapter_down, adapter_up, shared_qkv, sink_logits, lengths, block_table):
    group_size = lax.axis_size("seq")
    tok_rows = inputs.shape[0]
    total_rows = tok_rows * group_size
    heads_local = adapter_up.shape[2] // HD
    window_span = total_rows // 2
    low_codes = jnp.dot(inputs, adapter_down, preferred_element_type=jnp.float32).astype(
        jnp.bfloat16
    )
    shared_base = shared_qkv.reshape(tok_rows, 3, HEADS * HD)
    low_rank = jnp.einsum(
        "tcr,crf->tcf",
        low_codes.reshape(tok_rows, 3, RANK),
        lax.all_gather(adapter_up, "seq", axis=2, tiled=True),
        preferred_element_type=jnp.float32,
    )
    merged = (shared_base.astype(jnp.float32) + low_rank).astype(jnp.bfloat16)
    sending = merged.reshape(tok_rows, 3, HEADS, HD)
    arrived = lax.all_to_all(sending, "seq", split_axis=2, concat_axis=0, tiled=True)
    segment, position = segment_positions(lengths, total_rows)
    tile_rows = min(512, total_rows)
    tile_count = total_rows // tile_rows
    scale_factor = HD ** (-0.5)

    def one_head(head_index):
        query_all = arrived[:, 0, head_index]
        key_all = arrived[:, 1, head_index]
        value_all = arrived[:, 2, head_index]
        sink_logit = sink_logits[head_index]

        def query_tile(tile_index):
            query_first = tile_index * tile_rows
            query_rows = lax.dynamic_slice_in_dim(query_all, query_first, tile_rows, 0)
            query_segs = lax.dynamic_slice_in_dim(segment, query_first, tile_rows, 0)
            query_place = query_first + jnp.arange(tile_rows, dtype=jnp.int32)
            start_state = (
                jnp.full((tile_rows,), sink_logit, jnp.float32),
                jnp.zeros((tile_rows,), jnp.float32),
                jnp.zeros((tile_rows, HD), jnp.float32),
            )

            def visit(key_tile, state):
                key_first = key_tile * tile_rows
                running_max, running_sum, weighted = state
                key_rows = lax.dynamic_slice_in_dim(key_all, key_first, tile_rows, 0)
                value_rows = lax.dynamic_slice_in_dim(value_all, key_first, tile_rows, 0)
                key_segs = lax.dynamic_slice_in_dim(segment, key_first, tile_rows, 0)
                key_place = key_first + jnp.arange(tile_rows, dtype=jnp.int32)
                scores = (
                    jnp.dot(query_rows, key_rows.T, preferred_element_type=jnp.float32)
                    * scale_factor
                )
                visible = (
                    (query_segs[:, None] == key_segs[None, :])
                    & (key_place[None, :] <= query_place[:, None])
                    & (query_place[:, None] - key_place[None, :] < window_span)
                )
                scores = jnp.where(visible, scores, -jnp.inf)
                new_max = jnp.maximum(running_max, jnp.max(scores, axis=1))
                rescale = jnp.exp(running_max - new_max)
                weights = jnp.exp(scores - new_max[:, None])
                new_sum = running_sum * rescale + jnp.sum(weights, axis=1)
                new_weighted = weighted * rescale[:, None] + jnp.dot(
                    weights.astype(jnp.bfloat16), value_rows, preferred_element_type=jnp.float32
                )
                return (new_max, new_sum, new_weighted)

            final_max, final_sum, weighted = lax.fori_loop(0, tile_count, visit, start_state)
            denominator = final_sum + jnp.exp(sink_logit - final_max)
            return (weighted / denominator[:, None]).astype(jnp.bfloat16)

        return lax.map(query_tile, jnp.arange(tile_count, dtype=jnp.int32)).reshape(total_rows, HD)

    attended = lax.map(one_head, jnp.arange(heads_local, dtype=jnp.int32))
    returned = lax.all_to_all(attended, "seq", split_axis=1, concat_axis=0, tiled=True)
    hidden = returned.transpose(1, 0, 2).reshape(tok_rows, HEADS * HD)
    page_count = total_rows // PAGE + SEGS
    page_index = block_table.reshape(-1)[segment * block_table.shape[1] + position // PAGE]
    cache_row = page_index * PAGE + position % PAGE

    def place(values_in):
        flat_cache = (
            jnp.zeros((page_count * PAGE, heads_local, HD), jnp.bfloat16)
            .at[cache_row]
            .set(values_in)
        )
        return (
            flat_cache.reshape(page_count, PAGE, heads_local, HD)
            .transpose(2, 0, 1, 3)
            .reshape(heads_local, page_count, PAGE * HD)
        )

    kv_cache = jnp.stack([place(arrived[:, 1]), place(arrived[:, 2])], axis=2)
    return (hidden, kv_cache)


LANES = 128
SLABS = 1
BF16 = jnp.bfloat16
F32 = jnp.float32
ANYWHERE = pl.BlockSpec(memory_space=pl.ANY)
IN_HBM = pl.BlockSpec(memory_space=pltpu.HBM)
IN_VMEM = pl.BlockSpec(memory_space=pltpu.VMEM)
IN_SMEM = pl.BlockSpec(memory_space=pltpu.SMEM)


def sends(group_size):
    return sorted(range(1, group_size), key=lambda bits: (-bits.bit_count(), bits))


def to_partner(values, bits, group_size):
    return lax.ppermute(values, "seq", [(i, i ^ bits) for i in range(group_size)])


def map_partners(partners, parts, group_size):
    sent = [to_partner(part, bits, group_size) for bits, part in zip(partners, parts)]
    return sent + list(parts[len(partners) :])


def params(mebibytes=40):
    return pltpu.CompilerParams(vmem_limit_bytes=mebibytes * 1024 * 1024)


def stay(values):
    return pltpu.with_memory_space_constraint(values, pltpu.HBM)


def cost(flops, moved):
    return pl.CostEstimate(flops=flops, bytes_accessed=moved, transcendentals=0)


def start_columns(shared, outs, sem, width, wanted):
    me = lax.axis_index("seq")
    slab = shared.shape[0] // SLABS
    copies = []
    for n, (bits, kinds, tiles) in enumerate(wanted):
        span = (tiles[1] - tiles[0]) * LANES
        owner = jnp.bitwise_xor(me, bits)
        for m, c in enumerate(kinds):
            first = pl.multiple_of(c * HEADS * HD + owner * width + tiles[0] * LANES, LANES)
            for k in range(SLABS):
                rows = pl.ds(k * slab, slab)
                copies.append(
                    pltpu.make_async_copy(
                        shared.at[rows, pl.ds(first, span)],
                        outs[n].at[rows, pl.ds(m * span, span)],
                        sem.at[n, m, k],
                    )
                )
    for copy in copies:
        copy.start()
    return copies


def make_codes(inputs, adapter_down, shared_qkv, after, width, wanted):
    tok_rows, depth = inputs.shape
    code_width = adapter_down.shape[1]
    steps = 8
    chunk = depth // steps
    spans = [len(kinds) * (tiles[1] - tiles[0]) * LANES for _, kinds, tiles in wanted]

    def body(inputs_ref, down_ref, shared, _, *refs):
        outs, (held, down, in_sem, down_sem, sem) = refs[:-5], refs[-5:]
        loads = []
        for step in range(steps):
            at = pl.ds(step * chunk, chunk)
            loads.append(
                (
                    pltpu.make_async_copy(inputs_ref.at[:, at], held.at[:, at], in_sem.at[step]),
                    pltpu.make_async_copy(down_ref.at[at, :], down.at[at, :], down_sem.at[step]),
                )
            )
            for load in loads[-1]:
                load.start()
        copies = start_columns(shared, outs, sem, width, wanted)
        total = None
        for step in range(steps):
            for load in loads[step]:
                load.wait()
            at = slice(step * chunk, (step + 1) * chunk)
            term = jnp.dot(held[:, at], down[at, :], preferred_element_type=F32)
            total = term if total is None else total + term
        own_codes = total.astype(BF16)
        for out, span in zip(outs, spans):
            out[:, span:] = own_codes
        for copy in copies:
            copy.wait()

    return pl.pallas_call(
        body,
        out_shape=[jax.ShapeDtypeStruct((tok_rows, span + code_width), BF16) for span in spans],
        in_specs=[IN_HBM, IN_HBM, IN_HBM, ANYWHERE],
        out_specs=[IN_VMEM] * len(wanted),
        scratch_shapes=[
            pltpu.VMEM((tok_rows, depth), BF16),
            pltpu.VMEM((depth, code_width), BF16),
            pltpu.SemaphoreType.DMA((steps,)),
            pltpu.SemaphoreType.DMA((steps,)),
            pltpu.SemaphoreType.DMA((len(wanted), 3, SLABS)),
        ],
        compiler_params=params(20),
        cost_estimate=cost(2 * tok_rows * depth * code_width, depth * code_width * 2),
        name="make_codes",
    )(stay(inputs), stay(adapter_down), stay(shared_qkv), after)


def pack_qkv(shared_qkv, after, width, wanted):
    tok_rows = shared_qkv.shape[0]
    spans = [len(kinds) * (tiles[1] - tiles[0]) * LANES for _, kinds, tiles in wanted]

    def body(shared, *refs):
        outs, sem = refs[len(after) : -1], refs[-1]
        for copy in start_columns(shared, outs, sem, width, wanted):
            copy.wait()

    return pl.pallas_call(
        body,
        out_shape=[jax.ShapeDtypeStruct((tok_rows, span), BF16) for span in spans],
        in_specs=[IN_HBM] + [ANYWHERE] * len(after),
        out_specs=[IN_VMEM] * len(wanted),
        scratch_shapes=[pltpu.SemaphoreType.DMA((len(wanted), 3, SLABS))],
        compiler_params=params(20),
        cost_estimate=cost(0, 2 * tok_rows * sum(spans) * 2),
        name="pack_qkv",
    )(stay(shared_qkv), *after)


def head_tiles(h):
    return (h * HD // LANES, -(-(h + 1) * HD // LANES))


def side_by_side(ref, window, rows):
    return jnp.concatenate([ref[tile, rows, :] for tile in window], axis=1)


def attend(up, sink_logits, lengths, low_rank, arrived, places, carried, heads, tiles, done_tiles):
    group_size = len(places)
    tok_rows = arrived[0].shape[0]
    total_rows = tok_rows * group_size
    window_span = total_rows // 2
    scale_factor = HD ** (-0.5)
    span = (tiles[1] - tiles[0]) * LANES
    done_span = (done_tiles[1] - done_tiles[0]) * LANES
    low_tile = min(tiles[0], done_tiles[0])
    kept = (tiles[0] - low_tile) * LANES
    left = (tiles[1] - done_tiles[1]) * LANES
    first_call, last = low_rank is None, left == 0
    all_tiles = (kept + span) // LANES
    given_low = [] if first_call else [low_rank]
    rest = up.shape[2] - tiles[1] * LANES

    def body(*refs):
        refs = list(refs)
        take = lambda n: [refs.pop(0) for _ in range(n)]
        up_ref, sinks, lens = take(3)
        low_refs = take(len(given_low))
        arrived_refs = take(len(arrived))
        before = take(len(carried))
        outs = take(group_size)
        keys, values = take(2)
        carried_out = take(0 if last else 3)
        queries, merged = take(2)
        me = lax.axis_index("seq")
        kept_tiles = kept // LANES
        if kept:
            for target, source in zip((queries, merged, keys, values), before):
                target[:kept_tiles] = source[source.shape[0] - kept_tiles :]
        for bits in range(group_size):
            place = pl.ds(pl.multiple_of(jnp.bitwise_xor(me, bits) * tok_rows, tok_rows), tok_rows)
            for c, target in enumerate((queries, keys, values)):
                if first_call:
                    which, at = places[bits][3]
                    codes = arrived_refs[which][:, at + c * RANK : at + (c + 1) * RANK]
                    low = jnp.dot(codes, up_ref[c, :, :span], preferred_element_type=F32)
                    carried_out[0][bits, :, c * rest : (c + 1) * rest] = jnp.dot(
                        codes, up_ref[c, :, span:], preferred_element_type=F32
                    )
                else:
                    low = low_refs[0][bits, :, c * span : (c + 1) * span]
                which, at = places[bits][c]
                base = arrived_refs[which][:, at : at + span].astype(F32)
                new = (base + low).astype(BF16)
                for n in range(tiles[1] - tiles[0]):
                    target[kept_tiles + n, place, :] = new[:, n * LANES : (n + 1) * LANES]

        ends = []
        for s in range(SEGS):
            ends.append(lens[s] + (ends[-1] if ends else 0))
        blocks = []
        for b in range(group_size):
            first_query = b * tok_rows
            rows = slice(first_query, first_query + tok_rows)
            first_key = max(0, (first_query - window_span + 1) // tok_rows * tok_rows)
            key_rows = slice(first_key, first_query + tok_rows)
            query_place = first_query + lax.broadcasted_iota(jnp.int32, (tok_rows, 1), 0)
            earliest = query_place - (window_span - 1)
            for s in range(SEGS):
                earliest = jnp.where(ends[s] <= query_place, jnp.maximum(earliest, ends[s]), earliest)
            key_place = first_key + lax.broadcasted_iota(jnp.int32, (tok_rows, key_rows.stop - first_key), 1)
            visible = (key_place >= earliest) & (key_place <= query_place)
            scores = {}
            for h in heads:
                first_tile, end_tile = head_tiles(h)
                window = range(first_tile - low_tile, end_tile - low_tile)
                column = first_tile * LANES + lax.broadcasted_iota(jnp.int32, (1, len(window) * LANES), 1)
                mine = (column >= h * HD) & (column < (h + 1) * HD)
                query = side_by_side(queries, window, rows)
                query = jnp.where(mine, query, jnp.zeros_like(query))
                scores[h] = lax.dot_general(
                    query,
                    side_by_side(keys, window, key_rows),
                    (((1,), (1,)), ((), ())),
                    preferred_element_type=F32,
                )
            blocks.append((rows, key_rows, visible, scores))
        for rows, key_rows, visible, scores in blocks:
            parts = {}
            for tile in range(low_tile, tiles[0]):
                parts[tile] = merged[tile - low_tile, rows, :].astype(F32)
            for h in heads:
                first_tile, end_tile = head_tiles(h)
                window = range(first_tile - low_tile, end_tile - low_tile)
                seen = jnp.where(visible, scores[h] * scale_factor, -jnp.inf)
                top = jnp.maximum(jnp.max(seen, axis=1, keepdims=True), sinks[h])
                weights = jnp.exp(seen - top)
                denominator = jnp.sum(weights, axis=1, keepdims=True) + jnp.exp(sinks[h] - top)
                mixed = jnp.dot(
                    weights.astype(BF16),
                    side_by_side(values, window, key_rows),
                    preferred_element_type=F32,
                ) / denominator
                for tile in range(first_tile, end_tile):
                    at = (tile - first_tile) * LANES
                    piece = mixed[:, at : at + LANES]
                    if tile in parts:
                        lane = tile * LANES + lax.broadcasted_iota(jnp.int32, (1, LANES), 1)
                        piece = jnp.where(lane < h * HD, parts[tile], piece)
                    parts[tile] = piece
            for tile, piece in parts.items():
                merged[tile - low_tile, rows, :] = piece.astype(BF16)
        for bits in range(group_size):
            place = pl.ds(pl.multiple_of(jnp.bitwise_xor(me, bits) * tok_rows, tok_rows), tok_rows)
            outs[bits][...] = side_by_side(merged, range(done_tiles[1] - done_tiles[0]), place)
        if not last:
            carried_out[1][...] = queries[all_tiles - left // LANES :]
            carried_out[2][...] = merged[all_tiles - left // LANES :]

    block = jax.ShapeDtypeStruct((tok_rows, done_span), BF16)
    stream = jax.ShapeDtypeStruct((all_tiles, total_rows, LANES), BF16)
    leftover = jax.ShapeDtypeStruct((left // LANES, total_rows, LANES), BF16)
    next_low = jax.ShapeDtypeStruct((group_size, tok_rows, 3 * rest), F32)
    out_shape = [block] * group_size + [stream] * 2 + ([] if last else [next_low, leftover, leftover])
    results = pl.pallas_call(
        body,
        out_shape=out_shape,
        in_specs=[IN_VMEM, IN_SMEM, IN_SMEM]
        + [IN_VMEM] * (len(given_low) + len(arrived) + len(carried)),
        out_specs=[IN_VMEM] * len(out_shape),
        scratch_shapes=[pltpu.VMEM((all_tiles, total_rows, LANES), BF16)] * 2,
        compiler_params=params(),
        cost_estimate=cost(4 * total_rows * total_rows * span, 8 * total_rows * span * 2),
        name="attend",
    )(up, sink_logits, lengths, *given_low, *arrived, *carried)
    blocks, (keys, values) = results[:group_size], results[group_size : group_size + 2]
    if last:
        return blocks, keys, values, None, []
    next_low, *leftovers = results[group_size + 2 :]
    return blocks, keys, values, next_low, [*leftovers, keys, values]


def build_cache(keys, values, starts, lengths, block_table):
    total_rows = keys[0].shape[1]
    parts = len(keys)
    width = sum(part.shape[0] - start for part, start in zip(keys, starts)) * LANES
    heads_local = width // HD
    page_count = total_rows // PAGE + SEGS
    blocks = block_table.shape[1]
    group = 4

    def body(*refs):
        key_refs, value_refs = refs[:parts], refs[parts : 2 * parts]
        lens, table, out, built, sem = refs[2 * parts :]
        page = lax.broadcasted_iota(jnp.int32, (page_count, blocks), 0)
        block = lax.broadcasted_iota(jnp.int32, (page_count, blocks), 1)
        first = jnp.zeros((page_count, blocks), jnp.int32)
        count = jnp.zeros((page_count, blocks), jnp.int32)
        start = 0
        for s in range(SEGS):
            left = lens[s] - block * PAGE
            held = (table[s : s + 1, :] == page) & (left > 0)
            first = jnp.where(held, start + block * PAGE, first)
            count = jnp.where(held, jnp.minimum(left, PAGE), count)
            start = start + lens[s]
        first = jnp.sum(first, axis=1, keepdims=True)
        count = jnp.sum(count, axis=1, keepdims=True)
        place = lax.broadcasted_iota(jnp.int32, (group * page_count, total_rows), 1)

        def gathered(part_refs):
            every = [(ref, tile) for ref, low in zip(part_refs, starts) for tile in range(low, ref.shape[0])]
            return jnp.concatenate([ref[tile] for ref, tile in every], axis=1)

        all_keys, all_values = gathered(key_refs), gathered(value_refs)
        copies = []
        for r in range(0, PAGE, group):
            wanted = [jnp.where(count > r + n, first + r + n, -1) for n in range(group)]
            pick = (place == jnp.concatenate(wanted, axis=0)).astype(F32).astype(BF16)
            picked = [jnp.dot(pick, every, preferred_element_type=F32) for every in (all_keys, all_values)]
            lanes = slice(r * HD, (r + group) * HD)
            for h in range(heads_local):
                columns = slice(h * HD, (h + 1) * HD)
                for c in range(2):
                    line = jnp.concatenate(
                        [picked[c][m * page_count : (m + 1) * page_count, columns] for m in range(group)], axis=1
                    )
                    built[h, :, c, lanes] = line.astype(BF16)
                copies.append(
                    pltpu.make_async_copy(
                        built.at[h, :, :, lanes], out.at[h, :, :, lanes], sem.at[h, r // group]
                    )
                )
                copies[-1].start()
        for copy in copies:
            copy.wait()

    cache = (heads_local, page_count, 2, PAGE * HD)
    return pl.pallas_call(
        body,
        out_shape=jax.ShapeDtypeStruct(cache, BF16),
        in_specs=[IN_VMEM] * (2 * parts) + [IN_SMEM, IN_VMEM],
        out_specs=IN_HBM,
        scratch_shapes=[pltpu.VMEM(cache, BF16), pltpu.SemaphoreType.DMA((heads_local, PAGE // group))],
        compiler_params=params(),
        cost_estimate=cost(4 * page_count * PAGE * total_rows * width, 4 * total_rows * width * 2),
        name="build_cache",
    )(*keys, *values, lengths, block_table)


def join_heads(hidden, parts, width, group_size):
    tok_rows = parts[0][0].shape[0]
    slab = tok_rows // SLABS
    given = [] if hidden is None else [hidden]

    def body(*refs):
        out, sem = refs[-2:]
        me = lax.axis_index("seq")
        copies = []
        for n, (part, bits, begin) in enumerate(parts):
            first = pl.multiple_of(jnp.bitwise_xor(me, bits) * width + begin, LANES)
            for k in range(SLABS):
                rows = pl.ds(k * slab, slab)
                copies.append(
                    pltpu.make_async_copy(
                        refs[n].at[rows, :], out.at[rows, pl.ds(first, part.shape[1])], sem.at[n, k]
                    )
                )
        for copy in copies:
            copy.start()
        for copy in copies:
            copy.wait()

    return pl.pallas_call(
        body,
        out_shape=jax.ShapeDtypeStruct((tok_rows, width * group_size), BF16),
        in_specs=[ANYWHERE] * len(parts) + [IN_HBM] * len(given),
        out_specs=IN_HBM,
        scratch_shapes=[pltpu.SemaphoreType.DMA((len(parts), SLABS))],
        input_output_aliases={len(parts): 0} if given else {},
        compiler_params=params(),
        cost_estimate=cost(0, 4 * tok_rows * sum(part.shape[1] for part, _, _ in parts)),
        name="join_heads",
    )(*[part for part, _, _ in parts], *map(stay, given))


def per_device_tiled(inputs, adapter_down, adapter_up, shared_qkv, sink_logits, lengths, block_table):
    group_size = lax.axis_size("seq")
    partners = sends(group_size)
    width = adapter_up.shape[2]
    heads_local = width // HD
    half = heads_local // 2
    all_tiles = width // LANES
    cut = -(-half * HD // LANES)
    done_cut = half * HD // LANES
    tiles = [(0, cut), (cut, all_tiles)]
    done_tiles = [(0, done_cut), (done_cut, all_tiles)]
    heads = [tuple(range(half)), tuple(range(half, heads_local))]

    every = (0, 1, 2)
    first, others = partners[0], partners[1:]
    whole = (0, all_tiles)
    (early,) = pack_qkv(shared_qkv, [], width, [(first, (0, 1), whole)])
    wanted = [(bits, every, tiles[0]) for bits in others + [0]]
    parts = make_codes(inputs, adapter_down, shared_qkv, early, width, [(first, (2,), whole)] + wanted)
    early = to_partner(early, first, group_size)
    parts = map_partners(partners, parts, group_size)
    arrived = [[early, *parts]]
    wanted = [(bits, every, tiles[1]) for bits in others + [0]]
    later = pack_qkv(shared_qkv, [parts[-1], early], width, wanted)
    arrived.append([early, parts[0], *map_partners(others, later, group_size)])
    places = []
    for n in range(2):
        span = (tiles[n][1] - tiles[n][0]) * LANES
        at = {bits: [(m + 2, c * span) for c in range(4)] for m, bits in enumerate(others + [0])}
        begin = tiles[n][0] * LANES
        at[first] = [(0, begin), (0, width + begin), (1, begin), (1, width)]
        places.append([at[bits] for bits in range(group_size)])
    low_rank, carried, keys, values, own, back = None, [], [], [], [], []
    for n in range(2):
        blocks, new_keys, new_values, low_rank, carried = attend(
            adapter_up,
            sink_logits,
            lengths,
            low_rank,
            arrived[n],
            places[n],
            carried,
            heads[n],
            tiles[n],
            done_tiles[n],
        )
        begin = done_tiles[n][0] * LANES
        own.append((blocks[0], 0, begin))
        back.append([(to_partner(blocks[bits], bits, group_size), bits, begin) for bits in [partners[2], partners[0], partners[1]]])
        keys, values = keys + [new_keys], values + [new_values]
    starts = [0, cut - done_cut]
    cache = build_cache(keys, values, starts, lengths, block_table)
    hidden = join_heads(None, own + back[0], width, group_size)
    hidden = join_heads(hidden, back[1], width, group_size)
    return (hidden, cache)


def per_device(inputs, adapter_down, adapter_up, shared_qkv, sink_logits, lengths, block_table):
    group_size = lax.axis_size("seq")
    width = adapter_up.shape[2]
    tiled = (
        group_size & (group_size - 1) == 0
        and width % (2 * HD) == 0
        and width % LANES == 0
        and inputs.shape[0] % LANES == 0
        and inputs.shape[0] * group_size <= 512
    )
    chosen = per_device_tiled if tiled else per_device_general
    return chosen(inputs, adapter_down, adapter_up, shared_qkv, sink_logits, lengths, block_table)


def solution(mesh):
    return jax.shard_map(
        per_device,
        mesh=mesh,
        in_specs=(
            P(("batch", "seq"), None),
            P(),
            P(None, None, "seq"),
            P(("batch", "seq"), None),
            P("seq"),
            P("batch"),
            P("batch", None),
        ),
        out_specs=(P(("batch", "seq"), None), P("seq", "batch", None, None)),
        check_vma=False,
    )
```

```python
import jax
import jax.numpy as jnp
from jax import lax
from jax.experimental import pallas as pl
from jax.experimental.pallas import tpu as pltpu
from jax.sharding import PartitionSpec as P

HD = 224
RANK = 128
HEADS = 16
SEGS = 8
PAGE = 16


def segment_positions(lengths, total_rows):
    segment_ends = jnp.cumsum(lengths)
    segment_starts = segment_ends - lengths
    places = jnp.arange(total_rows, dtype=jnp.int32)
    segment = jnp.sum((places[:, None] >= segment_ends[None, :]).astype(jnp.int32), axis=1)
    member = segment[:, None] == jnp.arange(SEGS, dtype=jnp.int32)[None, :]
    offsets = jnp.sum(jnp.where(member, segment_starts[None, :], 0), axis=1)
    return (segment, places - offsets)


def per_device_general(inputs, adapter_down, adapter_up, shared_qkv, sink_logits, lengths, block_table):
    group_size = lax.axis_size("seq")
    tok_rows = inputs.shape[0]
    total_rows = tok_rows * group_size
    heads_local = adapter_up.shape[2] // HD
    window_span = total_rows // 2
    low_codes = jnp.dot(inputs, adapter_down, preferred_element_type=jnp.float32).astype(
        jnp.bfloat16
    )
    shared_base = shared_qkv.reshape(tok_rows, 3, HEADS * HD)
    low_rank = jnp.einsum(
        "tcr,crf->tcf",
        low_codes.reshape(tok_rows, 3, RANK),
        lax.all_gather(adapter_up, "seq", axis=2, tiled=True),
        preferred_element_type=jnp.float32,
    )
    merged = (shared_base.astype(jnp.float32) + low_rank).astype(jnp.bfloat16)
    sending = merged.reshape(tok_rows, 3, HEADS, HD)
    arrived = lax.all_to_all(sending, "seq", split_axis=2, concat_axis=0, tiled=True)
    segment, position = segment_positions(lengths, total_rows)
    tile_rows = min(512, total_rows)
    tile_count = total_rows // tile_rows
    scale_factor = HD ** (-0.5)

    def one_head(head_index):
        query_all = arrived[:, 0, head_index]
        key_all = arrived[:, 1, head_index]
        value_all = arrived[:, 2, head_index]
        sink_logit = sink_logits[head_index]

        def query_tile(tile_index):
            query_first = tile_index * tile_rows
            query_rows = lax.dynamic_slice_in_dim(query_all, query_first, tile_rows, 0)
            query_segs = lax.dynamic_slice_in_dim(segment, query_first, tile_rows, 0)
            query_place = query_first + jnp.arange(tile_rows, dtype=jnp.int32)
            start_state = (
                jnp.full((tile_rows,), sink_logit, jnp.float32),
                jnp.zeros((tile_rows,), jnp.float32),
                jnp.zeros((tile_rows, HD), jnp.float32),
            )

            def visit(key_tile, state):
                key_first = key_tile * tile_rows
                running_max, running_sum, weighted = state
                key_rows = lax.dynamic_slice_in_dim(key_all, key_first, tile_rows, 0)
                value_rows = lax.dynamic_slice_in_dim(value_all, key_first, tile_rows, 0)
                key_segs = lax.dynamic_slice_in_dim(segment, key_first, tile_rows, 0)
                key_place = key_first + jnp.arange(tile_rows, dtype=jnp.int32)
                scores = (
                    jnp.dot(query_rows, key_rows.T, preferred_element_type=jnp.float32)
                    * scale_factor
                )
                visible = (
                    (query_segs[:, None] == key_segs[None, :])
                    & (key_place[None, :] <= query_place[:, None])
                    & (query_place[:, None] - key_place[None, :] < window_span)
                )
                scores = jnp.where(visible, scores, -jnp.inf)
                new_max = jnp.maximum(running_max, jnp.max(scores, axis=1))
                rescale = jnp.exp(running_max - new_max)
                weights = jnp.exp(scores - new_max[:, None])
                new_sum = running_sum * rescale + jnp.sum(weights, axis=1)
                new_weighted = weighted * rescale[:, None] + jnp.dot(
                    weights.astype(jnp.bfloat16), value_rows, preferred_element_type=jnp.float32
                )
                return (new_max, new_sum, new_weighted)

            final_max, final_sum, weighted = lax.fori_loop(0, tile_count, visit, start_state)
            denominator = final_sum + jnp.exp(sink_logit - final_max)
            return (weighted / denominator[:, None]).astype(jnp.bfloat16)

        return lax.map(query_tile, jnp.arange(tile_count, dtype=jnp.int32)).reshape(total_rows, HD)

    attended = lax.map(one_head, jnp.arange(heads_local, dtype=jnp.int32))
    returned = lax.all_to_all(attended, "seq", split_axis=1, concat_axis=0, tiled=True)
    hidden = returned.transpose(1, 0, 2).reshape(tok_rows, HEADS * HD)
    page_count = total_rows // PAGE + SEGS
    page_index = block_table.reshape(-1)[segment * block_table.shape[1] + position // PAGE]
    cache_row = page_index * PAGE + position % PAGE

    def place(values_in):
        flat_cache = (
            jnp.zeros((page_count * PAGE, heads_local, HD), jnp.bfloat16)
            .at[cache_row]
            .set(values_in)
        )
        return (
            flat_cache.reshape(page_count, PAGE, heads_local, HD)
            .transpose(2, 0, 1, 3)
            .reshape(heads_local, page_count, PAGE * HD)
        )

    kv_cache = jnp.stack([place(arrived[:, 1]), place(arrived[:, 2])], axis=2)
    return (hidden, kv_cache)


LANES = 128
SLABS = 1
BF16 = jnp.bfloat16
F32 = jnp.float32
ANYWHERE = pl.BlockSpec(memory_space=pl.ANY)
IN_HBM = pl.BlockSpec(memory_space=pltpu.HBM)
IN_VMEM = pl.BlockSpec(memory_space=pltpu.VMEM)
IN_SMEM = pl.BlockSpec(memory_space=pltpu.SMEM)


def sends(group_size):
    return sorted(range(1, group_size), key=lambda bits: (-bits.bit_count(), bits))


def to_partner(values, bits, group_size):
    return lax.ppermute(values, "seq", [(i, i ^ bits) for i in range(group_size)])


def map_partners(partners, parts, group_size):
    sent = [to_partner(part, bits, group_size) for bits, part in zip(partners, parts)]
    return sent + list(parts[len(partners) :])


def params(mebibytes=40):
    return pltpu.CompilerParams(vmem_limit_bytes=mebibytes * 1024 * 1024)


def stay(values):
    return pltpu.with_memory_space_constraint(values, pltpu.HBM)


def cost(flops, moved):
    return pl.CostEstimate(flops=flops, bytes_accessed=moved, transcendentals=0)


def start_columns(shared, outs, sem, width, wanted):
    me = lax.axis_index("seq")
    slab = shared.shape[0] // SLABS
    copies = []
    for n, (bits, kinds, tiles) in enumerate(wanted):
        span = (tiles[1] - tiles[0]) * LANES
        owner = jnp.bitwise_xor(me, bits)
        for m, c in enumerate(kinds):
            first = pl.multiple_of(c * HEADS * HD + owner * width + tiles[0] * LANES, LANES)
            for k in range(SLABS):
                rows = pl.ds(k * slab, slab)
                copies.append(
                    pltpu.make_async_copy(
                        shared.at[rows, pl.ds(first, span)],
                        outs[n].at[rows, pl.ds(m * span, span)],
                        sem.at[n, m, k],
                    )
                )
    for copy in copies:
        copy.start()
    return copies


def make_codes(inputs, adapter_down, shared_qkv, after, width, wanted):
    tok_rows, depth = inputs.shape
    code_width = adapter_down.shape[1]
    steps = 8
    chunk = depth // steps
    spans = [len(kinds) * (tiles[1] - tiles[0]) * LANES for _, kinds, tiles in wanted]

    def body(inputs_ref, down_ref, shared, _, *refs):
        outs, (held, down, in_sem, down_sem, sem) = refs[:-5], refs[-5:]
        loads = []
        for step in range(steps):
            at = pl.ds(step * chunk, chunk)
            loads.append(
                (
                    pltpu.make_async_copy(inputs_ref.at[:, at], held.at[:, at], in_sem.at[step]),
                    pltpu.make_async_copy(down_ref.at[at, :], down.at[at, :], down_sem.at[step]),
                )
            )
            for load in loads[-1]:
                load.start()
        copies = start_columns(shared, outs, sem, width, wanted)
        total = None
        for step in range(steps):
            for load in loads[step]:
                load.wait()
            at = slice(step * chunk, (step + 1) * chunk)
            term = jnp.dot(held[:, at], down[at, :], preferred_element_type=F32)
            total = term if total is None else total + term
        own_codes = total.astype(BF16)
        for out, span in zip(outs, spans):
            out[:, span:] = own_codes
        for copy in copies:
            copy.wait()

    return pl.pallas_call(
        body,
        out_shape=[jax.ShapeDtypeStruct((tok_rows, span + code_width), BF16) for span in spans],
        in_specs=[IN_HBM, IN_HBM, IN_HBM, ANYWHERE],
        out_specs=[IN_VMEM] * len(wanted),
        scratch_shapes=[
            pltpu.VMEM((tok_rows, depth), BF16),
            pltpu.VMEM((depth, code_width), BF16),
            pltpu.SemaphoreType.DMA((steps,)),
            pltpu.SemaphoreType.DMA((steps,)),
            pltpu.SemaphoreType.DMA((len(wanted), 3, SLABS)),
        ],
        compiler_params=params(20),
        cost_estimate=cost(2 * tok_rows * depth * code_width, depth * code_width * 2),
        name="make_codes",
    )(stay(inputs), stay(adapter_down), stay(shared_qkv), after)


def pack_qkv(shared_qkv, after, width, wanted):
    tok_rows = shared_qkv.shape[0]
    spans = [len(kinds) * (tiles[1] - tiles[0]) * LANES for _, kinds, tiles in wanted]

    def body(shared, *refs):
        outs, sem = refs[len(after) : -1], refs[-1]
        for copy in start_columns(shared, outs, sem, width, wanted):
            copy.wait()

    return pl.pallas_call(
        body,
        out_shape=[jax.ShapeDtypeStruct((tok_rows, span), BF16) for span in spans],
        in_specs=[IN_HBM] + [ANYWHERE] * len(after),
        out_specs=[IN_VMEM] * len(wanted),
        scratch_shapes=[pltpu.SemaphoreType.DMA((len(wanted), 3, SLABS))],
        compiler_params=params(20),
        cost_estimate=cost(0, 2 * tok_rows * sum(spans) * 2),
        name="pack_qkv",
    )(stay(shared_qkv), *after)


def head_tiles(h):
    return (h * HD // LANES, -(-(h + 1) * HD // LANES))


def side_by_side(ref, window, rows):
    return jnp.concatenate([ref[tile, rows, :] for tile in window], axis=1)


def attend(up, sink_logits, lengths, low_rank, arrived, places, carried, heads, tiles, done_tiles):
    group_size = len(places)
    tok_rows = arrived[0].shape[0]
    total_rows = tok_rows * group_size
    window_span = total_rows // 2
    scale_factor = HD ** (-0.5)
    span = (tiles[1] - tiles[0]) * LANES
    done_span = (done_tiles[1] - done_tiles[0]) * LANES
    low_tile = min(tiles[0], done_tiles[0])
    kept = (tiles[0] - low_tile) * LANES
    left = (tiles[1] - done_tiles[1]) * LANES
    first_call, last = low_rank is None, left == 0
    all_tiles = (kept + span) // LANES
    given_low = [] if first_call else [low_rank]
    rest = up.shape[2] - tiles[1] * LANES

    def body(*refs):
        refs = list(refs)
        take = lambda n: [refs.pop(0) for _ in range(n)]
        up_ref, sinks, lens = take(3)
        low_refs = take(len(given_low))
        arrived_refs = take(len(arrived))
        before = take(len(carried))
        outs = take(group_size)
        keys, values = take(2)
        carried_out = take(0 if last else 3)
        queries, merged = take(2)
        me = lax.axis_index("seq")
        kept_tiles = kept // LANES
        if kept:
            for target, source in zip((queries, merged, keys, values), before):
                target[:kept_tiles] = source[source.shape[0] - kept_tiles :]
        for bits in range(group_size):
            place = pl.ds(pl.multiple_of(jnp.bitwise_xor(me, bits) * tok_rows, tok_rows), tok_rows)
            for c, target in enumerate((queries, keys, values)):
                if first_call:
                    which, at = places[bits][3]
                    codes = arrived_refs[which][:, at + c * RANK : at + (c + 1) * RANK]
                    low = jnp.dot(codes, up_ref[c, :, :span], preferred_element_type=F32)
                    carried_out[0][bits, :, c * rest : (c + 1) * rest] = jnp.dot(
                        codes, up_ref[c, :, span:], preferred_element_type=F32
                    )
                else:
                    low = low_refs[0][bits, :, c * span : (c + 1) * span]
                which, at = places[bits][c]
                base = arrived_refs[which][:, at : at + span].astype(F32)
                new = (base + low).astype(BF16)
                for n in range(tiles[1] - tiles[0]):
                    target[kept_tiles + n, place, :] = new[:, n * LANES : (n + 1) * LANES]

        ends = []
        for s in range(SEGS):
            ends.append(lens[s] + (ends[-1] if ends else 0))
        blocks = []
        for b in range(group_size):
            first_query = b * tok_rows
            rows = slice(first_query, first_query + tok_rows)
            first_key = max(0, (first_query - window_span + 1) // tok_rows * tok_rows)
            key_rows = slice(first_key, first_query + tok_rows)
            query_place = first_query + lax.broadcasted_iota(jnp.int32, (tok_rows, 1), 0)
            earliest = query_place - (window_span - 1)
            for s in range(SEGS):
                earliest = jnp.where(ends[s] <= query_place, jnp.maximum(earliest, ends[s]), earliest)
            key_place = first_key + lax.broadcasted_iota(jnp.int32, (tok_rows, key_rows.stop - first_key), 1)
            visible = (key_place >= earliest) & (key_place <= query_place)
            scores = {}
            for h in heads:
                first_tile, end_tile = head_tiles(h)
                window = range(first_tile - low_tile, end_tile - low_tile)
                column = first_tile * LANES + lax.broadcasted_iota(jnp.int32, (1, len(window) * LANES), 1)
                mine = (column >= h * HD) & (column < (h + 1) * HD)
                query = side_by_side(queries, window, rows)
                query = jnp.where(mine, query, jnp.zeros_like(query))
                scores[h] = lax.dot_general(
                    query,
                    side_by_side(keys, window, key_rows),
                    (((1,), (1,)), ((), ())),
                    preferred_element_type=F32,
                )
            blocks.append((rows, key_rows, visible, scores))
        for rows, key_rows, visible, scores in blocks:
            parts = {}
            for tile in range(low_tile, tiles[0]):
                parts[tile] = merged[tile - low_tile, rows, :].astype(F32)
            for h in heads:
                first_tile, end_tile = head_tiles(h)
                window = range(first_tile - low_tile, end_tile - low_tile)
                seen = jnp.where(visible, scores[h] * scale_factor, -jnp.inf)
                top = jnp.maximum(jnp.max(seen, axis=1, keepdims=True), sinks[h])
                weights = jnp.exp(seen - top)
                denominator = jnp.sum(weights, axis=1, keepdims=True) + jnp.exp(sinks[h] - top)
                mixed = jnp.dot(
                    weights.astype(BF16),
                    side_by_side(values, window, key_rows),
                    preferred_element_type=F32,
                ) / denominator
                for tile in range(first_tile, end_tile):
                    at = (tile - first_tile) * LANES
                    piece = mixed[:, at : at + LANES]
                    if tile in parts:
                        lane = tile * LANES + lax.broadcasted_iota(jnp.int32, (1, LANES), 1)
                        piece = jnp.where(lane < h * HD, parts[tile], piece)
                    parts[tile] = piece
            for tile, piece in parts.items():
                merged[tile - low_tile, rows, :] = piece.astype(BF16)
        for bits in range(group_size):
            place = pl.ds(pl.multiple_of(jnp.bitwise_xor(me, bits) * tok_rows, tok_rows), tok_rows)
            outs[bits][...] = side_by_side(merged, range(done_tiles[1] - done_tiles[0]), place)
        if not last:
            carried_out[1][...] = queries[all_tiles - left // LANES :]
            carried_out[2][...] = merged[all_tiles - left // LANES :]

    block = jax.ShapeDtypeStruct((tok_rows, done_span), BF16)
    stream = jax.ShapeDtypeStruct((all_tiles, total_rows, LANES), BF16)
    leftover = jax.ShapeDtypeStruct((left // LANES, total_rows, LANES), BF16)
    next_low = jax.ShapeDtypeStruct((group_size, tok_rows, 3 * rest), F32)
    out_shape = [block] * group_size + [stream] * 2 + ([] if last else [next_low, leftover, leftover])
    results = pl.pallas_call(
        body,
        out_shape=out_shape,
        in_specs=[IN_VMEM, IN_SMEM, IN_SMEM]
        + [IN_VMEM] * (len(given_low) + len(arrived) + len(carried)),
        out_specs=[IN_VMEM] * len(out_shape),
        scratch_shapes=[pltpu.VMEM((all_tiles, total_rows, LANES), BF16)] * 2,
        compiler_params=params(),
        cost_estimate=cost(4 * total_rows * total_rows * span, 8 * total_rows * span * 2),
        name="attend",
    )(up, sink_logits, lengths, *given_low, *arrived, *carried)
    blocks, (keys, values) = results[:group_size], results[group_size : group_size + 2]
    if last:
        return blocks, keys, values, None, []
    next_low, *leftovers = results[group_size + 2 :]
    return blocks, keys, values, next_low, [*leftovers, keys, values]


def build_cache(keys, values, starts, lengths, block_table):
    total_rows = keys[0].shape[1]
    parts = len(keys)
    width = sum(part.shape[0] - start for part, start in zip(keys, starts)) * LANES
    heads_local = width // HD
    page_count = total_rows // PAGE + SEGS
    blocks = block_table.shape[1]
    group = 4

    def body(*refs):
        key_refs, value_refs = refs[:parts], refs[parts : 2 * parts]
        lens, table, out, built, sem = refs[2 * parts :]
        page = lax.broadcasted_iota(jnp.int32, (page_count, blocks), 0)
        block = lax.broadcasted_iota(jnp.int32, (page_count, blocks), 1)
        first = jnp.zeros((page_count, blocks), jnp.int32)
        count = jnp.zeros((page_count, blocks), jnp.int32)
        start = 0
        for s in range(SEGS):
            left = lens[s] - block * PAGE
            held = (table[s : s + 1, :] == page) & (left > 0)
            first = jnp.where(held, start + block * PAGE, first)
            count = jnp.where(held, jnp.minimum(left, PAGE), count)
            start = start + lens[s]
        first = jnp.sum(first, axis=1, keepdims=True)
        count = jnp.sum(count, axis=1, keepdims=True)
        place = lax.broadcasted_iota(jnp.int32, (group * page_count, total_rows), 1)

        def gathered(part_refs):
            every = [(ref, tile) for ref, low in zip(part_refs, starts) for tile in range(low, ref.shape[0])]
            return jnp.concatenate([ref[tile] for ref, tile in every], axis=1)

        all_keys, all_values = gathered(key_refs), gathered(value_refs)
        copies = []
        for r in range(0, PAGE, group):
            wanted = [jnp.where(count > r + n, first + r + n, -1) for n in range(group)]
            pick = (place == jnp.concatenate(wanted, axis=0)).astype(F32).astype(BF16)
            picked = [jnp.dot(pick, every, preferred_element_type=F32) for every in (all_keys, all_values)]
            lanes = slice(r * HD, (r + group) * HD)
            for h in range(heads_local):
                columns = slice(h * HD, (h + 1) * HD)
                for c in range(2):
                    line = jnp.concatenate(
                        [picked[c][m * page_count : (m + 1) * page_count, columns] for m in range(group)], axis=1
                    )
                    built[h, :, c, lanes] = line.astype(BF16)
                copies.append(
                    pltpu.make_async_copy(
                        built.at[h, :, :, lanes], out.at[h, :, :, lanes], sem.at[h, r // group]
                    )
                )
                copies[-1].start()
        for copy in copies:
            copy.wait()

    cache = (heads_local, page_count, 2, PAGE * HD)
    return pl.pallas_call(
        body,
        out_shape=jax.ShapeDtypeStruct(cache, BF16),
        in_specs=[IN_VMEM] * (2 * parts) + [IN_SMEM, IN_VMEM],
        out_specs=IN_HBM,
        scratch_shapes=[pltpu.VMEM(cache, BF16), pltpu.SemaphoreType.DMA((heads_local, PAGE // group))],
        compiler_params=params(),
        cost_estimate=cost(4 * page_count * PAGE * total_rows * width, 4 * total_rows * width * 2),
        name="build_cache",
    )(*keys, *values, lengths, block_table)


def join_heads(hidden, parts, width, group_size):
    tok_rows = parts[0][0].shape[0]
    slab = tok_rows // SLABS
    given = [] if hidden is None else [hidden]

    def body(*refs):
        out, sem = refs[-2:]
        me = lax.axis_index("seq")
        copies = []
        for n, (part, bits, begin) in enumerate(parts):
            first = pl.multiple_of(jnp.bitwise_xor(me, bits) * width + begin, LANES)
            for k in range(SLABS):
                rows = pl.ds(k * slab, slab)
                copies.append(
                    pltpu.make_async_copy(
                        refs[n].at[rows, :], out.at[rows, pl.ds(first, part.shape[1])], sem.at[n, k]
                    )
                )
        for copy in copies:
            copy.start()
        for copy in copies:
            copy.wait()

    return pl.pallas_call(
        body,
        out_shape=jax.ShapeDtypeStruct((tok_rows, width * group_size), BF16),
        in_specs=[ANYWHERE] * len(parts) + [IN_HBM] * len(given),
        out_specs=IN_HBM,
        scratch_shapes=[pltpu.SemaphoreType.DMA((len(parts), SLABS))],
        input_output_aliases={len(parts): 0} if given else {},
        compiler_params=params(),
        cost_estimate=cost(0, 4 * tok_rows * sum(part.shape[1] for part, _, _ in parts)),
        name="join_heads",
    )(*[part for part, _, _ in parts], *map(stay, given))


def per_device_tiled(inputs, adapter_down, adapter_up, shared_qkv, sink_logits, lengths, block_table):
    group_size = lax.axis_size("seq")
    partners = sends(group_size)
    width = adapter_up.shape[2]
    heads_local = width // HD
    half = heads_local // 2
    all_tiles = width // LANES
    cut = -(-half * HD // LANES)
    done_cut = half * HD // LANES
    tiles = [(0, cut), (cut, all_tiles)]
    done_tiles = [(0, done_cut), (done_cut, all_tiles)]
    heads = [tuple(range(half)), tuple(range(half, heads_local))]

    every = (0, 1, 2)
    first, others = partners[0], partners[1:]
    whole = (0, all_tiles)
    (early,) = pack_qkv(shared_qkv, [], width, [(first, (0, 1), whole)])
    wanted = [(bits, every, tiles[0]) for bits in others + [0]]
    parts = make_codes(inputs, adapter_down, shared_qkv, early, width, [(first, (2,), whole)] + wanted)
    early = to_partner(early, first, group_size)
    parts = map_partners(partners, parts, group_size)
    arrived = [[early, *parts]]
    wanted = [(bits, every, tiles[1]) for bits in others + [0]]
    later = pack_qkv(shared_qkv, [parts[-1], early], width, wanted)
    arrived.append([early, parts[0], *map_partners(others, later, group_size)])
    places = []
    for n in range(2):
        span = (tiles[n][1] - tiles[n][0]) * LANES
        at = {bits: [(m + 2, c * span) for c in range(4)] for m, bits in enumerate(others + [0])}
        begin = tiles[n][0] * LANES
        at[first] = [(0, begin), (0, width + begin), (1, begin), (1, width)]
        places.append([at[bits] for bits in range(group_size)])
    low_rank, carried, keys, values, own, back = None, [], [], [], [], []
    for n in range(2):
        blocks, new_keys, new_values, low_rank, carried = attend(
            adapter_up,
            sink_logits,
            lengths,
            low_rank,
            arrived[n],
            places[n],
            carried,
            heads[n],
            tiles[n],
            done_tiles[n],
        )
        begin = done_tiles[n][0] * LANES
        own.append((blocks[0], 0, begin))
        back.append([(to_partner(blocks[bits], bits, group_size), bits, begin) for bits in ([partners[i] for i in ((2, 0, 1) if n else (2, 1, 0))])])
        keys, values = keys + [new_keys], values + [new_values]
    starts = [0, cut - done_cut]
    cache = build_cache(keys, values, starts, lengths, block_table)
    hidden = join_heads(None, own + back[0], width, group_size)
    hidden = join_heads(hidden, back[1], width, group_size)
    return (hidden, cache)


def per_device(inputs, adapter_down, adapter_up, shared_qkv, sink_logits, lengths, block_table):
    group_size = lax.axis_size("seq")
    width = adapter_up.shape[2]
    tiled = (
        group_size & (group_size - 1) == 0
        and width % (2 * HD) == 0
        and width % LANES == 0
        and inputs.shape[0] % LANES == 0
        and inputs.shape[0] * group_size <= 512
    )
    chosen = per_device_tiled if tiled else per_device_general
    return chosen(inputs, adapter_down, adapter_up, shared_qkv, sink_logits, lengths, block_table)


def solution(mesh):
    return jax.shard_map(
        per_device,
        mesh=mesh,
        in_specs=(
            P(("batch", "seq"), None),
            P(),
            P(None, None, "seq"),
            P(("batch", "seq"), None),
            P("seq"),
            P("batch"),
            P("batch", None),
        ),
        out_specs=(P(("batch", "seq"), None), P("seq", "batch", None, None)),
        check_vma=False,
    )
```

```python
import jax
import jax.numpy as jnp
from jax import lax
from jax.experimental import pallas as pl
from jax.experimental.pallas import tpu as pltpu
from jax.sharding import PartitionSpec as P

HD = 224
RANK = 128
HEADS = 16
SEGS = 8
PAGE = 16


def segment_positions(lengths, total_rows):
    segment_ends = jnp.cumsum(lengths)
    segment_starts = segment_ends - lengths
    places = jnp.arange(total_rows, dtype=jnp.int32)
    segment = jnp.sum((places[:, None] >= segment_ends[None, :]).astype(jnp.int32), axis=1)
    member = segment[:, None] == jnp.arange(SEGS, dtype=jnp.int32)[None, :]
    offsets = jnp.sum(jnp.where(member, segment_starts[None, :], 0), axis=1)
    return (segment, places - offsets)


def per_device_general(inputs, adapter_down, adapter_up, shared_qkv, sink_logits, lengths, block_table):
    group_size = lax.axis_size("seq")
    tok_rows = inputs.shape[0]
    total_rows = tok_rows * group_size
    heads_local = adapter_up.shape[2] // HD
    window_span = total_rows // 2
    low_codes = jnp.dot(inputs, adapter_down, preferred_element_type=jnp.float32).astype(
        jnp.bfloat16
    )
    shared_base = shared_qkv.reshape(tok_rows, 3, HEADS * HD)
    low_rank = jnp.einsum(
        "tcr,crf->tcf",
        low_codes.reshape(tok_rows, 3, RANK),
        lax.all_gather(adapter_up, "seq", axis=2, tiled=True),
        preferred_element_type=jnp.float32,
    )
    merged = (shared_base.astype(jnp.float32) + low_rank).astype(jnp.bfloat16)
    sending = merged.reshape(tok_rows, 3, HEADS, HD)
    arrived = lax.all_to_all(sending, "seq", split_axis=2, concat_axis=0, tiled=True)
    segment, position = segment_positions(lengths, total_rows)
    tile_rows = min(512, total_rows)
    tile_count = total_rows // tile_rows
    scale_factor = HD ** (-0.5)

    def one_head(head_index):
        query_all = arrived[:, 0, head_index]
        key_all = arrived[:, 1, head_index]
        value_all = arrived[:, 2, head_index]
        sink_logit = sink_logits[head_index]

        def query_tile(tile_index):
            query_first = tile_index * tile_rows
            query_rows = lax.dynamic_slice_in_dim(query_all, query_first, tile_rows, 0)
            query_segs = lax.dynamic_slice_in_dim(segment, query_first, tile_rows, 0)
            query_place = query_first + jnp.arange(tile_rows, dtype=jnp.int32)
            start_state = (
                jnp.full((tile_rows,), sink_logit, jnp.float32),
                jnp.zeros((tile_rows,), jnp.float32),
                jnp.zeros((tile_rows, HD), jnp.float32),
            )

            def visit(key_tile, state):
                key_first = key_tile * tile_rows
                running_max, running_sum, weighted = state
                key_rows = lax.dynamic_slice_in_dim(key_all, key_first, tile_rows, 0)
                value_rows = lax.dynamic_slice_in_dim(value_all, key_first, tile_rows, 0)
                key_segs = lax.dynamic_slice_in_dim(segment, key_first, tile_rows, 0)
                key_place = key_first + jnp.arange(tile_rows, dtype=jnp.int32)
                scores = (
                    jnp.dot(query_rows, key_rows.T, preferred_element_type=jnp.float32)
                    * scale_factor
                )
                visible = (
                    (query_segs[:, None] == key_segs[None, :])
                    & (key_place[None, :] <= query_place[:, None])
                    & (query_place[:, None] - key_place[None, :] < window_span)
                )
                scores = jnp.where(visible, scores, -jnp.inf)
                new_max = jnp.maximum(running_max, jnp.max(scores, axis=1))
                rescale = jnp.exp(running_max - new_max)
                weights = jnp.exp(scores - new_max[:, None])
                new_sum = running_sum * rescale + jnp.sum(weights, axis=1)
                new_weighted = weighted * rescale[:, None] + jnp.dot(
                    weights.astype(jnp.bfloat16), value_rows, preferred_element_type=jnp.float32
                )
                return (new_max, new_sum, new_weighted)

            final_max, final_sum, weighted = lax.fori_loop(0, tile_count, visit, start_state)
            denominator = final_sum + jnp.exp(sink_logit - final_max)
            return (weighted / denominator[:, None]).astype(jnp.bfloat16)

        return lax.map(query_tile, jnp.arange(tile_count, dtype=jnp.int32)).reshape(total_rows, HD)

    attended = lax.map(one_head, jnp.arange(heads_local, dtype=jnp.int32))
    returned = lax.all_to_all(attended, "seq", split_axis=1, concat_axis=0, tiled=True)
    hidden = returned.transpose(1, 0, 2).reshape(tok_rows, HEADS * HD)
    page_count = total_rows // PAGE + SEGS
    page_index = block_table.reshape(-1)[segment * block_table.shape[1] + position // PAGE]
    cache_row = page_index * PAGE + position % PAGE

    def place(values_in):
        flat_cache = (
            jnp.zeros((page_count * PAGE, heads_local, HD), jnp.bfloat16)
            .at[cache_row]
            .set(values_in)
        )
        return (
            flat_cache.reshape(page_count, PAGE, heads_local, HD)
            .transpose(2, 0, 1, 3)
            .reshape(heads_local, page_count, PAGE * HD)
        )

    kv_cache = jnp.stack([place(arrived[:, 1]), place(arrived[:, 2])], axis=2)
    return (hidden, kv_cache)


LANES = 128
SLABS = 1
BF16 = jnp.bfloat16
F32 = jnp.float32
ANYWHERE = pl.BlockSpec(memory_space=pl.ANY)
IN_HBM = pl.BlockSpec(memory_space=pltpu.HBM)
IN_VMEM = pl.BlockSpec(memory_space=pltpu.VMEM)
IN_SMEM = pl.BlockSpec(memory_space=pltpu.SMEM)


def sends(group_size):
    return sorted(range(1, group_size), key=lambda bits: (-bits.bit_count(), bits))


def to_partner(values, bits, group_size):
    return lax.ppermute(values, "seq", [(i, i ^ bits) for i in range(group_size)])


def map_partners(partners, parts, group_size):
    sent = [to_partner(part, bits, group_size) for bits, part in zip(partners, parts)]
    return sent + list(parts[len(partners) :])


def params(mebibytes=40):
    return pltpu.CompilerParams(vmem_limit_bytes=mebibytes * 1024 * 1024)


def stay(values):
    return pltpu.with_memory_space_constraint(values, pltpu.HBM)


def cost(flops, moved):
    return pl.CostEstimate(flops=flops, bytes_accessed=moved, transcendentals=0)


def start_columns(shared, outs, sem, width, wanted):
    me = lax.axis_index("seq")
    slab = shared.shape[0] // SLABS
    copies = []
    for n, (bits, kinds, tiles) in enumerate(wanted):
        span = (tiles[1] - tiles[0]) * LANES
        owner = jnp.bitwise_xor(me, bits)
        for m, c in enumerate(kinds):
            first = pl.multiple_of(c * HEADS * HD + owner * width + tiles[0] * LANES, LANES)
            for k in range(SLABS):
                rows = pl.ds(k * slab, slab)
                copies.append(
                    pltpu.make_async_copy(
                        shared.at[rows, pl.ds(first, span)],
                        outs[n].at[rows, pl.ds(m * span, span)],
                        sem.at[n, m, k],
                    )
                )
    for copy in copies:
        copy.start()
    return copies


def make_codes(inputs, adapter_down, shared_qkv, after, width, wanted):
    tok_rows, depth = inputs.shape
    code_width = adapter_down.shape[1]
    steps = 8
    chunk = depth // steps
    spans = [len(kinds) * (tiles[1] - tiles[0]) * LANES for _, kinds, tiles in wanted]

    def body(inputs_ref, down_ref, shared, _, *refs):
        outs, (held, down, in_sem, down_sem, sem) = refs[:-5], refs[-5:]
        loads = []
        for step in range(steps):
            at = pl.ds(step * chunk, chunk)
            loads.append(
                (
                    pltpu.make_async_copy(inputs_ref.at[:, at], held.at[:, at], in_sem.at[step]),
                    pltpu.make_async_copy(down_ref.at[at, :], down.at[at, :], down_sem.at[step]),
                )
            )
            for load in loads[-1]:
                load.start()
        copies = start_columns(shared, outs, sem, width, wanted)
        total = None
        for step in range(steps):
            for load in loads[step]:
                load.wait()
            at = slice(step * chunk, (step + 1) * chunk)
            term = jnp.dot(held[:, at], down[at, :], preferred_element_type=F32)
            total = term if total is None else total + term
        own_codes = total.astype(BF16)
        for out, span in zip(outs, spans):
            out[:, span:] = own_codes
        for copy in copies:
            copy.wait()

    return pl.pallas_call(
        body,
        out_shape=[jax.ShapeDtypeStruct((tok_rows, span + code_width), BF16) for span in spans],
        in_specs=[IN_HBM, IN_HBM, IN_HBM, ANYWHERE],
        out_specs=[IN_VMEM] * len(wanted),
        scratch_shapes=[
            pltpu.VMEM((tok_rows, depth), BF16),
            pltpu.VMEM((depth, code_width), BF16),
            pltpu.SemaphoreType.DMA((steps,)),
            pltpu.SemaphoreType.DMA((steps,)),
            pltpu.SemaphoreType.DMA((len(wanted), 3, SLABS)),
        ],
        compiler_params=params(20),
        cost_estimate=cost(2 * tok_rows * depth * code_width, depth * code_width * 2),
        name="make_codes",
    )(stay(inputs), stay(adapter_down), stay(shared_qkv), after)


def pack_qkv(shared_qkv, after, width, wanted):
    tok_rows = shared_qkv.shape[0]
    spans = [len(kinds) * (tiles[1] - tiles[0]) * LANES for _, kinds, tiles in wanted]

    def body(shared, *refs):
        outs, sem = refs[len(after) : -1], refs[-1]
        for copy in start_columns(shared, outs, sem, width, wanted):
            copy.wait()

    return pl.pallas_call(
        body,
        out_shape=[jax.ShapeDtypeStruct((tok_rows, span), BF16) for span in spans],
        in_specs=[IN_HBM] + [ANYWHERE] * len(after),
        out_specs=[IN_VMEM] * len(wanted),
        scratch_shapes=[pltpu.SemaphoreType.DMA((len(wanted), 3, SLABS))],
        compiler_params=params(20),
        cost_estimate=cost(0, 2 * tok_rows * sum(spans) * 2),
        name="pack_qkv",
    )(stay(shared_qkv), *after)


def head_tiles(h):
    return (h * HD // LANES, -(-(h + 1) * HD // LANES))


def side_by_side(ref, window, rows):
    return jnp.concatenate([ref[tile, rows, :] for tile in window], axis=1)


def attend(up, sink_logits, lengths, low_rank, arrived, places, carried, heads, tiles, done_tiles):
    group_size = len(places)
    tok_rows = arrived[0].shape[0]
    total_rows = tok_rows * group_size
    window_span = total_rows // 2
    scale_factor = HD ** (-0.5)
    span = (tiles[1] - tiles[0]) * LANES
    done_span = (done_tiles[1] - done_tiles[0]) * LANES
    low_tile = min(tiles[0], done_tiles[0])
    kept = (tiles[0] - low_tile) * LANES
    left = (tiles[1] - done_tiles[1]) * LANES
    first_call, last = low_rank is None, left == 0
    all_tiles = (kept + span) // LANES
    given_low = [] if first_call else [low_rank]
    rest = up.shape[2] - tiles[1] * LANES

    def body(*refs):
        refs = list(refs)
        take = lambda n: [refs.pop(0) for _ in range(n)]
        up_ref, sinks, lens = take(3)
        low_refs = take(len(given_low))
        arrived_refs = take(len(arrived))
        before = take(len(carried))
        outs = take(group_size)
        keys, values = take(2)
        carried_out = take(0 if last else 3)
        queries, merged = take(2)
        me = lax.axis_index("seq")
        kept_tiles = kept // LANES
        if kept:
            for target, source in zip((queries, merged, keys, values), before):
                target[:kept_tiles] = source[source.shape[0] - kept_tiles :]
        for bits in range(group_size):
            place = pl.ds(pl.multiple_of(jnp.bitwise_xor(me, bits) * tok_rows, tok_rows), tok_rows)
            for c, target in enumerate((queries, keys, values)):
                if first_call:
                    which, at = places[bits][3]
                    codes = arrived_refs[which][:, at + c * RANK : at + (c + 1) * RANK]
                    low = jnp.dot(codes, up_ref[c, :, :span], preferred_element_type=F32)
                    carried_out[0][bits, :, c * rest : (c + 1) * rest] = jnp.dot(
                        codes, up_ref[c, :, span:], preferred_element_type=F32
                    )
                else:
                    low = low_refs[0][bits, :, c * span : (c + 1) * span]
                which, at = places[bits][c]
                base = arrived_refs[which][:, at : at + span].astype(F32)
                new = (base + low).astype(BF16)
                for n in range(tiles[1] - tiles[0]):
                    target[kept_tiles + n, place, :] = new[:, n * LANES : (n + 1) * LANES]

        ends = []
        for s in range(SEGS):
            ends.append(lens[s] + (ends[-1] if ends else 0))
        blocks = []
        for b in range(group_size):
            first_query = b * tok_rows
            rows = slice(first_query, first_query + tok_rows)
            first_key = max(0, (first_query - window_span + 1) // tok_rows * tok_rows)
            key_rows = slice(first_key, first_query + tok_rows)
            query_place = first_query + lax.broadcasted_iota(jnp.int32, (tok_rows, 1), 0)
            earliest = query_place - (window_span - 1)
            for s in range(SEGS):
                earliest = jnp.where(ends[s] <= query_place, jnp.maximum(earliest, ends[s]), earliest)
            key_place = first_key + lax.broadcasted_iota(jnp.int32, (tok_rows, key_rows.stop - first_key), 1)
            visible = (key_place >= earliest) & (key_place <= query_place)
            scores = {}
            for h in heads:
                first_tile, end_tile = head_tiles(h)
                window = range(first_tile - low_tile, end_tile - low_tile)
                column = first_tile * LANES + lax.broadcasted_iota(jnp.int32, (1, len(window) * LANES), 1)
                mine = (column >= h * HD) & (column < (h + 1) * HD)
                query = side_by_side(queries, window, rows)
                query = jnp.where(mine, query, jnp.zeros_like(query))
                scores[h] = lax.dot_general(
                    query,
                    side_by_side(keys, window, key_rows),
                    (((1,), (1,)), ((), ())),
                    preferred_element_type=F32,
                )
            blocks.append((rows, key_rows, visible, scores))
        for rows, key_rows, visible, scores in blocks:
            parts = {}
            for tile in range(low_tile, tiles[0]):
                parts[tile] = merged[tile - low_tile, rows, :].astype(F32)
            for h in heads:
                first_tile, end_tile = head_tiles(h)
                window = range(first_tile - low_tile, end_tile - low_tile)
                seen = jnp.where(visible, scores[h] * scale_factor, -jnp.inf)
                top = jnp.maximum(jnp.max(seen, axis=1, keepdims=True), sinks[h])
                weights = jnp.exp(seen - top)
                denominator = jnp.sum(weights, axis=1, keepdims=True) + jnp.exp(sinks[h] - top)
                mixed = jnp.dot(
                    weights.astype(BF16),
                    side_by_side(values, window, key_rows),
                    preferred_element_type=F32,
                ) / denominator
                for tile in range(first_tile, end_tile):
                    at = (tile - first_tile) * LANES
                    piece = mixed[:, at : at + LANES]
                    if tile in parts:
                        lane = tile * LANES + lax.broadcasted_iota(jnp.int32, (1, LANES), 1)
                        piece = jnp.where(lane < h * HD, parts[tile], piece)
                    parts[tile] = piece
            for tile, piece in parts.items():
                merged[tile - low_tile, rows, :] = piece.astype(BF16)
        for bits in range(group_size):
            place = pl.ds(pl.multiple_of(jnp.bitwise_xor(me, bits) * tok_rows, tok_rows), tok_rows)
            outs[bits][...] = side_by_side(merged, range(done_tiles[1] - done_tiles[0]), place)
        if not last:
            carried_out[1][...] = queries[all_tiles - left // LANES :]
            carried_out[2][...] = merged[all_tiles - left // LANES :]

    block = jax.ShapeDtypeStruct((tok_rows, done_span), BF16)
    stream = jax.ShapeDtypeStruct((all_tiles, total_rows, LANES), BF16)
    leftover = jax.ShapeDtypeStruct((left // LANES, total_rows, LANES), BF16)
    next_low = jax.ShapeDtypeStruct((group_size, tok_rows, 3 * rest), F32)
    out_shape = [block] * group_size + [stream] * 2 + ([] if last else [next_low, leftover, leftover])
    results = pl.pallas_call(
        body,
        out_shape=out_shape,
        in_specs=[IN_VMEM, IN_SMEM, IN_SMEM]
        + [IN_VMEM] * (len(given_low) + len(arrived) + len(carried)),
        out_specs=[IN_VMEM] * len(out_shape),
        scratch_shapes=[pltpu.VMEM((all_tiles, total_rows, LANES), BF16)] * 2,
        compiler_params=params(),
        cost_estimate=cost(4 * total_rows * total_rows * span, 8 * total_rows * span * 2),
        name="attend",
    )(up, sink_logits, lengths, *given_low, *arrived, *carried)
    blocks, (keys, values) = results[:group_size], results[group_size : group_size + 2]
    if last:
        return blocks, keys, values, None, []
    next_low, *leftovers = results[group_size + 2 :]
    return blocks, keys, values, next_low, [*leftovers, keys, values]


def page_picks(lengths, block_table, total_rows):
    page_count = total_rows // PAGE + SEGS
    blocks = block_table.shape[1]
    group = 4

    def body(lens, table, picks):
        page = lax.broadcasted_iota(jnp.int32, (page_count, blocks), 0)
        block = lax.broadcasted_iota(jnp.int32, (page_count, blocks), 1)
        first = jnp.zeros((page_count, blocks), jnp.int32)
        count = jnp.zeros((page_count, blocks), jnp.int32)
        start = 0
        for s in range(SEGS):
            left = lens[s] - block * PAGE
            held = (table[s : s + 1, :] == page) & (left > 0)
            first = jnp.where(held, start + block * PAGE, first)
            count = jnp.where(held, jnp.minimum(left, PAGE), count)
            start = start + lens[s]
        first = jnp.sum(first, axis=1, keepdims=True)
        count = jnp.sum(count, axis=1, keepdims=True)
        place = lax.broadcasted_iota(jnp.int32, (group * page_count, total_rows), 1)
        for r in range(0, PAGE, group):
            wanted = [jnp.where(count > r + n, first + r + n, -1) for n in range(group)]
            pick = (place == jnp.concatenate(wanted, axis=0)).astype(F32).astype(BF16)
            picks[r * page_count : (r + group) * page_count, :] = pick

    return pl.pallas_call(
        body,
        out_shape=jax.ShapeDtypeStruct((PAGE * page_count, total_rows), BF16),
        in_specs=[IN_SMEM, IN_VMEM],
        out_specs=IN_VMEM,
        compiler_params=params(),
        cost_estimate=cost(4 * PAGE * page_count * total_rows, 2 * PAGE * page_count * total_rows),
        name="page_picks",
    )(lengths, block_table)


def build_cache(keys, values, starts, picks):
    total_rows = keys[0].shape[1]
    parts = len(keys)
    width = sum(part.shape[0] - start for part, start in zip(keys, starts)) * LANES
    heads_local = width // HD
    page_count = picks.shape[0] // PAGE
    group = 4

    def body(*refs):
        key_refs, value_refs = refs[:parts], refs[parts : 2 * parts]
        picks_ref, out, built, sem = refs[2 * parts :]
        def gathered(part_refs):
            every = [(ref, tile) for ref, low in zip(part_refs, starts) for tile in range(low, ref.shape[0])]
            return jnp.concatenate([ref[tile] for ref, tile in every], axis=1)

        all_keys, all_values = gathered(key_refs), gathered(value_refs)
        copies = []
        for r in range(0, PAGE, group):
            pick = picks_ref[r * page_count : (r + group) * page_count, :]
            picked = [jnp.dot(pick, every, preferred_element_type=F32) for every in (all_keys, all_values)]
            lanes = slice(r * HD, (r + group) * HD)
            for h in range(heads_local):
                columns = slice(h * HD, (h + 1) * HD)
                for c in range(2):
                    line = jnp.concatenate(
                        [picked[c][m * page_count : (m + 1) * page_count, columns] for m in range(group)], axis=1
                    )
                    built[h, :, c, lanes] = line.astype(BF16)
                copies.append(
                    pltpu.make_async_copy(
                        built.at[h, :, :, lanes], out.at[h, :, :, lanes], sem.at[h, r // group]
                    )
                )
                copies[-1].start()
        for copy in copies:
            copy.wait()

    cache = (heads_local, page_count, 2, PAGE * HD)
    return pl.pallas_call(
        body,
        out_shape=jax.ShapeDtypeStruct(cache, BF16),
        in_specs=[IN_VMEM] * (2 * parts + 1),
        out_specs=IN_HBM,
        scratch_shapes=[pltpu.VMEM(cache, BF16), pltpu.SemaphoreType.DMA((heads_local, PAGE // group))],
        compiler_params=params(),
        cost_estimate=cost(4 * page_count * PAGE * total_rows * width, 4 * total_rows * width * 2),
        name="build_cache",
    )(*keys, *values, picks)


def join_heads(hidden, parts, width, group_size):
    tok_rows = parts[0][0].shape[0]
    slab = tok_rows // SLABS
    given = [] if hidden is None else [hidden]

    def body(*refs):
        out, sem = refs[-2:]
        me = lax.axis_index("seq")
        copies = []
        for n, (part, bits, begin) in enumerate(parts):
            first = pl.multiple_of(jnp.bitwise_xor(me, bits) * width + begin, LANES)
            for k in range(SLABS):
                rows = pl.ds(k * slab, slab)
                copies.append(
                    pltpu.make_async_copy(
                        refs[n].at[rows, :], out.at[rows, pl.ds(first, part.shape[1])], sem.at[n, k]
                    )
                )
        for copy in copies:
            copy.start()
        for copy in copies:
            copy.wait()

    return pl.pallas_call(
        body,
        out_shape=jax.ShapeDtypeStruct((tok_rows, width * group_size), BF16),
        in_specs=[ANYWHERE] * len(parts) + [IN_HBM] * len(given),
        out_specs=IN_HBM,
        scratch_shapes=[pltpu.SemaphoreType.DMA((len(parts), SLABS))],
        input_output_aliases={len(parts): 0} if given else {},
        compiler_params=params(),
        cost_estimate=cost(0, 4 * tok_rows * sum(part.shape[1] for part, _, _ in parts)),
        name="join_heads",
    )(*[part for part, _, _ in parts], *map(stay, given))


def per_device_tiled(inputs, adapter_down, adapter_up, shared_qkv, sink_logits, lengths, block_table):
    group_size = lax.axis_size("seq")
    partners = sends(group_size)
    width = adapter_up.shape[2]
    heads_local = width // HD
    half = heads_local // 2
    all_tiles = width // LANES
    cut = -(-half * HD // LANES)
    done_cut = half * HD // LANES
    tiles = [(0, cut), (cut, all_tiles)]
    done_tiles = [(0, done_cut), (done_cut, all_tiles)]
    heads = [tuple(range(half)), tuple(range(half, heads_local))]

    every = (0, 1, 2)
    first, others = partners[0], partners[1:]
    whole = (0, all_tiles)
    (early,) = pack_qkv(shared_qkv, [], width, [(first, (0, 1), whole)])
    wanted = [(bits, every, tiles[0]) for bits in others + [0]]
    parts = make_codes(inputs, adapter_down, shared_qkv, early, width, [(first, (2,), whole)] + wanted)
    early = to_partner(early, first, group_size)
    parts = map_partners(partners, parts, group_size)
    arrived = [[early, *parts]]
    wanted = [(bits, every, tiles[1]) for bits in others + [0]]
    picks = page_picks(lengths, block_table, inputs.shape[0] * group_size)
    later = pack_qkv(shared_qkv, [parts[-1], early, picks], width, wanted)
    arrived.append([early, parts[0], *map_partners(others, later, group_size)])
    places = []
    for n in range(2):
        span = (tiles[n][1] - tiles[n][0]) * LANES
        at = {bits: [(m + 2, c * span) for c in range(4)] for m, bits in enumerate(others + [0])}
        begin = tiles[n][0] * LANES
        at[first] = [(0, begin), (0, width + begin), (1, begin), (1, width)]
        places.append([at[bits] for bits in range(group_size)])
    low_rank, carried, keys, values, own, back = None, [], [], [], [], []
    for n in range(2):
        blocks, new_keys, new_values, low_rank, carried = attend(
            adapter_up,
            sink_logits,
            lengths,
            low_rank,
            arrived[n],
            places[n],
            carried,
            heads[n],
            tiles[n],
            done_tiles[n],
        )
        begin = done_tiles[n][0] * LANES
        own.append((blocks[0], 0, begin))
        back.append([(to_partner(blocks[bits], bits, group_size), bits, begin) for bits in ([partners[i] for i in ((2, 0, 1) if n else (2, 1, 0))])])
        keys, values = keys + [new_keys], values + [new_values]
    starts = [0, cut - done_cut]
    cache = build_cache(keys, values, starts, picks)
    hidden = join_heads(None, own + back[0], width, group_size)
    hidden = join_heads(hidden, back[1], width, group_size)
    return (hidden, cache)


def per_device(inputs, adapter_down, adapter_up, shared_qkv, sink_logits, lengths, block_table):
    group_size = lax.axis_size("seq")
    width = adapter_up.shape[2]
    tiled = (
        group_size & (group_size - 1) == 0
        and width % (2 * HD) == 0
        and width % LANES == 0
        and inputs.shape[0] % LANES == 0
        and inputs.shape[0] * group_size <= 512
    )
    chosen = per_device_tiled if tiled else per_device_general
    return chosen(inputs, adapter_down, adapter_up, shared_qkv, sink_logits, lengths, block_table)


def solution(mesh):
    return jax.shard_map(
        per_device,
        mesh=mesh,
        in_specs=(
            P(("batch", "seq"), None),
            P(),
            P(None, None, "seq"),
            P(("batch", "seq"), None),
            P("seq"),
            P("batch"),
            P("batch", None),
        ),
        out_specs=(P(("batch", "seq"), None), P("seq", "batch", None, None)),
        check_vma=False,
    )
```

```python
import jax
import jax.numpy as jnp
from jax import lax
from jax.experimental import pallas as pl
from jax.experimental.pallas import tpu as pltpu
from jax.sharding import PartitionSpec as P

HD = 224
RANK = 128
HEADS = 16
SEGS = 8
PAGE = 16


def segment_positions(lengths, total_rows):
    segment_ends = jnp.cumsum(lengths)
    segment_starts = segment_ends - lengths
    places = jnp.arange(total_rows, dtype=jnp.int32)
    segment = jnp.sum((places[:, None] >= segment_ends[None, :]).astype(jnp.int32), axis=1)
    member = segment[:, None] == jnp.arange(SEGS, dtype=jnp.int32)[None, :]
    offsets = jnp.sum(jnp.where(member, segment_starts[None, :], 0), axis=1)
    return (segment, places - offsets)


def per_device_general(inputs, adapter_down, adapter_up, shared_qkv, sink_logits, lengths, block_table):
    group_size = lax.axis_size("seq")
    tok_rows = inputs.shape[0]
    total_rows = tok_rows * group_size
    heads_local = adapter_up.shape[2] // HD
    window_span = total_rows // 2
    low_codes = jnp.dot(inputs, adapter_down, preferred_element_type=jnp.float32).astype(
        jnp.bfloat16
    )
    shared_base = shared_qkv.reshape(tok_rows, 3, HEADS * HD)
    low_rank = jnp.einsum(
        "tcr,crf->tcf",
        low_codes.reshape(tok_rows, 3, RANK),
        lax.all_gather(adapter_up, "seq", axis=2, tiled=True),
        preferred_element_type=jnp.float32,
    )
    merged = (shared_base.astype(jnp.float32) + low_rank).astype(jnp.bfloat16)
    sending = merged.reshape(tok_rows, 3, HEADS, HD)
    arrived = lax.all_to_all(sending, "seq", split_axis=2, concat_axis=0, tiled=True)
    segment, position = segment_positions(lengths, total_rows)
    tile_rows = min(512, total_rows)
    tile_count = total_rows // tile_rows
    scale_factor = HD ** (-0.5)

    def one_head(head_index):
        query_all = arrived[:, 0, head_index]
        key_all = arrived[:, 1, head_index]
        value_all = arrived[:, 2, head_index]
        sink_logit = sink_logits[head_index]

        def query_tile(tile_index):
            query_first = tile_index * tile_rows
            query_rows = lax.dynamic_slice_in_dim(query_all, query_first, tile_rows, 0)
            query_segs = lax.dynamic_slice_in_dim(segment, query_first, tile_rows, 0)
            query_place = query_first + jnp.arange(tile_rows, dtype=jnp.int32)
            start_state = (
                jnp.full((tile_rows,), sink_logit, jnp.float32),
                jnp.zeros((tile_rows,), jnp.float32),
                jnp.zeros((tile_rows, HD), jnp.float32),
            )

            def visit(key_tile, state):
                key_first = key_tile * tile_rows
                running_max, running_sum, weighted = state
                key_rows = lax.dynamic_slice_in_dim(key_all, key_first, tile_rows, 0)
                value_rows = lax.dynamic_slice_in_dim(value_all, key_first, tile_rows, 0)
                key_segs = lax.dynamic_slice_in_dim(segment, key_first, tile_rows, 0)
                key_place = key_first + jnp.arange(tile_rows, dtype=jnp.int32)
                scores = (
                    jnp.dot(query_rows, key_rows.T, preferred_element_type=jnp.float32)
                    * scale_factor
                )
                visible = (
                    (query_segs[:, None] == key_segs[None, :])
                    & (key_place[None, :] <= query_place[:, None])
                    & (query_place[:, None] - key_place[None, :] < window_span)
                )
                scores = jnp.where(visible, scores, -jnp.inf)
                new_max = jnp.maximum(running_max, jnp.max(scores, axis=1))
                rescale = jnp.exp(running_max - new_max)
                weights = jnp.exp(scores - new_max[:, None])
                new_sum = running_sum * rescale + jnp.sum(weights, axis=1)
                new_weighted = weighted * rescale[:, None] + jnp.dot(
                    weights.astype(jnp.bfloat16), value_rows, preferred_element_type=jnp.float32
                )
                return (new_max, new_sum, new_weighted)

            final_max, final_sum, weighted = lax.fori_loop(0, tile_count, visit, start_state)
            denominator = final_sum + jnp.exp(sink_logit - final_max)
            return (weighted / denominator[:, None]).astype(jnp.bfloat16)

        return lax.map(query_tile, jnp.arange(tile_count, dtype=jnp.int32)).reshape(total_rows, HD)

    attended = lax.map(one_head, jnp.arange(heads_local, dtype=jnp.int32))
    returned = lax.all_to_all(attended, "seq", split_axis=1, concat_axis=0, tiled=True)
    hidden = returned.transpose(1, 0, 2).reshape(tok_rows, HEADS * HD)
    page_count = total_rows // PAGE + SEGS
    page_index = block_table.reshape(-1)[segment * block_table.shape[1] + position // PAGE]
    cache_row = page_index * PAGE + position % PAGE

    def place(values_in):
        flat_cache = (
            jnp.zeros((page_count * PAGE, heads_local, HD), jnp.bfloat16)
            .at[cache_row]
            .set(values_in)
        )
        return (
            flat_cache.reshape(page_count, PAGE, heads_local, HD)
            .transpose(2, 0, 1, 3)
            .reshape(heads_local, page_count, PAGE * HD)
        )

    kv_cache = jnp.stack([place(arrived[:, 1]), place(arrived[:, 2])], axis=2)
    return (hidden, kv_cache)


LANES = 128
SLABS = 1
BF16 = jnp.bfloat16
F32 = jnp.float32
ANYWHERE = pl.BlockSpec(memory_space=pl.ANY)
IN_HBM = pl.BlockSpec(memory_space=pltpu.HBM)
IN_VMEM = pl.BlockSpec(memory_space=pltpu.VMEM)
IN_SMEM = pl.BlockSpec(memory_space=pltpu.SMEM)


def sends(group_size):
    return sorted(range(1, group_size), key=lambda bits: (-bits.bit_count(), bits))


def to_partner(values, bits, group_size):
    return lax.ppermute(values, "seq", [(i, i ^ bits) for i in range(group_size)])


def map_partners(partners, parts, group_size):
    sent = [to_partner(part, bits, group_size) for bits, part in zip(partners, parts)]
    return sent + list(parts[len(partners) :])


def params(mebibytes=40):
    return pltpu.CompilerParams(vmem_limit_bytes=mebibytes * 1024 * 1024)


def stay(values):
    return pltpu.with_memory_space_constraint(values, pltpu.HBM)


def cost(flops, moved):
    return pl.CostEstimate(flops=flops, bytes_accessed=moved, transcendentals=0)


def start_columns(shared, outs, sem, width, wanted):
    me = lax.axis_index("seq")
    slab = shared.shape[0] // SLABS
    copies = []
    for n, (bits, kinds, tiles) in enumerate(wanted):
        span = (tiles[1] - tiles[0]) * LANES
        owner = jnp.bitwise_xor(me, bits)
        for m, c in enumerate(kinds):
            first = pl.multiple_of(c * HEADS * HD + owner * width + tiles[0] * LANES, LANES)
            for k in range(SLABS):
                rows = pl.ds(k * slab, slab)
                copies.append(
                    pltpu.make_async_copy(
                        shared.at[rows, pl.ds(first, span)],
                        outs[n].at[rows, pl.ds(m * span, span)],
                        sem.at[n, m, k],
                    )
                )
    for copy in copies:
        copy.start()
    return copies


def make_codes(inputs, adapter_down, shared_qkv, after, width, wanted):
    tok_rows, depth = inputs.shape
    code_width = adapter_down.shape[1]
    steps = 8
    chunk = depth // steps
    spans = [len(kinds) * (tiles[1] - tiles[0]) * LANES for _, kinds, tiles in wanted]

    def body(inputs_ref, down_ref, shared, _, *refs):
        outs, (held, down, in_sem, down_sem, sem) = refs[:-5], refs[-5:]
        loads = []
        for step in range(steps):
            at = pl.ds(step * chunk, chunk)
            loads.append(
                (
                    pltpu.make_async_copy(inputs_ref.at[:, at], held.at[:, at], in_sem.at[step]),
                    pltpu.make_async_copy(down_ref.at[at, :], down.at[at, :], down_sem.at[step]),
                )
            )
            for load in loads[-1]:
                load.start()
        copies = start_columns(shared, outs, sem, width, wanted)
        total = None
        for step in range(steps):
            for load in loads[step]:
                load.wait()
            at = slice(step * chunk, (step + 1) * chunk)
            term = jnp.dot(held[:, at], down[at, :], preferred_element_type=F32)
            total = term if total is None else total + term
        own_codes = total.astype(BF16)
        for out, span in zip(outs, spans):
            out[:, span:] = own_codes
        for copy in copies:
            copy.wait()

    return pl.pallas_call(
        body,
        out_shape=[jax.ShapeDtypeStruct((tok_rows, span + code_width), BF16) for span in spans],
        in_specs=[IN_HBM, IN_HBM, IN_HBM, ANYWHERE],
        out_specs=[IN_VMEM] * len(wanted),
        scratch_shapes=[
            pltpu.VMEM((tok_rows, depth), BF16),
            pltpu.VMEM((depth, code_width), BF16),
            pltpu.SemaphoreType.DMA((steps,)),
            pltpu.SemaphoreType.DMA((steps,)),
            pltpu.SemaphoreType.DMA((len(wanted), 3, SLABS)),
        ],
        compiler_params=params(20),
        cost_estimate=cost(2 * tok_rows * depth * code_width, depth * code_width * 2),
        name="make_codes",
    )(stay(inputs), stay(adapter_down), stay(shared_qkv), after)


def pack_qkv(shared_qkv, after, width, wanted):
    tok_rows = shared_qkv.shape[0]
    spans = [len(kinds) * (tiles[1] - tiles[0]) * LANES for _, kinds, tiles in wanted]

    def body(shared, *refs):
        outs, sem = refs[len(after) : -1], refs[-1]
        for copy in start_columns(shared, outs, sem, width, wanted):
            copy.wait()

    return pl.pallas_call(
        body,
        out_shape=[jax.ShapeDtypeStruct((tok_rows, span), BF16) for span in spans],
        in_specs=[IN_HBM] + [ANYWHERE] * len(after),
        out_specs=[IN_VMEM] * len(wanted),
        scratch_shapes=[pltpu.SemaphoreType.DMA((len(wanted), 3, SLABS))],
        compiler_params=params(20),
        cost_estimate=cost(0, 2 * tok_rows * sum(spans) * 2),
        name="pack_qkv",
    )(stay(shared_qkv), *after)


def head_tiles(h):
    return (h * HD // LANES, -(-(h + 1) * HD // LANES))


def side_by_side(ref, window, rows):
    return jnp.concatenate([ref[tile, rows, :] for tile in window], axis=1)


def attend(up, sink_logits, lengths, low_rank, arrived, places, carried, heads, tiles, done_tiles):
    group_size = len(places)
    tok_rows = arrived[0].shape[0]
    total_rows = tok_rows * group_size
    window_span = total_rows // 2
    scale_factor = HD ** (-0.5)
    span = (tiles[1] - tiles[0]) * LANES
    done_span = (done_tiles[1] - done_tiles[0]) * LANES
    low_tile = min(tiles[0], done_tiles[0])
    kept = (tiles[0] - low_tile) * LANES
    left = (tiles[1] - done_tiles[1]) * LANES
    first_call, last = low_rank is None, left == 0
    all_tiles = (kept + span) // LANES
    given_low = [] if first_call else [low_rank]
    rest = up.shape[2] - tiles[1] * LANES

    def body(*refs):
        refs = list(refs)
        take = lambda n: [refs.pop(0) for _ in range(n)]
        up_ref, sinks, lens = take(3)
        low_refs = take(len(given_low))
        arrived_refs = take(len(arrived))
        before = take(len(carried))
        outs = take(group_size)
        keys, values = take(2)
        carried_out = take(0 if last else 3)
        queries, merged = take(2)
        me = lax.axis_index("seq")
        kept_tiles = kept // LANES
        if kept:
            for target, source in zip((queries, merged, keys, values), before):
                target[:kept_tiles] = source[source.shape[0] - kept_tiles :]
        for bits in range(group_size):
            place = pl.ds(pl.multiple_of(jnp.bitwise_xor(me, bits) * tok_rows, tok_rows), tok_rows)
            for c, target in enumerate((queries, keys, values)):
                if first_call:
                    which, at = places[bits][3]
                    codes = arrived_refs[which][:, at + c * RANK : at + (c + 1) * RANK]
                    low = jnp.dot(codes, up_ref[c, :, :span], preferred_element_type=F32)
                    carried_out[0][bits, :, c * rest : (c + 1) * rest] = jnp.dot(
                        codes, up_ref[c, :, span:], preferred_element_type=F32
                    )
                else:
                    low = low_refs[0][bits, :, c * span : (c + 1) * span]
                which, at = places[bits][c]
                base = arrived_refs[which][:, at : at + span].astype(F32)
                new = (base + low).astype(BF16)
                for n in range(tiles[1] - tiles[0]):
                    target[kept_tiles + n, place, :] = new[:, n * LANES : (n + 1) * LANES]

        ends = []
        for s in range(SEGS):
            ends.append(lens[s] + (ends[-1] if ends else 0))
        blocks = []
        for b in range(group_size):
            first_query = b * tok_rows
            rows = slice(first_query, first_query + tok_rows)
            first_key = max(0, (first_query - window_span + 1) // tok_rows * tok_rows)
            key_rows = slice(first_key, first_query + tok_rows)
            query_place = first_query + lax.broadcasted_iota(jnp.int32, (tok_rows, 1), 0)
            earliest = query_place - (window_span - 1)
            for s in range(SEGS):
                earliest = jnp.where(ends[s] <= query_place, jnp.maximum(earliest, ends[s]), earliest)
            key_place = first_key + lax.broadcasted_iota(jnp.int32, (tok_rows, key_rows.stop - first_key), 1)
            visible = (key_place >= earliest) & (key_place <= query_place)
            scores = {}
            for h in heads:
                first_tile, end_tile = head_tiles(h)
                window = range(first_tile - low_tile, end_tile - low_tile)
                column = first_tile * LANES + lax.broadcasted_iota(jnp.int32, (1, len(window) * LANES), 1)
                mine = (column >= h * HD) & (column < (h + 1) * HD)
                query = side_by_side(queries, window, rows)
                query = jnp.where(mine, query, jnp.zeros_like(query))
                scores[h] = lax.dot_general(
                    query,
                    side_by_side(keys, window, key_rows),
                    (((1,), (1,)), ((), ())),
                    preferred_element_type=F32,
                )
            blocks.append((rows, key_rows, visible, scores))
        for rows, key_rows, visible, scores in blocks:
            parts = {}
            for tile in range(low_tile, tiles[0]):
                parts[tile] = merged[tile - low_tile, rows, :].astype(F32)
            for h in heads:
                first_tile, end_tile = head_tiles(h)
                window = range(first_tile - low_tile, end_tile - low_tile)
                seen = jnp.where(visible, scores[h] * scale_factor, -jnp.inf)
                top = jnp.maximum(jnp.max(seen, axis=1, keepdims=True), sinks[h])
                weights = jnp.exp(seen - top)
                denominator = jnp.sum(weights, axis=1, keepdims=True) + jnp.exp(sinks[h] - top)
                mixed = jnp.dot(
                    weights.astype(BF16),
                    side_by_side(values, window, key_rows),
                    preferred_element_type=F32,
                ) / denominator
                for tile in range(first_tile, end_tile):
                    at = (tile - first_tile) * LANES
                    piece = mixed[:, at : at + LANES]
                    if tile in parts:
                        lane = tile * LANES + lax.broadcasted_iota(jnp.int32, (1, LANES), 1)
                        piece = jnp.where(lane < h * HD, parts[tile], piece)
                    parts[tile] = piece
            for tile, piece in parts.items():
                merged[tile - low_tile, rows, :] = piece.astype(BF16)
        for bits in range(group_size):
            place = pl.ds(pl.multiple_of(jnp.bitwise_xor(me, bits) * tok_rows, tok_rows), tok_rows)
            outs[bits][...] = side_by_side(merged, range(done_tiles[1] - done_tiles[0]), place)
        if not last:
            carried_out[1][...] = queries[all_tiles - left // LANES :]
            carried_out[2][...] = merged[all_tiles - left // LANES :]

    block = jax.ShapeDtypeStruct((tok_rows, done_span), BF16)
    stream = jax.ShapeDtypeStruct((all_tiles, total_rows, LANES), BF16)
    leftover = jax.ShapeDtypeStruct((left // LANES, total_rows, LANES), BF16)
    next_low = jax.ShapeDtypeStruct((group_size, tok_rows, 3 * rest), F32)
    out_shape = [block] * group_size + [stream] * 2 + ([] if last else [next_low, leftover, leftover])
    results = pl.pallas_call(
        body,
        out_shape=out_shape,
        in_specs=[IN_VMEM, IN_SMEM, IN_SMEM]
        + [IN_VMEM] * (len(given_low) + len(arrived) + len(carried)),
        out_specs=[IN_VMEM] * len(out_shape),
        scratch_shapes=[pltpu.VMEM((all_tiles, total_rows, LANES), BF16)] * 2,
        compiler_params=params(),
        cost_estimate=cost(4 * total_rows * total_rows * span, 8 * total_rows * span * 2),
        name="attend",
    )(up, sink_logits, lengths, *given_low, *arrived, *carried)
    blocks, (keys, values) = results[:group_size], results[group_size : group_size + 2]
    if last:
        return blocks, keys, values, None, []
    next_low, *leftovers = results[group_size + 2 :]
    return blocks, keys, values, next_low, [*leftovers, keys, values]


def page_picks(lengths, block_table, total_rows):
    page_count = total_rows // PAGE + SEGS
    blocks = block_table.shape[1]
    group = 4

    def body(lens, table, picks):
        page = lax.broadcasted_iota(jnp.int32, (page_count, blocks), 0)
        block = lax.broadcasted_iota(jnp.int32, (page_count, blocks), 1)
        first = jnp.zeros((page_count, blocks), jnp.int32)
        count = jnp.zeros((page_count, blocks), jnp.int32)
        start = 0
        for s in range(SEGS):
            left = lens[s] - block * PAGE
            held = (table[s : s + 1, :] == page) & (left > 0)
            first = jnp.where(held, start + block * PAGE, first)
            count = jnp.where(held, jnp.minimum(left, PAGE), count)
            start = start + lens[s]
        first = jnp.sum(first, axis=1, keepdims=True)
        count = jnp.sum(count, axis=1, keepdims=True)
        place = lax.broadcasted_iota(jnp.int32, (group * page_count, total_rows), 1)
        for r in range(0, PAGE, group):
            wanted = [jnp.where(count > r + n, first + r + n, -1) for n in range(group)]
            pick = (place == jnp.concatenate(wanted, axis=0)).astype(F32).astype(BF16)
            picks[r * page_count : (r + group) * page_count, :] = pick

    return pl.pallas_call(
        body,
        out_shape=jax.ShapeDtypeStruct((PAGE * page_count, total_rows), BF16),
        in_specs=[IN_SMEM, IN_VMEM],
        out_specs=IN_VMEM,
        compiler_params=params(),
        cost_estimate=cost(4 * PAGE * page_count * total_rows, 2 * PAGE * page_count * total_rows),
        name="page_picks",
    )(lengths, block_table)


def build_cache(keys, values, starts, picks):
    total_rows = keys[0].shape[1]
    parts = len(keys)
    width = sum(part.shape[0] - start for part, start in zip(keys, starts)) * LANES
    heads_local = width // HD
    page_count = picks.shape[0] // PAGE
    group = 4

    def body(*refs):
        key_refs, value_refs = refs[:parts], refs[parts : 2 * parts]
        picks_ref, out, built, sem = refs[2 * parts :]
        def gathered(part_refs):
            every = [(ref, tile) for ref, low in zip(part_refs, starts) for tile in range(low, ref.shape[0])]
            return jnp.concatenate([ref[tile] for ref, tile in every], axis=1)

        all_keys, all_values = gathered(key_refs), gathered(value_refs)
        copies = []
        for r in range(0, PAGE, group):
            pick = picks_ref[r * page_count : (r + group) * page_count, :]
            picked = [jnp.dot(pick, every, preferred_element_type=F32) for every in (all_keys, all_values)]
            lanes = slice(r * HD, (r + group) * HD)
            for h in range(heads_local):
                columns = slice(h * HD, (h + 1) * HD)
                for c in range(2):
                    line = jnp.concatenate(
                        [picked[c][m * page_count : (m + 1) * page_count, columns] for m in range(group)], axis=1
                    )
                    built[h, :, c, lanes] = line.astype(BF16)
                copies.append(
                    pltpu.make_async_copy(
                        built.at[h, :, :, lanes], out.at[h, :, :, lanes], sem.at[h, r // group]
                    )
                )
                copies[-1].start()
        for copy in copies:
            copy.wait()

    cache = (heads_local, page_count, 2, PAGE * HD)
    return pl.pallas_call(
        body,
        out_shape=jax.ShapeDtypeStruct(cache, BF16),
        in_specs=[IN_VMEM] * (2 * parts + 1),
        out_specs=IN_HBM,
        scratch_shapes=[pltpu.VMEM(cache, BF16), pltpu.SemaphoreType.DMA((heads_local, PAGE // group))],
        compiler_params=params(),
        cost_estimate=cost(4 * page_count * PAGE * total_rows * width, 4 * total_rows * width * 2),
        name="build_cache",
    )(*keys, *values, picks)


def join_heads(hidden, parts, width, group_size):
    tok_rows = parts[0][0].shape[0]
    slab = tok_rows // SLABS
    given = [] if hidden is None else [hidden]

    def body(*refs):
        out, sem = refs[-2:]
        me = lax.axis_index("seq")
        copies = []
        for n, (part, bits, begin) in enumerate(parts):
            first = pl.multiple_of(jnp.bitwise_xor(me, bits) * width + begin, LANES)
            for k in range(SLABS):
                rows = pl.ds(k * slab, slab)
                copies.append(
                    pltpu.make_async_copy(
                        refs[n].at[rows, :], out.at[rows, pl.ds(first, part.shape[1])], sem.at[n, k]
                    )
                )
        for copy in copies:
            copy.start()
        for copy in copies:
            copy.wait()

    return pl.pallas_call(
        body,
        out_shape=jax.ShapeDtypeStruct((tok_rows, width * group_size), BF16),
        in_specs=[ANYWHERE] * len(parts) + [IN_HBM] * len(given),
        out_specs=IN_HBM,
        scratch_shapes=[pltpu.SemaphoreType.DMA((len(parts), SLABS))],
        input_output_aliases={len(parts): 0} if given else {},
        compiler_params=params(),
        cost_estimate=cost(0, 4 * tok_rows * sum(part.shape[1] for part, _, _ in parts)),
        name="join_heads",
    )(*[part for part, _, _ in parts], *map(stay, given))


def per_device_tiled(inputs, adapter_down, adapter_up, shared_qkv, sink_logits, lengths, block_table):
    group_size = lax.axis_size("seq")
    partners = sends(group_size)
    width = adapter_up.shape[2]
    heads_local = width // HD
    half = heads_local // 2
    all_tiles = width // LANES
    cut = -(-half * HD // LANES)
    done_cut = half * HD // LANES
    tiles = [(0, cut), (cut, all_tiles)]
    done_tiles = [(0, done_cut), (done_cut, all_tiles)]
    heads = [tuple(range(half)), tuple(range(half, heads_local))]

    every = (0, 1, 2)
    first, others = partners[0], partners[1:]
    whole = (0, all_tiles)
    (early,) = pack_qkv(shared_qkv, [], width, [(first, (0, 1), whole)])
    wanted = [(bits, every, tiles[0]) for bits in others + [0]]
    parts = make_codes(inputs, adapter_down, shared_qkv, early, width, [(first, (2,), whole)] + wanted)
    early = to_partner(early, first, group_size)
    parts = map_partners(partners, parts, group_size)
    arrived = [[early, *parts]]
    wanted = [(bits, every, tiles[1]) for bits in others + [0]]
    picks = page_picks(lengths, block_table, inputs.shape[0] * group_size)
    later = pack_qkv(shared_qkv, [parts[-1], early, picks], width, wanted)
    arrived.append([early, parts[0], *map_partners(others, later, group_size)])
    places = []
    for n in range(2):
        span = (tiles[n][1] - tiles[n][0]) * LANES
        at = {bits: [(m + 2, c * span) for c in range(4)] for m, bits in enumerate(others + [0])}
        begin = tiles[n][0] * LANES
        at[first] = [(0, begin), (0, width + begin), (1, begin), (1, width)]
        places.append([at[bits] for bits in range(group_size)])
    low_rank, carried, keys, values, own, back = None, [], [], [], [], []
    for n in range(2):
        blocks, new_keys, new_values, low_rank, carried = attend(
            adapter_up,
            sink_logits,
            lengths,
            low_rank,
            arrived[n],
            places[n],
            carried,
            heads[n],
            tiles[n],
            done_tiles[n],
        )
        begin = done_tiles[n][0] * LANES
        own.append((blocks[0], 0, begin))
        back.append([(to_partner(blocks[bits], bits, group_size), bits, begin) for bits in ([partners[i] for i in ((2, 0, 1) if n else (1, 2, 0))])])
        keys, values = keys + [new_keys], values + [new_values]
    starts = [0, cut - done_cut]
    cache = build_cache(keys, values, starts, picks)
    hidden = join_heads(None, own + back[0], width, group_size)
    hidden = join_heads(hidden, back[1], width, group_size)
    return (hidden, cache)


def per_device(inputs, adapter_down, adapter_up, shared_qkv, sink_logits, lengths, block_table):
    group_size = lax.axis_size("seq")
    width = adapter_up.shape[2]
    tiled = (
        group_size & (group_size - 1) == 0
        and width % (2 * HD) == 0
        and width % LANES == 0
        and inputs.shape[0] % LANES == 0
        and inputs.shape[0] * group_size <= 512
    )
    chosen = per_device_tiled if tiled else per_device_general
    return chosen(inputs, adapter_down, adapter_up, shared_qkv, sink_logits, lengths, block_table)


def solution(mesh):
    return jax.shard_map(
        per_device,
        mesh=mesh,
        in_specs=(
            P(("batch", "seq"), None),
            P(),
            P(None, None, "seq"),
            P(("batch", "seq"), None),
            P("seq"),
            P("batch"),
            P("batch", None),
        ),
        out_specs=(P(("batch", "seq"), None), P("seq", "batch", None, None)),
        check_vma=False,
    )
```
